512 devices in a mesh: gx: 32 (over x, y, core), gz: 16 (over z).
Axes of the slice: x: 4, y: 4, z: 16, core: 2. Of those that a mesh axis runs over, the one named last changes fastest.
Arguments:
- element_rhs_load: float32 [32, 8, 32, 8, 128], P('gx', None, 'gz'), may hold values from -6 to 6
- metric: float32 [3, 32, 32, 16], P(None, 'gx', 'gz'), may hold values from 0.5 to 2
- coarse_factor: float32 [32, 16, 10, 32, 16], P('gx', 'gz'), may hold values from -1 to 1
Outputs:
- solution_field: float32 [32, 8, 32, 8, 128], P('gx', None, 'gz')
- residual: float32 [32, 8, 32, 8, 128], P('gx', None, 'gz')
The draws below stay inside these ranges and needn't reach their ends.
All inputs are finite; a program needn't handle non-finite values.
Results may differ from the reference program's by a relative error of at most 0.00019.
Values sent between devices are 32-bit elements; how exact they have to be, the bound alone decides.
No kernel may reach another device: no remote copies, remote signals or barrier semaphores. Data moves between devices by JAX's collectives and lax.ppermute only.
A program may use at most 64 MiB of HBM per device.

```python
import math
import jax
import jax.numpy as jnp
import numpy as np
from jax import lax

EX = 1
EZ = 2
ELEMENTS_WALLS = 16
CHEB = 4
COARSE = 32
SEP = 16
LEVELS = 9
ELEMENTS_STREAM = 32
ELEMENTS_SPAN = 32
N_GX = 32
N_GZ = 16


def draw_coarse_factor(key, part):
    key = jax.random.fold_in(key, 11)
    nodes = EX * EZ * ELEMENTS_WALLS * 512
    base = math.sqrt(0.5) / ((nodes / 8.0) ** 0.25 * (32.0 * SEP) ** 0.25 * (LEVELS + 1.0) ** 0.25)
    levels = jnp.arange(LEVELS + 1).astype(jnp.float32)
    scale = base * jnp.exp2(-levels / 4.0)
    values = jnp.clip(jax.random.normal(key, (N_GX, N_GZ, LEVELS + 1, COARSE, SEP), jnp.float32), -5.0, 5.0)
    return values * scale[None, None, :, None, None]


def block_levels(key, dims, split, low, largest):
    loudness = 1.0
    for dim, blocks in split:
        steps = jax.random.uniform(jax.random.fold_in(jax.random.fold_in(key, 6), dim), (blocks,), jnp.float32, low / len(split), largest / len(split))
        loudness = loudness * jnp.repeat(jnp.exp(steps), dims[dim] // blocks).reshape((-1,) + (1,) * (len(dims) - 1 - dim))
    return loudness


def gaussian(key, shape, width, most, shards=(), held_as=jnp.bfloat16):
    values = width * jax.random.normal(key, shape, jnp.float32)
    if shards:
        values = values * block_levels(key, shape, shards, -0.22, 0.18)
    return jnp.clip(values, -most, most).astype(held_as)


def setup_inputs(seed: int = 0) -> dict:
    seeds = jax.random.split(jax.random.key(seed), 4)
    element_rhs_load = gaussian(seeds[0], (ELEMENTS_STREAM, 8, ELEMENTS_SPAN, 8, ELEMENTS_WALLS * 8), 1.0, 6.0, ((0, 32), (2, 16)), jnp.float32)
    metric = jnp.clip(jnp.exp(math.log(2.0) - 1.3862944 * jax.random.uniform(seeds[1], (3, ELEMENTS_STREAM, ELEMENTS_SPAN, ELEMENTS_WALLS), jnp.float32) ** block_levels(seeds[1], (3, ELEMENTS_STREAM, ELEMENTS_SPAN, ELEMENTS_WALLS), ((1, 32), (2, 16)), -0.2, 0.2)), 0.5, 2.0)
    coarse_factor = draw_coarse_factor(jax.random.fold_in(seeds[3], 71), 0)
    return {"element_rhs_load": element_rhs_load, "metric": metric, "coarse_factor": coarse_factor}


cheb_high = 2.0
cheb_low = 0.1
gll_inner = (-0.8717401485096066, -0.5917001814331423, -0.2092992179024789, 0.2092992179024789, 0.5917001814331423, 0.8717401485096066)


def legendre_seven(points):
    before = np.ones(points.shape[0])
    current = points.copy()
    for degree in range(1, 7):
        following = ((2.0 * degree + 1.0) * points * current - degree * before) / (degree + 1.0)
        before = current
        current = following
    return current


def gll_tables():
    order = 7
    points = np.concatenate([[-1.0], np.array(gll_inner), [1.0]])
    values = legendre_seven(points)
    weights = 2.0 / (order * (order + 1) * values ** 2)
    count = order + 1
    deriv = np.zeros((count, count))
    for row_index in range(count):
        for col_index in range(count):
            if row_index != col_index:
                deriv[row_index, col_index] = values[row_index] / (values[col_index] * (points[row_index] - points[col_index]))
    deriv[0, 0] = -order * (order + 1) / 4.0
    deriv[-1, -1] = order * (order + 1) / 4.0
    stiff = deriv.T @ (weights[:, None] * deriv)
    return points, weights, stiff


def bump_tables(count_x, count_z, count_across):
    points, weights, stiff = gll_tables()

    def positions(count):
        return ((np.arange(count)[:, None] + (1.0 + points[None, :]) / 2.0) / count).reshape(-1)

    along_x = np.stack([np.sin(np.pi * mode * positions(count_x)) for mode in (1, 2)])
    along_z = np.stack([np.sin(np.pi * mode * positions(count_z)) for mode in (1, 2)])
    along_y = np.stack([np.sin(np.pi * mode * positions(count_across)) for mode in range(1, 9)])
    return jnp.asarray(along_x, jnp.float32), jnp.asarray(along_z, jnp.float32), jnp.asarray(along_y, jnp.float32)


def wall_mask(count_across):
    table = np.ones(count_across * 8)
    table[0] = 0.0
    table[-1] = 0.0
    return jnp.asarray(table, jnp.float32)


def node_weights(count_across):
    edge = np.ones(8)
    edge[0] = 0.5
    edge[7] = 0.5
    across = np.ones(count_across * 8)
    for element in range(count_across):
        if element > 0:
            across[8 * element] = 0.5
        if element < count_across - 1:
            across[8 * element + 7] = 0.5
    table = edge[:, None, None] * edge[None, :, None] * across[None, None, :]
    return jnp.asarray(table, jnp.float32).reshape(1, 8, 1, 8, count_across * 8)


def element_apply(field, metric):
    points, weights, stiff = gll_tables()
    stiffness = jnp.asarray(stiff, jnp.float32)
    weight = jnp.asarray(weights, jnp.float32)
    count_x, count_z, count_across = metric.shape[1], metric.shape[2], metric.shape[3]
    cube = field.reshape(count_x, 8, count_z, 8, count_across, 8)
    highest = lax.Precision.HIGHEST
    weight_i = weight[None, :, None, None, None, None]
    weight_j = weight[None, None, None, :, None, None]
    weight_l = weight[None, None, None, None, None, :]
    term_x = jnp.einsum('aibjcl,ip->apbjcl', cube, stiffness, precision=highest) * (weight_j * weight_l)
    term_z = jnp.einsum('aibjcl,jp->aibpcl', cube, stiffness, precision=highest) * (weight_i * weight_l)
    term_y = jnp.einsum('aibjcl,lp->aibjcp', cube, stiffness, precision=highest) * (weight_i * weight_j)
    factor_x = metric[0][:, None, :, None, :, None]
    factor_z = metric[1][:, None, :, None, :, None]
    factor_y = metric[2][:, None, :, None, :, None]
    result = factor_x * term_x + factor_z * term_z + factor_y * term_y
    return result.reshape(count_x, 8, count_z, 8, count_across * 8)


def element_diagonal(metric):
    points, weights, stiff = gll_tables()
    weight = jnp.asarray(weights, jnp.float32)
    kdiag = jnp.asarray(stiff[np.arange(8), np.arange(8)], jnp.float32)
    count_x, count_z, count_across = metric.shape[1], metric.shape[2], metric.shape[3]
    weight_i = weight[None, :, None, None, None, None]
    weight_j = weight[None, None, None, :, None, None]
    weight_l = weight[None, None, None, None, None, :]
    stiff_i = kdiag[None, :, None, None, None, None]
    stiff_j = kdiag[None, None, None, :, None, None]
    stiff_l = kdiag[None, None, None, None, None, :]
    factor_x = metric[0][:, None, :, None, :, None]
    factor_z = metric[1][:, None, :, None, :, None]
    factor_y = metric[2][:, None, :, None, :, None]
    result = factor_x * (stiff_i * weight_j * weight_l) + factor_z * (weight_i * stiff_j * weight_l) + factor_y * (weight_i * weight_j * stiff_l)
    return result.reshape(count_x, 8, count_z, 8, count_across * 8)


def sum_y(field):
    shape = field.shape
    cube = field.reshape(shape[:-1] + (shape[-1] // 8, 8))
    lower = cube[..., 0]
    upper = cube[..., 7]
    joined = upper[..., :-1] + lower[..., 1:]
    cube = cube.at[..., 1:, 0].set(joined).at[..., :-1, 7].set(joined)
    return cube.reshape(shape)


def chebyshev(rhs, inv_diag, operator):
    theta = 0.5 * (cheb_high + cheb_low)
    delta = 0.5 * (cheb_high - cheb_low)
    sigma = theta / delta
    rho = 1.0 / sigma
    update = inv_diag * rhs / theta
    smooth = update
    for sweep in range(CHEB - 1):
        remainder = rhs - operator(smooth)
        rho_next = 1.0 / (2.0 * sigma - rho)
        update = rho_next * rho * update + (2.0 * rho_next / delta) * inv_diag * remainder
        smooth = smooth + update
        rho = rho_next
    return smooth


def sum_x(field):
    lower = field[:, 0]
    upper = field[:, 7]
    new_lower = lower + jnp.roll(upper, 1, axis=0)
    new_upper = upper + jnp.roll(lower, -1, axis=0)
    return field.at[:, 0].set(new_lower).at[:, 7].set(new_upper)


def sum_z(field):
    lower = field[:, :, :, 0]
    upper = field[:, :, :, 7]
    new_lower = lower + jnp.roll(upper, 1, axis=2)
    new_upper = upper + jnp.roll(lower, -1, axis=2)
    return field.at[:, :, :, 0].set(new_lower).at[:, :, :, 7].set(new_upper)


def reference(element_rhs_load, metric, coarse_factor):
    highest = lax.Precision.HIGHEST
    count_across = ELEMENTS_WALLS
    boundary_mask = wall_mask(count_across)
    mult = node_weights(count_across)

    def assemble(field):
        return sum_y(sum_z(sum_x(field)))

    def operator(field):
        return assemble(element_apply(field, metric)) * boundary_mask

    rhs = assemble(element_rhs_load) * boundary_mask
    inv_diag = boundary_mask / assemble(element_diagonal(metric))
    smooth = chebyshev(rhs, inv_diag, operator)

    along_x, along_z, along_y = bump_tables(EX, EZ, count_across)
    weighted = (rhs * mult).reshape(N_GX, EX * 8, N_GZ, EZ * 8, count_across * 8)
    partial_y = jnp.einsum('pxqzy,ky->pxqzk', weighted, along_y, precision=highest)
    partial_x = jnp.einsum('pxqzk,ax->paqzk', partial_y, along_x, precision=highest)
    coarse_rhs = jnp.einsum('paqzk,bz->pqabk', partial_x, along_z, precision=highest)
    devices = N_GX * N_GZ
    coarse_rhs = coarse_rhs.reshape(devices, COARSE)
    factor = coarse_factor.reshape(devices, LEVELS + 1, COARSE, SEP)
    own = jnp.einsum('plck,pc->plk', factor, coarse_rhs, precision=highest)
    totals = []
    for level in range(LEVELS + 1):
        group = own[:, level].reshape(devices >> level, 1 << level, SEP).sum(axis=1)
        totals.append(jnp.repeat(group, 1 << level, axis=0))
    column_sum = jnp.stack(totals, axis=1)
    coarse_sol = jnp.einsum('plck,plk->pc', factor, column_sum, precision=highest)
    coarse_sol = coarse_sol.reshape(N_GX, N_GZ, 2, 2, 8)
    spread_y = jnp.einsum('pqabk,ky->pqaby', coarse_sol, along_y, precision=highest)
    spread_z = jnp.einsum('pqaby,bz->pqazy', spread_y, along_z, precision=highest)
    streamwise_spread = jnp.einsum('pqazy,ax->pxqzy', spread_z, along_x, precision=highest)
    coarse_solution = streamwise_spread.reshape(ELEMENTS_STREAM, 8, ELEMENTS_SPAN, 8, count_across * 8) * boundary_mask
    precond = smooth + coarse_solution

    rz = jnp.sum(mult * rhs * precond)
    image = operator(precond)
    curvature = jnp.sum(mult * precond * image)
    alpha = rz / curvature
    solution_field = alpha * precond
    residual = rhs - alpha * image
    return solution_field, residual
```

```python
import jax
import jax.numpy as jnp
import numpy as np
from jax import lax
from jax.experimental import pallas as pl
from jax.experimental.pallas import tpu as pltpu
from jax.sharding import PartitionSpec as P

CHEB = 4
N_GX = 32
N_GZ = 16
F32 = jnp.float32
HIGHEST = lax.Precision.HIGHEST

cheb_high = 2.0
cheb_low = 0.1
gll_inner = (
    -0.8717401485096066,
    -0.5917001814331423,
    -0.2092992179024789,
    0.2092992179024789,
    0.5917001814331423,
    0.8717401485096066,
)


def legendre_seven(points):
    before = np.ones(points.shape[0])
    current = points.copy()
    for degree in range(1, 7):
        following = ((2.0 * degree + 1.0) * points * current - degree * before) / (degree + 1.0)
        before = current
        current = following
    return current


def gll_tables():
    order = 7
    points = np.concatenate([[-1.0], np.array(gll_inner), [1.0]])
    values = legendre_seven(points)
    weights = 2.0 / (order * (order + 1) * values**2)
    count = order + 1
    deriv = np.zeros((count, count))
    for row_index in range(count):
        for col_index in range(count):
            if row_index != col_index:
                deriv[row_index, col_index] = values[row_index] / (
                    values[col_index] * (points[row_index] - points[col_index])
                )
    deriv[0, 0] = -order * (order + 1) / 4.0
    deriv[-1, -1] = order * (order + 1) / 4.0
    stiff = deriv.T @ (weights[:, None] * deriv)
    return (points, weights, stiff)


POINTS, WEIGHTS, STIFF = gll_tables()
KDIAG = np.diag(STIFF)
W = [float(v) for v in WEIGHTS]
KD = [float(v) for v in KDIAG]
K = [[float(v) for v in row] for row in STIFF]


def positions(count):
    return ((np.arange(count)[:, None] + (1.0 + POINTS[None, :]) / 2.0) / count).reshape(-1)


ALONG_X = np.stack([np.sin(np.pi * mode * positions(1)) for mode in (1, 2)])
ALONG_Z = np.stack([np.sin(np.pi * mode * positions(2)) for mode in (1, 2)])
ALONG_Y = np.stack([np.sin(np.pi * mode * positions(16)) for mode in range(1, 9)])
EDGE = np.array([0.5] + [1.0] * 6 + [0.5])


def build_tables():
    w_l = np.tile(WEIGHTS, 16)[None, :]
    k_l = np.tile(KDIAG, 16)[None, :]
    w_j = WEIGHTS[:, None]
    k_j = KDIAG[:, None]
    ones = np.ones((1, 128))
    across = np.ones(128)
    across[8::8] = 0.5
    across[7:127:8] = 0.5
    pieces = {
        "stiff": np.kron(np.eye(16), STIFF),
        "ww": w_j * w_l,
        "kw": k_j * w_l,
        "wk": w_j * k_l,
        "wl": np.ones((8, 1)) * w_l,
        "wj": w_j * ones,
        "mult": EDGE[:, None] * across[None, :],
        "expand": np.kron(np.eye(16), np.ones((1, 8))),
        "modes": np.tile(ALONG_Y, (4, 1)),
    }
    for b in range(2):
        for z in range(2):
            pieces[f"bz{b}{z}"] = ALONG_Z[b, 8 * z : 8 * z + 8, None] * ones
    offsets = {}
    rows = []
    start = 0
    for name, piece in pieces.items():
        offsets[name] = (start, start + piece.shape[0])
        rows.append(piece)
        start += piece.shape[0]
    return np.concatenate(rows).astype(np.float32), offsets


TABLE, OFFSETS = build_tables()


def chebyshev_steps():
    theta = 0.5 * (cheb_high + cheb_low)
    delta = 0.5 * (cheb_high - cheb_low)
    sigma = theta / delta
    rho = 1.0 / sigma
    steps = []
    for sweep in range(CHEB - 1):
        rho_next = 1.0 / (2.0 * sigma - rho)
        steps.append((rho_next * rho, 2.0 * rho_next / delta))
        rho = rho_next
    return theta, steps


THETA, STEPS = chebyshev_steps()


def table(table_ref, name):
    low, high = OFFSETS[name]
    return table_ref[low:high, :]


def lane_iota():
    return lax.broadcasted_iota(jnp.int32, (8, 128), 1)


def read(ref):
    return [[ref[i, z] for z in range(2)] for i in range(8)]


def write(ref, field):
    for i in range(8):
        for z in range(2):
            ref[i, z] = field[i][z]


def spread(row):
    return jnp.broadcast_to(row, (8, 128))


def sum_x(field, left, right):
    out = [list(pair) for pair in field]
    for z in range(2):
        out[0][z] = field[0][z] + left[z]
        out[7][z] = field[7][z] + right[z]
    return out


def sum_z(field, before, after):
    node = lax.broadcasted_iota(jnp.int32, (8, 128), 0)
    out = []
    for i in range(8):
        low, high = field[i]
        add_low = jnp.where(node == 0, spread(before(i)), jnp.where(node == 7, spread(high[0:1, :]), 0.0))
        add_high = jnp.where(node == 7, spread(after(i)), jnp.where(node == 0, spread(low[7:8, :]), 0.0))
        out.append([low + add_low, high + add_high])
    return out


def sum_y(field):
    lane = lane_iota()
    first = (lane % 8 == 0) & (lane > 0)
    last = (lane % 8 == 7) & (lane < 127)
    return [
        [
            value
            + jnp.where(
                last, pltpu.roll(value, 127, 1), jnp.where(first, pltpu.roll(value, 1, 1), 0.0)
            )
            for value in pair
        ]
        for pair in field
    ]


def wall(value):
    lane = lane_iota()
    return jnp.where((lane == 0) | (lane == 127), 0.0, value)


def each(function, *fields):
    return [[function(*(f[i][z] for f in fields)) for z in range(2)] for i in range(8)]


def metric_rows(metric_ref, m, z):
    return spread(metric_ref[2 * m + z : 2 * m + z + 1, :])


def element_apply(field, metric_ref, table_ref):
    stiff = table(table_ref, "stiff")
    stacked = jnp.concatenate([value for pair in field for value in pair], axis=0)
    along_l = jnp.dot(stacked, stiff, precision=HIGHEST, preferred_element_type=F32)
    along_j = jnp.dot(stiff, stacked, precision=HIGHEST, preferred_element_type=F32)
    out = [[None, None] for i in range(8)]
    for z in range(2):
        scale_x = metric_rows(metric_ref, 0, z) * table(table_ref, "ww")
        scale_z = metric_rows(metric_ref, 1, z) * table(table_ref, "wl")
        scale_y = metric_rows(metric_ref, 2, z) * table(table_ref, "wj")
        for p in range(8):
            along_i = K[0][p] * field[0][z]
            for i in range(1, 8):
                along_i = along_i + K[i][p] * field[i][z]
            row = 8 * (2 * p + z)
            out[p][z] = scale_x * along_i + W[p] * (
                scale_z * along_j[row : row + 8, :] + scale_y * along_l[row : row + 8, :]
            )
    return out


def diagonal_parts(metric_ref, base, table_ref, z):
    def row(m):
        return spread(metric_ref[base + 2 * m + z : base + 2 * m + z + 1, :])

    part_x = row(0) * table(table_ref, "ww")
    part_rest = row(1) * table(table_ref, "kw") + row(2) * table(table_ref, "wk")
    return part_x, part_rest


def write_x_faces(field, low_ref, high_ref):
    for z in range(2):
        low_ref[8 * z : 8 * z + 8, :] = field[0][z]
        high_ref[8 * z : 8 * z + 8, :] = field[7][z]


def write_z_faces(field, low_ref, high_ref):
    for i in range(8):
        low_ref[i : i + 1, :] = field[i][0][0:1, :]
        high_ref[i : i + 1, :] = field[i][1][7:8, :]


def halves(ref):
    return [ref[0:8, :], ref[8:16, :]]


def first_faces(load_ref, metric_ref, table_ref, rows_ref, low_ref, high_ref):
    expanded = jnp.dot(
        metric_ref[...], table(table_ref, "expand"), precision=HIGHEST, preferred_element_type=F32
    )
    rows_ref[0:6, :] = expanded
    rows_ref[6:8, :] = jnp.zeros((2, 128), F32)
    for face, ref in ((0, low_ref), (7, high_ref)):
        for z in range(2):
            ref[8 * z : 8 * z + 8, :] = load_ref[face, z]
        ref[16:22, :] = expanded
        ref[22:24, :] = jnp.zeros((2, 128), F32)


def first_z_faces(load_ref, rows_ref, left_ref, right_ref, table_ref, low_ref, high_ref):
    for z, node, ref in ((0, 0, low_ref), (1, 7, high_ref)):
        part_x, part_rest = diagonal_parts(rows_ref, 0, table_ref, z)
        for i in range(8):
            load = load_ref[i, z, node : node + 1, :]
            sum_of_x, sum_of_rest = part_x, part_rest
            if i in (0, 7):
                side = left_ref if i == 0 else right_ref
                load = load + side[8 * z + node : 8 * z + node + 1, :]
                side_x, side_rest = diagonal_parts(side, 16, table_ref, z)
                sum_of_x, sum_of_rest = part_x + side_x, part_rest + side_rest
            diagonal = KD[i] * sum_of_x + W[i] * sum_of_rest
            ref[i : i + 1, :] = load
            ref[8 + i : 9 + i, :] = diagonal[node : node + 1, :]


def send_along_z(field, extra, send_ref):
    here = lax.axis_index("gz")
    above = lax.rem(here + 1, N_GZ)
    for i in range(8):
        for chunk in range(N_GZ):
            send_ref[chunk, i : i + 1, :] = jnp.where(
                above == chunk, field[i][1][7:8, :], field[i][0][0:1, :]
            )
    for chunk in range(N_GZ):
        send_ref[chunk, 8:16, :] = extra


def send_along_x(field, extra, send_ref):
    here = lax.axis_index("gx")
    above = lax.rem(here + 1, N_GX)
    for chunk in range(N_GX):
        for z in range(2):
            send_ref[chunk, 8 * z : 8 * z + 8, :] = jnp.where(
                above == chunk, field[7][z], field[0][z]
            )
        send_ref[chunk, 16:24, :] = extra


def two_rows(first, second):
    node = lax.broadcasted_iota(jnp.int32, (8, 128), 0)
    return jnp.where(node == 0, spread(first), jnp.where(node == 1, spread(second), 0.0))


def begin(
    load_ref, rows_ref, left_ref, right_ref, before_ref, after_ref, factor_ref, table_ref,
    rhs_ref, inverse_ref, smooth_ref, applied_ref, send_ref,
):
    load = sum_x(read(load_ref), halves(left_ref), halves(right_ref))
    load = sum_z(load, lambda i: before_ref[i : i + 1, :], lambda i: after_ref[i : i + 1, :])
    rhs = each(wall, sum_y(load))
    diagonal = [[None, None] for i in range(8)]
    for z in range(2):
        part_x, part_rest = diagonal_parts(rows_ref, 0, table_ref, z)
        for i in range(8):
            sum_of_x, sum_of_rest = part_x, part_rest
            if i in (0, 7):
                side = left_ref if i == 0 else right_ref
                side_x, side_rest = diagonal_parts(side, 16, table_ref, z)
                sum_of_x, sum_of_rest = part_x + side_x, part_rest + side_rest
            diagonal[i][z] = KD[i] * sum_of_x + W[i] * sum_of_rest
    diagonal = sum_z(
        diagonal, lambda i: before_ref[8 + i : 9 + i, :], lambda i: after_ref[8 + i : 9 + i, :]
    )
    inverse = each(lambda d: wall(1.0 / d), sum_y(diagonal))
    smooth = each(lambda d, r: d * r / THETA, inverse, rhs)
    write(rhs_ref, rhs)
    write(inverse_ref, inverse)
    write(smooth_ref, smooth)
    applied = element_apply(smooth, rows_ref, table_ref)
    write(applied_ref, applied)

    mult = table(table_ref, "mult")
    weighted = [[rhs[i][z] * (mult * float(EDGE[i])) for z in range(2)] for i in range(8)]
    parts = []
    for a in range(2):
        along_x = []
        for z in range(2):
            total = float(ALONG_X[a, 0]) * weighted[0][z]
            for i in range(1, 8):
                total = total + float(ALONG_X[a, i]) * weighted[i][z]
            along_x.append(total)
        for b in range(2):
            both = (
                table(table_ref, f"bz{b}0") * along_x[0] + table(table_ref, f"bz{b}1") * along_x[1]
            )
            parts.append(jnp.sum(both, axis=0, keepdims=True))
    node = lax.broadcasted_iota(jnp.int32, (8, 128), 0)
    stacked = jnp.zeros((8, 128), F32)
    for index, part in enumerate(parts):
        stacked = jnp.where(node == index, spread(part), stacked)
    modes = lax.dot_general(
        stacked, table(table_ref, "modes"), (((1,), (1,)), ((), ())),
        precision=HIGHEST, preferred_element_type=F32,
    )
    owner = lax.broadcasted_iota(jnp.int32, (8, 32), 1) // 8
    row = lax.broadcasted_iota(jnp.int32, (8, 32), 0)
    coarse_rhs = jnp.sum(jnp.where(owner == row, modes, 0.0), axis=0, keepdims=True)
    own = jnp.dot(
        jnp.broadcast_to(coarse_rhs, (8, 32)), factor_ref[...],
        precision=HIGHEST, preferred_element_type=F32,
    )
    send_along_z(applied, two_rows(own[0:1, 0:128], own[0:1, 128:256]), send_ref)


def level_of_lane(first):
    return first + lax.broadcasted_iota(jnp.int32, (1, 128), 1) // 16


def tree_sum(rows_of, count, here, shift):
    total = jnp.zeros((1, 128), F32)
    mine = lax.shift_right_logical(jnp.full((1, 128), here, jnp.int32), shift)
    for e in range(count):
        other = lax.shift_right_logical(jnp.full((1, 128), e, jnp.int32), shift)
        total = total + jnp.where(other == mine, rows_of(e), 0.0)
    return total


def neighbours(axis, count):
    here = lax.axis_index(axis)
    return lax.rem(here + count - 1, count), lax.rem(here + 1, count)


def middle(applied_ref, received_ref, summed_ref, send_ref, *, tree):
    below, above = neighbours("gz", N_GZ)
    field = sum_z(
        read(applied_ref),
        lambda i: received_ref[below, i : i + 1, :],
        lambda i: received_ref[above, i : i + 1, :],
    )
    write(summed_ref, field)
    here = lax.axis_index("gz")
    if tree:
        first = tree_sum(lambda e: received_ref[e, 8:9, :], N_GZ, here, level_of_lane(0))
        second = tree_sum(lambda e: received_ref[e, 9:10, :], N_GZ, here, level_of_lane(8))
        extra = two_rows(first, second)
    else:
        extra = received_ref[0, 8:16, :]
        for e in range(1, N_GZ):
            extra = extra + received_ref[e, 8:16, :]
    send_along_x(field, extra, send_ref)


def x_faces_received(received_ref):
    below, above = neighbours("gx", N_GX)
    left = [received_ref[below, 8 * z : 8 * z + 8, :] for z in range(2)]
    right = [received_ref[above, 8 * z : 8 * z + 8, :] for z in range(2)]
    return left, right


def relax(step, image, rhs_ref, inverse_ref, smooth_ref, update_ref):
    first, second = STEPS[step]
    rhs, inverse, smooth, update = (
        read(rhs_ref), read(inverse_ref), read(smooth_ref), read(update_ref)
    )
    update = each(
        lambda u, d, r, a: first * u + (second * d) * (r - a), update, inverse, rhs, image
    )
    return each(lambda s, u: s + u, smooth, update), update


def after_tree(
    summed_ref, received_ref, rows_ref, rhs_ref, inverse_ref, smooth_ref, factor_ref, table_ref,
    next_ref, update_ref, coarse_ref, applied_ref, low_ref, high_ref, zlow_ref, zhigh_ref,
):
    left, right = x_faces_received(received_ref)
    image = each(wall, sum_y(sum_x(read(summed_ref), left, right)))
    smooth, update = relax(0, image, rhs_ref, inverse_ref, smooth_ref, smooth_ref)
    write(next_ref, smooth)
    write(update_ref, update)
    applied = element_apply(smooth, rows_ref, table_ref)
    write(applied_ref, applied)
    write_x_faces(applied, low_ref, high_ref)
    write_z_faces(applied, zlow_ref, zhigh_ref)

    here = lax.axis_index("gx")
    first = tree_sum(
        lambda e: received_ref[e, 16:17, :], N_GX, here, jnp.maximum(level_of_lane(0) - 4, 0)
    )
    second = tree_sum(lambda e: received_ref[e, 17:18, :], N_GX, here, level_of_lane(8) - 4)
    columns = jnp.broadcast_to(jnp.concatenate([first, second], axis=1), (8, 256))
    coarse = lax.dot_general(
        columns, factor_ref[...], (((1,), (1,)), ((), ())),
        precision=HIGHEST, preferred_element_type=F32,
    )
    owner = lax.broadcasted_iota(jnp.int32, (8, 32), 1) // 8
    row = lax.broadcasted_iota(jnp.int32, (8, 32), 0)
    across = jnp.dot(
        jnp.where(owner == row, coarse, 0.0), table(table_ref, "modes"),
        precision=HIGHEST, preferred_element_type=F32,
    )
    for z in range(2):
        along_z = []
        for a in range(2):
            along_z.append(
                table(table_ref, f"bz0{z}") * spread(across[2 * a : 2 * a + 1, :])
                + table(table_ref, f"bz1{z}") * spread(across[2 * a + 1 : 2 * a + 2, :])
            )
        for i in range(8):
            coarse_ref[i, z] = wall(
                float(ALONG_X[0, i]) * along_z[0] + float(ALONG_X[1, i]) * along_z[1]
            )


def join_edges(zlow_ref, zhigh_ref, left_ref, right_ref, low_ref, high_ref):
    for z, node, source, target in ((0, 0, zlow_ref, low_ref), (1, 7, zhigh_ref, high_ref)):
        row = 8 * z + node
        target[...] = source[...]
        target[0:1, :] = source[0:1, :] + left_ref[row : row + 1, :]
        target[7:8, :] = source[7:8, :] + right_ref[row : row + 1, :]


def assembled(applied_ref, left_ref, right_ref, before_ref, after_ref):
    field = sum_x(read(applied_ref), halves(left_ref), halves(right_ref))
    field = sum_z(field, lambda i: before_ref[i : i + 1, :], lambda i: after_ref[i : i + 1, :])
    return each(wall, sum_y(field))


def sweep_two(
    applied_ref, left_ref, right_ref, before_ref, after_ref,
    rows_ref, rhs_ref, inverse_ref, smooth_ref, update_ref, table_ref,
    next_ref, next_update_ref, out_ref, low_ref, high_ref, zlow_ref, zhigh_ref,
):
    image = assembled(applied_ref, left_ref, right_ref, before_ref, after_ref)
    smooth, update = relax(1, image, rhs_ref, inverse_ref, smooth_ref, update_ref)
    write(next_ref, smooth)
    write(next_update_ref, update)
    applied = element_apply(smooth, rows_ref, table_ref)
    write(out_ref, applied)
    write_x_faces(applied, low_ref, high_ref)
    write_z_faces(applied, zlow_ref, zhigh_ref)


def sweep_three(
    applied_ref, left_ref, right_ref, before_ref, after_ref,
    rows_ref, rhs_ref, inverse_ref, smooth_ref, update_ref, coarse_ref, load_ref, table_ref,
    precond_ref, out_ref, send_ref,
):
    image = assembled(applied_ref, left_ref, right_ref, before_ref, after_ref)
    smooth, update = relax(2, image, rhs_ref, inverse_ref, smooth_ref, update_ref)
    precond = each(lambda s, c: s + c, smooth, read(coarse_ref))
    write(precond_ref, precond)
    applied = element_apply(precond, rows_ref, table_ref)
    write(out_ref, applied)
    first = jnp.zeros((8, 128), F32)
    second = jnp.zeros((8, 128), F32)
    load = read(load_ref)
    for i in range(8):
        for z in range(2):
            first = first + load[i][z] * precond[i][z]
            second = second + applied[i][z] * precond[i][z]
    extra = two_rows(jnp.sum(first, axis=0, keepdims=True), jnp.sum(second, axis=0, keepdims=True))
    send_along_z(applied, extra, send_ref)


def finish(summed_ref, received_ref, precond_ref, rhs_ref, solution_ref, residual_ref):
    left, right = x_faces_received(received_ref)
    image = each(wall, sum_y(sum_x(read(summed_ref), left, right)))
    extra = received_ref[0, 16:24, :]
    for e in range(1, N_GX):
        extra = extra + received_ref[e, 16:24, :]
    totals = jnp.sum(extra, axis=1, keepdims=True)
    alpha = spread(totals[0:1, :] / totals[1:2, :])
    write(solution_ref, each(lambda p: alpha * p, read(precond_ref)))
    write(residual_ref, each(lambda r, a: r - alpha * a, read(rhs_ref), image))


FIELD = (8, 2, 8, 128)


def run(kernel, shapes, *operands, last=False):
    spec = pl.BlockSpec(memory_space=pltpu.VMEM)
    outs = [
        jax.ShapeDtypeStruct(shape, F32) if last else pltpu.VMEM(shape, F32) for shape in shapes
    ]
    operands = [pltpu.with_memory_space_constraint(value, pltpu.VMEM) for value in operands]
    return pl.pallas_call(
        kernel, out_shape=outs, in_specs=[spec] * len(operands), out_specs=[spec] * len(outs)
    )(*operands)


def exchange(low, high, axis):
    count = lax.axis_size(axis)
    up = [(i, (i + 1) % count) for i in range(count)]
    down = [(target, source) for source, target in up]
    return lax.ppermute(high, axis, up), lax.ppermute(low, axis, down)


def per_device(element_rhs_load, metric, coarse_factor):
    load = element_rhs_load.reshape(FIELD)
    constants = jnp.asarray(TABLE)
    factor = coarse_factor.reshape(10, 32, 16).transpose(1, 0, 2).reshape(32, 160)
    factor = jnp.pad(factor, ((0, 0), (0, 96)))
    rows, low, high = run(
        first_faces, [(8, 128), (24, 128), (24, 128)], load, metric.reshape(6, 16), constants
    )
    left, right = exchange(low, high, "gx")
    low, high = run(
        first_z_faces, [(16, 128), (16, 128)], load, rows, left, right, constants
    )
    before, after = exchange(low, high, "gz")
    rhs, inverse, smooth, applied, send = run(
        begin, [FIELD] * 4 + [(N_GZ, 16, 128)],
        load, rows, left, right, before, after, factor, constants,
    )
    received = lax.all_to_all(send, "gz", 0, 0, tiled=True)

    def middle_tree(*refs):
        middle(*refs, tree=True)

    def middle_plain(*refs):
        middle(*refs, tree=False)

    summed, send = run(middle_tree, [FIELD, (N_GX, 24, 128)], applied, received)
    received = lax.all_to_all(send, "gx", 0, 0, tiled=True)
    faces = [(16, 128)] * 2 + [(8, 128)] * 2
    smooth, update, coarse, applied, low, high, zlow, zhigh = run(
        after_tree, [FIELD] * 4 + faces,
        summed, received, rows, rhs, inverse, smooth, factor, constants,
    )
    left, right = exchange(low, high, "gx")
    zlow, zhigh = run(join_edges, [(8, 128)] * 2, zlow, zhigh, left, right)
    before, after = exchange(zlow, zhigh, "gz")
    smooth, update, applied, low, high, zlow, zhigh = run(
        sweep_two, [FIELD] * 3 + faces,
        applied, left, right, before, after, rows, rhs, inverse, smooth, update, constants,
    )
    left, right = exchange(low, high, "gx")
    zlow, zhigh = run(join_edges, [(8, 128)] * 2, zlow, zhigh, left, right)
    before, after = exchange(zlow, zhigh, "gz")
    precond, applied, send = run(
        sweep_three, [FIELD] * 2 + [(N_GZ, 16, 128)],
        applied, left, right, before, after,
        rows, rhs, inverse, smooth, update, coarse, load, constants,
    )
    received = lax.all_to_all(send, "gz", 0, 0, tiled=True)
    summed, send = run(middle_plain, [FIELD, (N_GX, 24, 128)], applied, received)
    received = lax.all_to_all(send, "gx", 0, 0, tiled=True)
    solution_field, residual = run(
        finish, [FIELD] * 2, summed, received, precond, rhs, last=True
    )
    shape = element_rhs_load.shape
    return solution_field.reshape(shape), residual.reshape(shape)


def solution(mesh):
    placed = (
        P("gx", None, "gz", None, None),
        P(None, "gx", "gz", None),
        P("gx", "gz", None, None, None),
    )
    return jax.shard_map(
        per_device,
        mesh=mesh,
        in_specs=placed,
        out_specs=(P("gx", None, "gz", None, None), P("gx", None, "gz", None, None)),
        check_vma=False,
    )
```

```python
import jax
import jax.numpy as jnp
import numpy as np
from jax import lax
from jax.experimental import pallas as pl
from jax.experimental.pallas import tpu as pltpu
from jax.sharding import PartitionSpec as P

CHEB = 4
N_GX = 32
N_GZ = 16
F32 = jnp.float32
HIGHEST = lax.Precision.HIGHEST

cheb_high = 2.0
cheb_low = 0.1
gll_inner = (
    -0.8717401485096066,
    -0.5917001814331423,
    -0.2092992179024789,
    0.2092992179024789,
    0.5917001814331423,
    0.8717401485096066,
)


def legendre_seven(points):
    before = np.ones(points.shape[0])
    current = points.copy()
    for degree in range(1, 7):
        following = ((2.0 * degree + 1.0) * points * current - degree * before) / (degree + 1.0)
        before = current
        current = following
    return current


def gll_tables():
    order = 7
    points = np.concatenate([[-1.0], np.array(gll_inner), [1.0]])
    values = legendre_seven(points)
    weights = 2.0 / (order * (order + 1) * values**2)
    count = order + 1
    deriv = np.zeros((count, count))
    for row_index in range(count):
        for col_index in range(count):
            if row_index != col_index:
                deriv[row_index, col_index] = values[row_index] / (
                    values[col_index] * (points[row_index] - points[col_index])
                )
    deriv[0, 0] = -order * (order + 1) / 4.0
    deriv[-1, -1] = order * (order + 1) / 4.0
    stiff = deriv.T @ (weights[:, None] * deriv)
    return (points, weights, stiff)


POINTS, WEIGHTS, STIFF = gll_tables()
KDIAG = np.diag(STIFF)
W = [float(v) for v in WEIGHTS]
KD = [float(v) for v in KDIAG]
K = [[float(v) for v in row] for row in STIFF]


def positions(count):
    return ((np.arange(count)[:, None] + (1.0 + POINTS[None, :]) / 2.0) / count).reshape(-1)


ALONG_X = np.stack([np.sin(np.pi * mode * positions(1)) for mode in (1, 2)])
ALONG_Z = np.stack([np.sin(np.pi * mode * positions(2)) for mode in (1, 2)])
ALONG_Y = np.stack([np.sin(np.pi * mode * positions(16)) for mode in range(1, 9)])
EDGE = np.array([0.5] + [1.0] * 6 + [0.5])


def build_tables():
    w_l = np.tile(WEIGHTS, 16)[None, :]
    k_l = np.tile(KDIAG, 16)[None, :]
    w_j = WEIGHTS[:, None]
    k_j = KDIAG[:, None]
    ones = np.ones((1, 128))
    across = np.ones(128)
    across[8::8] = 0.5
    across[7:127:8] = 0.5
    pieces = {
        "stiff": np.kron(np.eye(16), STIFF),
        "ww": w_j * w_l,
        "kw": k_j * w_l,
        "wk": w_j * k_l,
        "wl": np.ones((8, 1)) * w_l,
        "wj": w_j * ones,
        "mult": EDGE[:, None] * across[None, :],
        "expand": np.kron(np.eye(16), np.ones((1, 8))),
        "modes": np.tile(ALONG_Y, (4, 1)),
    }
    for b in range(2):
        for z in range(2):
            pieces[f"bz{b}{z}"] = ALONG_Z[b, 8 * z : 8 * z + 8, None] * ones
    offsets = {}
    rows = []
    start = 0
    for name, piece in pieces.items():
        offsets[name] = (start, start + piece.shape[0])
        rows.append(piece)
        start += piece.shape[0]
    return np.concatenate(rows).astype(np.float32), offsets


TABLE, OFFSETS = build_tables()


def chebyshev_steps():
    theta = 0.5 * (cheb_high + cheb_low)
    delta = 0.5 * (cheb_high - cheb_low)
    sigma = theta / delta
    rho = 1.0 / sigma
    steps = []
    for sweep in range(CHEB - 1):
        rho_next = 1.0 / (2.0 * sigma - rho)
        steps.append((rho_next * rho, 2.0 * rho_next / delta))
        rho = rho_next
    return theta, steps


THETA, STEPS = chebyshev_steps()


def table(table_ref, name):
    low, high = OFFSETS[name]
    return table_ref[low:high, :]


def lane_iota():
    return lax.broadcasted_iota(jnp.int32, (8, 128), 1)


def read(ref, first=0, count=2):
    return [[ref[i, c] for c in range(first, first + count)] for i in range(8)]


def write(ref, field):
    for i in range(8):
        for c, value in enumerate(field[i]):
            ref[i, c] = value


def spread(row):
    return jnp.broadcast_to(row, (8, 128))


def sum_x(field, left, right):
    out = [list(row) for row in field]
    for c in range(len(field[0])):
        out[0][c] = field[0][c] + left[c]
        out[7][c] = field[7][c] + right[c]
    return out


def sum_z(field, before=None, after=None):
    node = lax.broadcasted_iota(jnp.int32, (8, 128), 0)
    count = len(field[0])
    out = []
    for i in range(8):
        lows = [None] + [field[i][c][7:8, :] for c in range(count - 1)]
        highs = [field[i][c][0:1, :] for c in range(1, count)] + [None]
        if before is not None:
            lows[0], highs[-1] = before(i), after(i)
        out.append(
            [
                field[i][c]
                + jnp.where(node == 0, spread(lows[c]), jnp.where(node == 7, spread(highs[c]), 0.0))
                for c in range(count)
                if lows[c] is not None and highs[c] is not None
            ]
        )
    return out


def sum_y(field):
    lane = lane_iota()
    first = (lane % 8 == 0) & (lane > 0)
    last = (lane % 8 == 7) & (lane < 127)
    return each(
        lambda value: value
        + jnp.where(last, pltpu.roll(value, 127, 1), jnp.where(first, pltpu.roll(value, 1, 1), 0.0)),
        field,
    )


def wall(value):
    lane = lane_iota()
    return jnp.where((lane == 0) | (lane == 127), 0.0, value)


def each(function, *fields):
    return [[function(*values) for values in zip(*rows)] for rows in zip(*fields)]


ROWS = 10


def metric_row(ref, base, m, column):
    row = base + ROWS * m + 4 + column
    return ref[row : row + 1, :]


def element_apply(field, first, metric_ref, table_ref):
    count = len(field[0])
    stiff = table(table_ref, "stiff")
    out = [[None] * count for i in range(8)]
    for c in range(count):
        stacked = jnp.concatenate([field[i][c] for i in range(8)], axis=0)
        along_l = jnp.dot(stacked, stiff, precision=HIGHEST, preferred_element_type=F32)
        along_j = jnp.dot(
            stiff[0:64, 0:64], stacked, precision=HIGHEST, preferred_element_type=F32
        )
        rows = [spread(metric_row(metric_ref, 0, m, first + c)) for m in range(3)]
        scale_x = rows[0] * table(table_ref, "ww")
        scale_z = rows[1] * table(table_ref, "wl")
        scale_y = rows[2] * table(table_ref, "wj")
        for p in range(8):
            along_i = K[0][p] * field[0][c]
            for i in range(1, 8):
                along_i = along_i + K[i][p] * field[i][c]
            out[p][c] = scale_x * along_i + W[p] * (
                scale_z * along_j[8 * p : 8 * p + 8, :] + scale_y * along_l[8 * p : 8 * p + 8, :]
            )
    return out


def diagonal_parts(ref, base, column, table_ref):
    part_x = spread(metric_row(ref, base, 0, column)) * table(table_ref, "ww")
    part_rest = spread(metric_row(ref, base, 1, column)) * table(table_ref, "kw") + spread(
        metric_row(ref, base, 2, column)
    ) * table(table_ref, "wk")
    return part_x, part_rest


def diagonal_sum_x(rows_ref, left_ref, right_ref, column, table_ref):
    part_x, part_rest = diagonal_parts(rows_ref, 0, column, table_ref)
    out = []
    for i in range(8):
        sum_of_x, sum_of_rest = part_x, part_rest
        if i in (0, 7):
            side = left_ref if i == 0 else right_ref
            side_x, side_rest = diagonal_parts(side, FACE_METRIC, column, table_ref)
            sum_of_x, sum_of_rest = part_x + side_x, part_rest + side_rest
        out.append(KD[i] * sum_of_x + W[i] * sum_of_rest)
    return out


def write_x_faces(field, low_ref, high_ref):
    for c in range(len(field[0])):
        low_ref[8 * c : 8 * c + 8, :] = field[0][c]
        high_ref[8 * c : 8 * c + 8, :] = field[7][c]


def faces(ref, count):
    return [ref[8 * c : 8 * c + 8, :] for c in range(count)]


def pack(load_ref, metric_ref, table_ref, near_ref, up_ref, down_ref):
    expanded = jnp.dot(
        metric_ref[...], table(table_ref, "expand"), precision=HIGHEST, preferred_element_type=F32
    )
    for ref, start in ((near_ref, 128), (up_ref, 72), (down_ref, 72)):
        ref[start : start + 6, :] = expanded
        ref[start + 6 : start + 8, :] = jnp.zeros((2, 128), F32)
    for i in range(8):
        for z in range(2):
            near_ref[8 * (2 * i + z) : 8 * (2 * i + z) + 8, :] = load_ref[i, z]
        up_ref[8 * i : 8 * i + 8, :] = load_ref[i, 1]
        up_ref[64 + i : 65 + i, :] = load_ref[i, 0, 7:8, :]
        down_ref[8 * i : 8 * i + 8, :] = load_ref[i, 0]
        down_ref[64 + i : 65 + i, :] = load_ref[i, 1, 0:1, :]


FACE_METRIC = 72
FACE_ROWS = 104


def gather(
    near_ref, below_ref, far_below_ref, above_ref, far_above_ref,
    load_ref, edge_ref, rows_ref, low_ref, high_ref,
):
    for i in range(8):
        load_ref[i, 0] = far_below_ref[8 * i : 8 * i + 8, :]
        load_ref[i, 7] = far_above_ref[8 * i : 8 * i + 8, :]
        for z in range(2):
            start = 8 * (2 * i + z)
            load_ref[i, 1 + z] = below_ref[start : start + 8, :]
            load_ref[i, 3 + z] = near_ref[start : start + 8, :]
            load_ref[i, 5 + z] = above_ref[start : start + 8, :]
    edge_ref[0:8, :] = far_below_ref[64:72, :]
    edge_ref[8:16, :] = far_above_ref[64:72, :]
    sources = (
        (far_below_ref, 72), (below_ref, 128), (near_ref, 128), (above_ref, 128), (far_above_ref, 72),
    )
    for index, (source, start) in enumerate(sources):
        for m in range(3):
            row = ROWS * m + 2 * index
            rows_ref[row : row + 2, :] = source[start + 2 * m : start + 2 * m + 2, :]
    rows_ref[30:32, :] = jnp.zeros((2, 128), F32)
    rows = rows_ref[...]
    for face, ref in ((0, low_ref), (7, high_ref)):
        for c in range(8):
            ref[8 * c : 8 * c + 8, :] = load_ref[face, c]
        ref[64:65, :] = far_below_ref[64 + face : 65 + face, :]
        ref[65:66, :] = far_above_ref[64 + face : 65 + face, :]
        ref[66:72, :] = jnp.zeros((6, 128), F32)
        ref[FACE_METRIC:FACE_ROWS, :] = rows


def send_along_z(field, extra, send_ref):
    here = lax.axis_index("gz")
    above = lax.rem(here + 1, N_GZ)
    for i in range(8):
        for chunk in range(N_GZ):
            send_ref[chunk, i : i + 1, :] = jnp.where(
                above == chunk, field[i][1][7:8, :], field[i][0][0:1, :]
            )
    for chunk in range(N_GZ):
        send_ref[chunk, 8:16, :] = extra


def send_along_x(field, extra, send_ref):
    here = lax.axis_index("gx")
    above = lax.rem(here + 1, N_GX)
    for chunk in range(N_GX):
        for z in range(2):
            send_ref[chunk, 8 * z : 8 * z + 8, :] = jnp.where(
                above == chunk, field[7][z], field[0][z]
            )
        send_ref[chunk, 16:24, :] = extra


def two_rows(first, second):
    node = lax.broadcasted_iota(jnp.int32, (8, 128), 0)
    return jnp.where(node == 0, spread(first), jnp.where(node == 1, spread(second), 0.0))


def begin(
    load_ref, edge_ref, rows_ref, left_ref, right_ref, factor_ref, table_ref,
    rhs_ref, inverse_ref, smooth_ref, applied_ref, low_ref, high_ref, send_ref,
):
    def edge(which):
        start = 8 * which

        def row(i):
            value = edge_ref[start + i : start + i + 1, :]
            if i == 0:
                value = value + left_ref[64 + which : 65 + which, :]
            if i == 7:
                value = value + right_ref[64 + which : 65 + which, :]
            return value

        return row

    load = sum_x(read(load_ref, 0, 8), faces(left_ref, 8), faces(right_ref, 8))
    rhs = each(wall, sum_y(sum_z(load, edge(0), edge(1))))
    columns = [
        diagonal_sum_x(rows_ref, left_ref, right_ref, column, table_ref) for column in range(-4, 6)
    ]
    diagonal = sum_z([[columns[c][i] for c in range(10)] for i in range(8)])
    inverse = each(lambda d: wall(1.0 / d), sum_y(diagonal))
    smooth = each(lambda d, r: d * r / THETA, inverse, rhs)
    write(rhs_ref, [row[1:7] for row in rhs])
    write(inverse_ref, [row[1:7] for row in inverse])
    write(smooth_ref, [row[1:7] for row in smooth])
    applied = element_apply(smooth, -3, rows_ref, table_ref)
    write(applied_ref, applied)
    write_x_faces(applied, low_ref, high_ref)

    mult = table(table_ref, "mult")
    weighted = [[rhs[i][3 + z] * (mult * float(EDGE[i])) for z in range(2)] for i in range(8)]
    parts = []
    for a in range(2):
        along_x = []
        for z in range(2):
            total = float(ALONG_X[a, 0]) * weighted[0][z]
            for i in range(1, 8):
                total = total + float(ALONG_X[a, i]) * weighted[i][z]
            along_x.append(total)
        for b in range(2):
            both = (
                table(table_ref, f"bz{b}0") * along_x[0] + table(table_ref, f"bz{b}1") * along_x[1]
            )
            parts.append(jnp.sum(both, axis=0, keepdims=True))
    node = lax.broadcasted_iota(jnp.int32, (8, 128), 0)
    stacked = jnp.zeros((8, 128), F32)
    for index, part in enumerate(parts):
        stacked = jnp.where(node == index, spread(part), stacked)
    modes = lax.dot_general(
        stacked, table(table_ref, "modes"), (((1,), (1,)), ((), ())),
        precision=HIGHEST, preferred_element_type=F32,
    )
    owner = lax.broadcasted_iota(jnp.int32, (8, 32), 1) // 8
    row = lax.broadcasted_iota(jnp.int32, (8, 32), 0)
    coarse_rhs = jnp.sum(jnp.where(owner == row, modes, 0.0), axis=0, keepdims=True)
    own = jnp.dot(
        jnp.broadcast_to(coarse_rhs, (8, 32)), factor_ref[...],
        precision=HIGHEST, preferred_element_type=F32,
    )
    for chunk in range(N_GZ):
        send_ref[chunk, 0:1, :] = own[0:1, 0:128]
        send_ref[chunk, 1:2, :] = own[0:1, 128:256]


def level_of_lane(first):
    return first + lax.broadcasted_iota(jnp.int32, (1, 128), 1) // 16


def tree_sum(rows_of, count, here, shift):
    total = jnp.zeros((1, 128), F32)
    mine = lax.shift_right_logical(jnp.full((1, 128), here, jnp.int32), shift)
    for e in range(count):
        other = lax.shift_right_logical(jnp.full((1, 128), e, jnp.int32), shift)
        total = total + jnp.where(other == mine, rows_of(e), 0.0)
    return total


def neighbours(axis, count):
    here = lax.axis_index(axis)
    return lax.rem(here + count - 1, count), lax.rem(here + 1, count)


def lower_tree(received_ref, send_ref):
    here = lax.axis_index("gz")
    for row in range(2):
        total = tree_sum(
            lambda e: received_ref[e, row : row + 1, :], N_GZ, here, level_of_lane(8 * row)
        )
        for chunk in range(N_GX):
            send_ref[chunk, row : row + 1, :] = total


def middle(applied_ref, received_ref, summed_ref, send_ref):
    below, above = neighbours("gz", N_GZ)
    field = sum_z(
        read(applied_ref),
        lambda i: received_ref[below, i : i + 1, :],
        lambda i: received_ref[above, i : i + 1, :],
    )
    write(summed_ref, field)
    extra = received_ref[0, 8:16, :]
    for e in range(1, N_GZ):
        extra = extra + received_ref[e, 8:16, :]
    send_along_x(field, extra, send_ref)


def x_faces_received(received_ref):
    below, above = neighbours("gx", N_GX)
    left = [received_ref[below, 8 * z : 8 * z + 8, :] for z in range(2)]
    right = [received_ref[above, 8 * z : 8 * z + 8, :] for z in range(2)]
    return left, right


def relax(step, count, applied_ref, left_ref, right_ref, rhs_ref, inverse_ref, smooth_ref, update_ref):
    field = sum_x(
        read(applied_ref, 0, count + 2), faces(left_ref, count + 2), faces(right_ref, count + 2)
    )
    image = each(wall, sum_y(sum_z(field)))
    first, second = STEPS[step]
    inset = (6 - count) // 2
    shift = 1 if step else 0
    update = each(
        lambda u, d, r, a: first * u + (second * d) * (r - a),
        read(update_ref, shift, count), read(inverse_ref, inset, count), read(rhs_ref, inset, count),
        image,
    )
    return each(lambda s, u: s + u, read(smooth_ref, shift, count), update), update


def sweep(
    applied_ref, left_ref, right_ref, rhs_ref, inverse_ref, smooth_ref, update_ref, rows_ref, table_ref,
    next_ref, next_update_ref, out_ref, low_ref, high_ref, *, step, count,
):
    smooth, update = relax(
        step, count, applied_ref, left_ref, right_ref, rhs_ref, inverse_ref, smooth_ref, update_ref
    )
    write(next_ref, smooth)
    write(next_update_ref, update)
    applied = element_apply(smooth, 1 - count // 2, rows_ref, table_ref)
    write(out_ref, applied)
    write_x_faces(applied, low_ref, high_ref)


def coarse_field(received_ref, factor_ref, table_ref):
    here = lax.axis_index("gx")
    first = tree_sum(
        lambda e: received_ref[e, 0:1, :], N_GX, here, jnp.maximum(level_of_lane(0) - 4, 0)
    )
    second = tree_sum(lambda e: received_ref[e, 1:2, :], N_GX, here, level_of_lane(8) - 4)
    columns = jnp.broadcast_to(jnp.concatenate([first, second], axis=1), (8, 256))
    coarse = lax.dot_general(
        columns, factor_ref[...], (((1,), (1,)), ((), ())),
        precision=HIGHEST, preferred_element_type=F32,
    )
    owner = lax.broadcasted_iota(jnp.int32, (8, 32), 1) // 8
    row = lax.broadcasted_iota(jnp.int32, (8, 32), 0)
    across = jnp.dot(
        jnp.where(owner == row, coarse, 0.0), table(table_ref, "modes"),
        precision=HIGHEST, preferred_element_type=F32,
    )
    out = [[None, None] for i in range(8)]
    for z in range(2):
        along_z = []
        for a in range(2):
            along_z.append(
                table(table_ref, f"bz0{z}") * spread(across[2 * a : 2 * a + 1, :])
                + table(table_ref, f"bz1{z}") * spread(across[2 * a + 1 : 2 * a + 2, :])
            )
        for i in range(8):
            out[i][z] = wall(float(ALONG_X[0, i]) * along_z[0] + float(ALONG_X[1, i]) * along_z[1])
    return out


def last_sweep(
    applied_ref, left_ref, right_ref, rhs_ref, inverse_ref, smooth_ref, update_ref, rows_ref,
    tree_ref, factor_ref, near_ref, table_ref,
    precond_ref, out_ref, send_ref,
):
    smooth, update = relax(
        2, 2, applied_ref, left_ref, right_ref, rhs_ref, inverse_ref, smooth_ref, update_ref
    )
    coarse = coarse_field(tree_ref, factor_ref, table_ref)
    precond = each(lambda s, c: s + c, smooth, coarse)
    write(precond_ref, precond)
    applied = element_apply(precond, 0, rows_ref, table_ref)
    write(out_ref, applied)
    first = jnp.zeros((8, 128), F32)
    second = jnp.zeros((8, 128), F32)
    for i in range(8):
        for z in range(2):
            start = 8 * (2 * i + z)
            first = first + near_ref[start : start + 8, :] * precond[i][z]
            second = second + applied[i][z] * precond[i][z]
    extra = two_rows(jnp.sum(first, axis=0, keepdims=True), jnp.sum(second, axis=0, keepdims=True))
    send_along_z(applied, extra, send_ref)


def finish(summed_ref, received_ref, precond_ref, rhs_ref, solution_ref, residual_ref):
    left, right = x_faces_received(received_ref)
    image = each(wall, sum_y(sum_x(read(summed_ref), left, right)))
    extra = received_ref[0, 16:24, :]
    for e in range(1, N_GX):
        extra = extra + received_ref[e, 16:24, :]
    totals = jnp.sum(extra, axis=1, keepdims=True)
    alpha = spread(totals[0:1, :] / totals[1:2, :])
    write(solution_ref, each(lambda p: alpha * p, read(precond_ref)))
    write(residual_ref, each(lambda r, a: r - alpha * a, read(rhs_ref, 2, 2), image))


def field_shape(count):
    return (8, count, 8, 128)


def run(kernel, shapes, *operands, last=False):
    spec = pl.BlockSpec(memory_space=pltpu.VMEM)
    outs = [
        jax.ShapeDtypeStruct(shape, F32) if last else pltpu.VMEM(shape, F32) for shape in shapes
    ]
    operands = [pltpu.with_memory_space_constraint(value, pltpu.VMEM) for value in operands]
    return pl.pallas_call(
        kernel, out_shape=outs, in_specs=[spec] * len(operands), out_specs=[spec] * len(outs)
    )(*operands)


def shifted(value, axis, distance):
    count = lax.axis_size(axis)
    return lax.ppermute(value, axis, [(i, (i + distance) % count) for i in range(count)])


def exchange(low, high, axis):
    return shifted(high, axis, 1), shifted(low, axis, -1)


def per_device(element_rhs_load, metric, coarse_factor):
    load = element_rhs_load.reshape(field_shape(2))
    constants = jnp.asarray(TABLE)
    factor = coarse_factor.reshape(10, 32, 16).transpose(1, 0, 2).reshape(32, 160)
    factor = jnp.pad(factor, ((0, 0), (0, 96)))
    near, up, down = run(
        pack, [(136, 128), (80, 128), (80, 128)], load, metric.reshape(6, 16), constants
    )
    below, far_below = shifted(near, "gz", 1), shifted(up, "gz", 2)
    above, far_above = shifted(near, "gz", -1), shifted(down, "gz", -2)
    wide, edge, rows, low, high = run(
        gather, [field_shape(8), (16, 128), (32, 128)] + [(FACE_ROWS, 128)] * 2,
        near, below, far_below, above, far_above,
    )
    left, right = exchange(low, high, "gx")
    rhs, inverse, smooth, applied, low, high, send = run(
        begin, [field_shape(6)] * 3 + [field_shape(8)] + [(64, 128)] * 2 + [(N_GZ, 2, 128)],
        wide, edge, rows, left, right, factor, constants,
    )
    tree = lax.all_to_all(send, "gz", 0, 0, tiled=True)
    left, right = exchange(low, high, "gx")
    update = smooth
    for step, count in ((0, 6), (1, 4)):

        def stage(*refs, step=step, count=count):
            sweep(*refs, step=step, count=count)

        smooth, update, applied, low, high = run(
            stage, [field_shape(count)] * 3 + [(8 * count, 128)] * 2,
            applied, left, right, rhs, inverse, smooth, update, rows, constants,
        )
        left, right = exchange(low, high, "gx")
        if step == 0:
            (send,) = run(lower_tree, [(N_GX, 2, 128)], tree)
            tree = lax.all_to_all(send, "gx", 0, 0, tiled=True)
    precond, applied, send = run(
        last_sweep, [field_shape(2)] * 2 + [(N_GZ, 16, 128)],
        applied, left, right, rhs, inverse, smooth, update, rows, tree, factor, near, constants,
    )
    received = lax.all_to_all(send, "gz", 0, 0, tiled=True)
    summed, send = run(middle, [field_shape(2), (N_GX, 24, 128)], applied, received)
    received = lax.all_to_all(send, "gx", 0, 0, tiled=True)
    solution_field, residual = run(
        finish, [field_shape(2)] * 2, summed, received, precond, rhs, last=True
    )
    shape = element_rhs_load.shape
    return solution_field.reshape(shape), residual.reshape(shape)


def solution(mesh):
    placed = (
        P("gx", None, "gz", None, None),
        P(None, "gx", "gz", None),
        P("gx", "gz", None, None, None),
    )
    return jax.shard_map(
        per_device,
        mesh=mesh,
        in_specs=placed,
        out_specs=(P("gx", None, "gz", None, None), P("gx", None, "gz", None, None)),
        check_vma=False,
    )
```

```python
import jax
import jax.numpy as jnp
import numpy as np
from jax import lax
from jax.experimental import pallas as pl
from jax.experimental.pallas import tpu as pltpu
from jax.sharding import PartitionSpec as P

CHEB = 4
N_GX = 32
N_GZ = 16
DEVICES = N_GX * N_GZ
F32 = jnp.float32
HIGHEST = lax.Precision.HIGHEST

cheb_high = 2.0
cheb_low = 0.1
gll_inner = (
    -0.8717401485096066,
    -0.5917001814331423,
    -0.2092992179024789,
    0.2092992179024789,
    0.5917001814331423,
    0.8717401485096066,
)


def legendre_seven(points):
    before = np.ones(points.shape[0])
    current = points.copy()
    for degree in range(1, 7):
        following = ((2.0 * degree + 1.0) * points * current - degree * before) / (degree + 1.0)
        before = current
        current = following
    return current


def gll_tables():
    order = 7
    points = np.concatenate([[-1.0], np.array(gll_inner), [1.0]])
    values = legendre_seven(points)
    weights = 2.0 / (order * (order + 1) * values**2)
    count = order + 1
    deriv = np.zeros((count, count))
    for row_index in range(count):
        for col_index in range(count):
            if row_index != col_index:
                deriv[row_index, col_index] = values[row_index] / (
                    values[col_index] * (points[row_index] - points[col_index])
                )
    deriv[0, 0] = -order * (order + 1) / 4.0
    deriv[-1, -1] = order * (order + 1) / 4.0
    stiff = deriv.T @ (weights[:, None] * deriv)
    return (points, weights, stiff)


POINTS, WEIGHTS, STIFF = gll_tables()
KDIAG = np.diag(STIFF)
W = [float(v) for v in WEIGHTS]
KD = [float(v) for v in KDIAG]
K = [[float(v) for v in row] for row in STIFF]


def positions(count):
    return ((np.arange(count)[:, None] + (1.0 + POINTS[None, :]) / 2.0) / count).reshape(-1)


ALONG_X = np.stack([np.sin(np.pi * mode * positions(1)) for mode in (1, 2)])
ALONG_Z = np.stack([np.sin(np.pi * mode * positions(2)) for mode in (1, 2)])
ALONG_Y = np.stack([np.sin(np.pi * mode * positions(16)) for mode in range(1, 9)])
EDGE = np.array([0.5] + [1.0] * 6 + [0.5])


def build_tables():
    w_l = np.tile(WEIGHTS, 16)[None, :]
    k_l = np.tile(KDIAG, 16)[None, :]
    w_j = WEIGHTS[:, None]
    k_j = KDIAG[:, None]
    ones = np.ones((1, 128))
    across = np.ones(128)
    across[8::8] = 0.5
    across[7:127:8] = 0.5
    pieces = {
        "stiff": np.kron(np.eye(16), STIFF),
        "ww": w_j * w_l,
        "kw": k_j * w_l,
        "wk": w_j * k_l,
        "wl": np.ones((8, 1)) * w_l,
        "wj": w_j * ones,
        "mult": EDGE[:, None] * across[None, :],
        "modes": np.tile(ALONG_Y, (4, 1)),
    }
    for b in range(2):
        for z in range(2):
            pieces[f"bz{b}{z}"] = ALONG_Z[b, 8 * z : 8 * z + 8, None] * ones
    offsets = {}
    rows = []
    start = 0
    for name, piece in pieces.items():
        offsets[name] = (start, start + piece.shape[0])
        rows.append(piece)
        start += piece.shape[0]
    return np.concatenate(rows).astype(np.float32), offsets


TABLE, OFFSETS = build_tables()


def chebyshev_steps():
    theta = 0.5 * (cheb_high + cheb_low)
    delta = 0.5 * (cheb_high - cheb_low)
    sigma = theta / delta
    rho = 1.0 / sigma
    steps = []
    for sweep in range(CHEB - 1):
        rho_next = 1.0 / (2.0 * sigma - rho)
        steps.append((rho_next * rho, 2.0 * rho_next / delta))
        rho = rho_next
    return theta, steps


THETA, STEPS = chebyshev_steps()


def table(table_ref, name):
    low, high = OFFSETS[name]
    return table_ref[low:high, :]


def lane_iota():
    return lax.broadcasted_iota(jnp.int32, (8, 128), 1)


def read(ref, first=0, count=2):
    return [[ref[i, c] for c in range(first, first + count)] for i in range(8)]


def write(ref, field):
    for i in range(8):
        for c, value in enumerate(field[i]):
            ref[i, c] = value


def spread(row):
    return jnp.broadcast_to(row, (8, 128))


def sum_x(field, left, right):
    out = [list(row) for row in field]
    for c in range(len(field[0])):
        out[0][c] = field[0][c] + left[c]
        out[7][c] = field[7][c] + right[c]
    return out


def sum_z(field, before=None, after=None):
    node = lax.broadcasted_iota(jnp.int32, (8, 128), 0)
    count = len(field[0])
    out = []
    for i in range(8):
        lows = [None] + [field[i][c][7:8, :] for c in range(count - 1)]
        highs = [field[i][c][0:1, :] for c in range(1, count)] + [None]
        if before is not None:
            lows[0], highs[-1] = before(i), after(i)
        out.append(
            [
                field[i][c]
                + jnp.where(node == 0, spread(lows[c]), jnp.where(node == 7, spread(highs[c]), 0.0))
                for c in range(count)
                if lows[c] is not None and highs[c] is not None
            ]
        )
    return out


def sum_y(field):
    lane = lane_iota()
    first = (lane % 8 == 0) & (lane > 0)
    last = (lane % 8 == 7) & (lane < 127)
    return each(
        lambda value: value
        + jnp.where(last, pltpu.roll(value, 127, 1), jnp.where(first, pltpu.roll(value, 1, 1), 0.0)),
        field,
    )


def wall(value):
    lane = lane_iota()
    return jnp.where((lane == 0) | (lane == 127), 0.0, value)


def each(function, *fields):
    return [[function(*values) for values in zip(*rows)] for rows in zip(*fields)]


ROWS = 10


def metric_row(ref, base, m, column):
    row = base + ROWS * m + 4 + column
    return ref[row : row + 1, :]


def element_apply(field, first, metric_ref, table_ref):
    count = len(field[0])
    stiff = table(table_ref, "stiff")
    out = [[None] * count for i in range(8)]
    for c in range(count):
        stacked = jnp.concatenate([field[i][c] for i in range(8)], axis=0)
        along_l = jnp.dot(stacked, stiff, precision=HIGHEST, preferred_element_type=F32)
        along_j = jnp.dot(
            stiff[0:64, 0:64], stacked, precision=HIGHEST, preferred_element_type=F32
        )
        rows = [spread(metric_row(metric_ref, 0, m, first + c)) for m in range(3)]
        scale_x = rows[0] * table(table_ref, "ww")
        scale_z = rows[1] * table(table_ref, "wl")
        scale_y = rows[2] * table(table_ref, "wj")
        for p in range(8):
            along_i = K[0][p] * field[0][c]
            for i in range(1, 8):
                along_i = along_i + K[i][p] * field[i][c]
            out[p][c] = scale_x * along_i + W[p] * (
                scale_z * along_j[8 * p : 8 * p + 8, :] + scale_y * along_l[8 * p : 8 * p + 8, :]
            )
    return out


def diagonal_parts(ref, base, column, table_ref):
    part_x = spread(metric_row(ref, base, 0, column)) * table(table_ref, "ww")
    part_rest = spread(metric_row(ref, base, 1, column)) * table(table_ref, "kw") + spread(
        metric_row(ref, base, 2, column)
    ) * table(table_ref, "wk")
    return part_x, part_rest


def diagonal_sum_x(rows_ref, left_ref, right_ref, column, table_ref):
    part_x, part_rest = diagonal_parts(rows_ref, 0, column, table_ref)
    out = []
    for i in range(8):
        sum_of_x, sum_of_rest = part_x, part_rest
        if i in (0, 7):
            side = left_ref if i == 0 else right_ref
            side_x, side_rest = diagonal_parts(side, FACE_METRIC, column, table_ref)
            sum_of_x, sum_of_rest = part_x + side_x, part_rest + side_rest
        out.append(KD[i] * sum_of_x + W[i] * sum_of_rest)
    return out


def write_x_faces(field, low_ref, high_ref):
    for c in range(len(field[0])):
        low_ref[8 * c : 8 * c + 8, :] = field[0][c]
        high_ref[8 * c : 8 * c + 8, :] = field[7][c]


def faces(ref, count):
    return [ref[8 * c : 8 * c + 8, :] for c in range(count)]


def pack(load_ref, metric_ref, near_ref, up_ref, down_ref):
    element = lax.broadcasted_iota(jnp.int32, (16, 128), 0)
    lane = lax.broadcasted_iota(jnp.int32, (16, 128), 1)
    expand = jnp.where(element == lane // 8, 1.0, 0.0)
    for ref, start in ((near_ref, 128), (up_ref, 72), (down_ref, 72)):
        ref[start + 6 : start + 8, :] = jnp.zeros((2, 128), F32)
    for m in range(3):
        expanded = jnp.dot(
            metric_ref[m, 0], expand, precision=HIGHEST, preferred_element_type=F32
        )
        for ref, start in ((near_ref, 128), (up_ref, 72), (down_ref, 72)):
            ref[start + 2 * m : start + 2 * m + 2, :] = expanded
    for i in range(8):
        for z in range(2):
            near_ref[8 * (2 * i + z) : 8 * (2 * i + z) + 8, :] = load_ref[0, i, z]
        up_ref[8 * i : 8 * i + 8, :] = load_ref[0, i, 1]
        up_ref[64 + i : 65 + i, :] = load_ref[0, i, 0, 7:8, :]
        down_ref[8 * i : 8 * i + 8, :] = load_ref[0, i, 0]
        down_ref[64 + i : 65 + i, :] = load_ref[0, i, 1, 0:1, :]


FACE_METRIC = 72
FACE_ROWS = 104


def gather(
    near_ref, below_ref, far_below_ref, above_ref, far_above_ref,
    load_ref, edge_ref, rows_ref, low_ref, high_ref,
):
    for i in range(8):
        load_ref[i, 0] = far_below_ref[8 * i : 8 * i + 8, :]
        load_ref[i, 7] = far_above_ref[8 * i : 8 * i + 8, :]
        for z in range(2):
            start = 8 * (2 * i + z)
            load_ref[i, 1 + z] = below_ref[start : start + 8, :]
            load_ref[i, 3 + z] = near_ref[start : start + 8, :]
            load_ref[i, 5 + z] = above_ref[start : start + 8, :]
    edge_ref[0:8, :] = far_below_ref[64:72, :]
    edge_ref[8:16, :] = far_above_ref[64:72, :]
    sources = (
        (far_below_ref, 72), (below_ref, 128), (near_ref, 128), (above_ref, 128), (far_above_ref, 72),
    )
    for index, (source, start) in enumerate(sources):
        for m in range(3):
            row = ROWS * m + 2 * index
            rows_ref[row : row + 2, :] = source[start + 2 * m : start + 2 * m + 2, :]
    rows_ref[30:32, :] = jnp.zeros((2, 128), F32)
    rows = rows_ref[...]
    for face, ref in ((0, low_ref), (7, high_ref)):
        for c in range(8):
            ref[8 * c : 8 * c + 8, :] = load_ref[face, c]
        ref[64:65, :] = far_below_ref[64 + face : 65 + face, :]
        ref[65:66, :] = far_above_ref[64 + face : 65 + face, :]
        ref[66:72, :] = jnp.zeros((6, 128), F32)
        ref[FACE_METRIC:FACE_ROWS, :] = rows


def write_z_faces(field, low_ref, high_ref):
    for i in range(8):
        low_ref[i : i + 1, :] = field[i][0][0:1, :]
        high_ref[i : i + 1, :] = field[i][-1][7:8, :]


def begin(
    load_ref, edge_ref, rows_ref, left_ref, right_ref, factor_ref, table_ref,
    rhs_ref, inverse_ref, smooth_ref, applied_ref, low_ref, high_ref, send_ref,
):
    def edge(which):
        start = 8 * which

        def row(i):
            value = edge_ref[start + i : start + i + 1, :]
            if i == 0:
                value = value + left_ref[64 + which : 65 + which, :]
            if i == 7:
                value = value + right_ref[64 + which : 65 + which, :]
            return value

        return row

    load = sum_x(read(load_ref, 0, 8), faces(left_ref, 8), faces(right_ref, 8))
    rhs = each(wall, sum_y(sum_z(load, edge(0), edge(1))))
    columns = [
        diagonal_sum_x(rows_ref, left_ref, right_ref, column, table_ref) for column in range(-4, 6)
    ]
    diagonal = sum_z([[columns[c][i] for c in range(10)] for i in range(8)])
    inverse = each(lambda d: wall(1.0 / d), sum_y(diagonal))
    smooth = each(lambda d, r: d * r / THETA, inverse, rhs)
    write(rhs_ref, [row[1:7] for row in rhs])
    write(inverse_ref, [row[1:7] for row in inverse])
    write(smooth_ref, [row[1:7] for row in smooth])
    applied = element_apply(smooth, -3, rows_ref, table_ref)
    write(applied_ref, applied)
    write_x_faces(applied, low_ref, high_ref)

    mult = table(table_ref, "mult")
    weighted = [[rhs[i][3 + z] * (mult * float(EDGE[i])) for z in range(2)] for i in range(8)]
    parts = []
    for a in range(2):
        along_x = []
        for z in range(2):
            total = float(ALONG_X[a, 0]) * weighted[0][z]
            for i in range(1, 8):
                total = total + float(ALONG_X[a, i]) * weighted[i][z]
            along_x.append(total)
        for b in range(2):
            both = (
                table(table_ref, f"bz{b}0") * along_x[0] + table(table_ref, f"bz{b}1") * along_x[1]
            )
            parts.append(jnp.sum(both, axis=0, keepdims=True))
    node = lax.broadcasted_iota(jnp.int32, (8, 128), 0)
    stacked = jnp.zeros((8, 128), F32)
    for index, part in enumerate(parts):
        stacked = jnp.where(node == index, spread(part), stacked)
    modes = lax.dot_general(
        stacked, table(table_ref, "modes"), (((1,), (1,)), ((), ())),
        precision=HIGHEST, preferred_element_type=F32,
    )
    owner = lax.broadcasted_iota(jnp.int32, (8, 32), 1) // 8
    row = lax.broadcasted_iota(jnp.int32, (8, 32), 0)
    coarse_rhs = jnp.sum(jnp.where(owner == row, modes, 0.0), axis=0, keepdims=True)
    own = jnp.dot(
        jnp.broadcast_to(coarse_rhs, (8, 32)), factor_ref[...],
        precision=HIGHEST, preferred_element_type=F32,
    )
    node = lax.broadcasted_iota(jnp.int32, (8, 128), 0)
    pairs = jnp.where(node % 2 == 0, spread(own[0:1, 0:128]), spread(own[0:1, 128:256]))
    for chunk in range(0, 2 * DEVICES, 8):
        send_ref[chunk : chunk + 8, :] = pairs


def device():
    return lax.axis_index("gx") * N_GZ + lax.axis_index("gz")


def tree_sums(received_ref):
    row = lax.broadcasted_iota(jnp.int32, (8, 128), 0)
    level = (row % 2) * 8 + lane_iota() // 16
    mine = lax.shift_right_logical(jnp.full((8, 128), device(), jnp.int32), level)
    total = jnp.zeros((8, 128), F32)
    for start in range(0, 2 * DEVICES, 8):
        other = lax.shift_right_logical(start // 2 + row // 2, level)
        total = total + jnp.where(other == mine, received_ref[start : start + 8, :], 0.0)
    first = jnp.sum(jnp.where(row % 2 == 0, total, 0.0), axis=0, keepdims=True)
    second = jnp.sum(jnp.where(row % 2 == 1, total, 0.0), axis=0, keepdims=True)
    return first, second


def relax(step, count, applied_ref, left_ref, right_ref, rhs_ref, inverse_ref, smooth_ref, update_ref):
    field = sum_x(
        read(applied_ref, 0, count + 2), faces(left_ref, count + 2), faces(right_ref, count + 2)
    )
    image = each(wall, sum_y(sum_z(field)))
    first, second = STEPS[step]
    inset = (6 - count) // 2
    shift = 1 if step else 0
    update = each(
        lambda u, d, r, a: first * u + (second * d) * (r - a),
        read(update_ref, shift, count), read(inverse_ref, inset, count), read(rhs_ref, inset, count),
        image,
    )
    return each(lambda s, u: s + u, read(smooth_ref, shift, count), update), update


def sweep(
    applied_ref, left_ref, right_ref, rhs_ref, inverse_ref, smooth_ref, update_ref, rows_ref, table_ref,
    next_ref, next_update_ref, out_ref, low_ref, high_ref, *, step, count,
):
    smooth, update = relax(
        step, count, applied_ref, left_ref, right_ref, rhs_ref, inverse_ref, smooth_ref, update_ref
    )
    write(next_ref, smooth)
    write(next_update_ref, update)
    applied = element_apply(smooth, 1 - count // 2, rows_ref, table_ref)
    write(out_ref, applied)
    write_x_faces(applied, low_ref, high_ref)


def coarse_field(received_ref, factor_ref, table_ref):
    first, second = tree_sums(received_ref)
    columns = jnp.broadcast_to(jnp.concatenate([first, second], axis=1), (8, 256))
    coarse = lax.dot_general(
        columns, factor_ref[...], (((1,), (1,)), ((), ())),
        precision=HIGHEST, preferred_element_type=F32,
    )
    owner = lax.broadcasted_iota(jnp.int32, (8, 32), 1) // 8
    row = lax.broadcasted_iota(jnp.int32, (8, 32), 0)
    across = jnp.dot(
        jnp.where(owner == row, coarse, 0.0), table(table_ref, "modes"),
        precision=HIGHEST, preferred_element_type=F32,
    )
    out = [[None, None] for i in range(8)]
    for z in range(2):
        along_z = []
        for a in range(2):
            along_z.append(
                table(table_ref, f"bz0{z}") * spread(across[2 * a : 2 * a + 1, :])
                + table(table_ref, f"bz1{z}") * spread(across[2 * a + 1 : 2 * a + 2, :])
            )
        for i in range(8):
            out[i][z] = wall(float(ALONG_X[0, i]) * along_z[0] + float(ALONG_X[1, i]) * along_z[1])
    return out


def last_sweep(
    applied_ref, left_ref, right_ref, rhs_ref, inverse_ref, smooth_ref, update_ref, rows_ref,
    tree_ref, factor_ref, near_ref, table_ref,
    precond_ref, out_ref, low_ref, high_ref, zlow_ref, zhigh_ref, send_ref,
):
    smooth, update = relax(
        2, 2, applied_ref, left_ref, right_ref, rhs_ref, inverse_ref, smooth_ref, update_ref
    )
    coarse = coarse_field(tree_ref, factor_ref, table_ref)
    precond = each(lambda s, c: s + c, smooth, coarse)
    write(precond_ref, precond)
    applied = element_apply(precond, 0, rows_ref, table_ref)
    write(out_ref, applied)
    first = jnp.zeros((8, 128), F32)
    second = jnp.zeros((8, 128), F32)
    for i in range(8):
        for z in range(2):
            start = 8 * (2 * i + z)
            first = first + near_ref[start : start + 8, :] * precond[i][z]
            second = second + applied[i][z] * precond[i][z]
    write_x_faces(applied, low_ref, high_ref)
    write_z_faces(applied, zlow_ref, zhigh_ref)
    first = first + pltpu.roll(first, 64, 1)
    second = second + pltpu.roll(second, 64, 1)
    both = jnp.where(lane_iota() < 64, first, second)
    both = spread(jnp.sum(both, axis=0, keepdims=True))
    for chunk in range(0, DEVICES, 8):
        send_ref[chunk : chunk + 8, :] = both


def join_edges(zlow_ref, zhigh_ref, left_ref, right_ref, low_ref, high_ref):
    for z, node, source, target in ((0, 0, zlow_ref, low_ref), (1, 7, zhigh_ref, high_ref)):
        row = 8 * z + node
        target[...] = source[...]
        target[0:1, :] = source[0:1, :] + left_ref[row : row + 1, :]
        target[7:8, :] = source[7:8, :] + right_ref[row : row + 1, :]


def finish(
    applied_ref, left_ref, right_ref, before_ref, after_ref, received_ref, precond_ref, rhs_ref,
    solution_ref, residual_ref,
):
    field = sum_x(read(applied_ref), faces(left_ref, 2), faces(right_ref, 2))
    field = sum_z(field, lambda i: before_ref[i : i + 1, :], lambda i: after_ref[i : i + 1, :])
    image = each(wall, sum_y(field))
    total = received_ref[0:8, :]
    for start in range(8, DEVICES, 8):
        total = total + received_ref[start : start + 8, :]
    total = jnp.sum(total, axis=0, keepdims=True)
    lane = lax.broadcasted_iota(jnp.int32, (1, 128), 1)
    product = jnp.sum(jnp.where(lane < 64, total, 0.0), axis=1, keepdims=True)
    curvature = jnp.sum(jnp.where(lane < 64, 0.0, total), axis=1, keepdims=True)
    alpha = spread(product / curvature)
    write(solution_ref, each(lambda p: alpha * p, read(precond_ref)))
    write(residual_ref, each(lambda r, a: r - alpha * a, read(rhs_ref, 2, 2), image))


def field_shape(count):
    return (8, count, 8, 128)


def run(kernel, shapes, *operands, last=False):
    spec = pl.BlockSpec(memory_space=pltpu.VMEM)
    outs = [
        jax.ShapeDtypeStruct(shape, F32) if last else pltpu.VMEM(shape, F32) for shape in shapes
    ]
    operands = [pltpu.with_memory_space_constraint(value, pltpu.VMEM) for value in operands]
    return pl.pallas_call(
        kernel, out_shape=outs, in_specs=[spec] * len(operands), out_specs=[spec] * len(outs)
    )(*operands)


def shifted(value, axis, distance):
    count = lax.axis_size(axis)
    return lax.ppermute(value, axis, [(i, (i + distance) % count) for i in range(count)])


def exchange(low, high, axis):
    return shifted(high, axis, 1), shifted(low, axis, -1)


def send_to_all(value, rows):
    chunks = value.reshape(DEVICES, rows, 128)
    return lax.all_to_all(chunks, ("gx", "gz"), 0, 0, tiled=True).reshape(value.shape)


def per_device(element_rhs_load, metric, coarse_factor):
    constants = jnp.asarray(TABLE)
    factor = coarse_factor.reshape(10, 32, 16).transpose(1, 0, 2).reshape(32, 160)
    factor = jnp.pad(factor, ((0, 0), (0, 96)))
    near, up, down = run(
        pack, [(136, 128), (80, 128), (80, 128)], element_rhs_load, metric
    )
    below, far_below = shifted(near, "gz", 1), shifted(up, "gz", 2)
    above, far_above = shifted(near, "gz", -1), shifted(down, "gz", -2)
    wide, edge, rows, low, high = run(
        gather, [field_shape(8), (16, 128), (32, 128)] + [(FACE_ROWS, 128)] * 2,
        near, below, far_below, above, far_above,
    )
    left, right = exchange(low, high, "gx")
    rhs, inverse, smooth, applied, low, high, send = run(
        begin, [field_shape(6)] * 3 + [field_shape(8)] + [(64, 128)] * 2 + [(2 * DEVICES, 128)],
        wide, edge, rows, left, right, factor, constants,
    )
    tree = send_to_all(send, 2)
    left, right = exchange(low, high, "gx")
    update = smooth
    for step, count in ((0, 6), (1, 4)):

        def stage(*refs, step=step, count=count):
            sweep(*refs, step=step, count=count)

        smooth, update, applied, low, high = run(
            stage, [field_shape(count)] * 3 + [(8 * count, 128)] * 2,
            applied, left, right, rhs, inverse, smooth, update, rows, constants,
        )
        left, right = exchange(low, high, "gx")
    precond, applied, low, high, zlow, zhigh, send = run(
        last_sweep, [field_shape(2)] * 2 + [(16, 128)] * 2 + [(8, 128)] * 2 + [(DEVICES, 128)],
        applied, left, right, rhs, inverse, smooth, update, rows, tree, factor, near, constants,
    )
    received = send_to_all(send, 1)
    left, right = exchange(low, high, "gx")
    zlow, zhigh = run(join_edges, [(8, 128)] * 2, zlow, zhigh, left, right)
    before, after = exchange(zlow, zhigh, "gz")
    solution_field, residual = run(
        finish, [field_shape(2)] * 2,
        applied, left, right, before, after, received, precond, rhs, last=True,
    )
    shape = element_rhs_load.shape
    return solution_field.reshape(shape), residual.reshape(shape)


def solution(mesh):
    placed = (
        P("gx", None, "gz", None, None),
        P(None, "gx", "gz", None),
        P("gx", "gz", None, None, None),
    )
    return jax.shard_map(
        per_device,
        mesh=mesh,
        in_specs=placed,
        out_specs=(P("gx", None, "gz", None, None), P("gx", None, "gz", None, None)),
        check_vma=False,
    )
```

```python
import jax
import jax.numpy as jnp
import numpy as np
from jax import lax
from jax.experimental import pallas as pl
from jax.experimental.pallas import tpu as pltpu
from jax.sharding import PartitionSpec as P

CHEB = 4
N_GX = 32
N_GZ = 16
F32 = jnp.float32
HIGHEST = lax.Precision.HIGHEST

cheb_high = 2.0
cheb_low = 0.1
gll_inner = (
    -0.8717401485096066,
    -0.5917001814331423,
    -0.2092992179024789,
    0.2092992179024789,
    0.5917001814331423,
    0.8717401485096066,
)


def legendre_seven(points):
    before = np.ones(points.shape[0])
    current = points.copy()
    for degree in range(1, 7):
        following = ((2.0 * degree + 1.0) * points * current - degree * before) / (degree + 1.0)
        before = current
        current = following
    return current


def gll_tables():
    order = 7
    points = np.concatenate([[-1.0], np.array(gll_inner), [1.0]])
    values = legendre_seven(points)
    weights = 2.0 / (order * (order + 1) * values**2)
    count = order + 1
    deriv = np.zeros((count, count))
    for row_index in range(count):
        for col_index in range(count):
            if row_index != col_index:
                deriv[row_index, col_index] = values[row_index] / (
                    values[col_index] * (points[row_index] - points[col_index])
                )
    deriv[0, 0] = -order * (order + 1) / 4.0
    deriv[-1, -1] = order * (order + 1) / 4.0
    stiff = deriv.T @ (weights[:, None] * deriv)
    return (points, weights, stiff)


POINTS, WEIGHTS, STIFF = gll_tables()
KDIAG = np.diag(STIFF)
W = [float(v) for v in WEIGHTS]
KD = [float(v) for v in KDIAG]
K = [[float(v) for v in row] for row in STIFF]


def positions(count):
    return ((np.arange(count)[:, None] + (1.0 + POINTS[None, :]) / 2.0) / count).reshape(-1)


ALONG_X = np.stack([np.sin(np.pi * mode * positions(1)) for mode in (1, 2)])
ALONG_Z = np.stack([np.sin(np.pi * mode * positions(2)) for mode in (1, 2)])
ALONG_Y = np.stack([np.sin(np.pi * mode * positions(16)) for mode in range(1, 9)])
EDGE = np.array([0.5] + [1.0] * 6 + [0.5])


def build_tables():
    w_l = np.tile(WEIGHTS, 16)[None, :]
    k_l = np.tile(KDIAG, 16)[None, :]
    w_j = WEIGHTS[:, None]
    k_j = KDIAG[:, None]
    ones = np.ones((1, 128))
    across = np.ones(128)
    across[8::8] = 0.5
    across[7:127:8] = 0.5
    pieces = {
        "stiff": np.kron(np.eye(16), STIFF),
        "ww": w_j * w_l,
        "kw": k_j * w_l,
        "wk": w_j * k_l,
        "wl": np.ones((8, 1)) * w_l,
        "wj": w_j * ones,
        "mult": EDGE[:, None] * across[None, :],
        "modes": np.tile(ALONG_Y, (4, 1)),
    }
    for b in range(2):
        for z in range(2):
            pieces[f"bz{b}{z}"] = ALONG_Z[b, 8 * z : 8 * z + 8, None] * ones
    offsets = {}
    rows = []
    start = 0
    for name, piece in pieces.items():
        offsets[name] = (start, start + piece.shape[0])
        rows.append(piece)
        start += piece.shape[0]
    return np.concatenate(rows).astype(np.float32), offsets


TABLE, OFFSETS = build_tables()


def chebyshev_steps():
    theta = 0.5 * (cheb_high + cheb_low)
    delta = 0.5 * (cheb_high - cheb_low)
    sigma = theta / delta
    rho = 1.0 / sigma
    steps = []
    for sweep in range(CHEB - 1):
        rho_next = 1.0 / (2.0 * sigma - rho)
        steps.append((rho_next * rho, 2.0 * rho_next / delta))
        rho = rho_next
    return theta, steps


THETA, STEPS = chebyshev_steps()


def table(table_ref, name):
    low, high = OFFSETS[name]
    return table_ref[low:high, :]


def lane_iota():
    return lax.broadcasted_iota(jnp.int32, (8, 128), 1)


def read(ref, first=0, count=2):
    return [[ref[i, c] for c in range(first, first + count)] for i in range(8)]


def write(ref, field):
    for i in range(8):
        for c, value in enumerate(field[i]):
            ref[i, c] = value


def spread(row):
    return jnp.broadcast_to(row, (8, 128))


def sum_x(field, left, right):
    out = [list(row) for row in field]
    for c in range(len(field[0])):
        out[0][c] = field[0][c] + left[c]
        out[7][c] = field[7][c] + right[c]
    return out


def sum_z(field, before=None, after=None):
    node = lax.broadcasted_iota(jnp.int32, (8, 128), 0)
    count = len(field[0])
    out = []
    for i in range(8):
        lows = [None] + [field[i][c][7:8, :] for c in range(count - 1)]
        highs = [field[i][c][0:1, :] for c in range(1, count)] + [None]
        if before is not None:
            lows[0], highs[-1] = before(i), after(i)
        out.append(
            [
                field[i][c]
                + jnp.where(node == 0, spread(lows[c]), jnp.where(node == 7, spread(highs[c]), 0.0))
                for c in range(count)
                if lows[c] is not None and highs[c] is not None
            ]
        )
    return out


def sum_y(field):
    lane = lane_iota()
    first = (lane % 8 == 0) & (lane > 0)
    last = (lane % 8 == 7) & (lane < 127)
    return each(
        lambda value: value
        + jnp.where(last, pltpu.roll(value, 127, 1), jnp.where(first, pltpu.roll(value, 1, 1), 0.0)),
        field,
    )


def wall(value):
    lane = lane_iota()
    return jnp.where((lane == 0) | (lane == 127), 0.0, value)


def each(function, *fields):
    return [[function(*values) for values in zip(*rows)] for rows in zip(*fields)]


ROWS = 10


def metric_row(ref, base, m, column):
    row = base + ROWS * m + 4 + column
    return ref[row : row + 1, :]


def element_apply(field, first, metric_ref, table_ref):
    count = len(field[0])
    stiff = table(table_ref, "stiff")
    out = [[None] * count for i in range(8)]
    for c in range(count):
        stacked = jnp.concatenate([field[i][c] for i in range(8)], axis=0)
        along_l = jnp.dot(stacked, stiff, precision=HIGHEST, preferred_element_type=F32)
        along_j = jnp.dot(
            stiff[0:64, 0:64], stacked, precision=HIGHEST, preferred_element_type=F32
        )
        rows = [spread(metric_row(metric_ref, 0, m, first + c)) for m in range(3)]
        scale_x = rows[0] * table(table_ref, "ww")
        scale_z = rows[1] * table(table_ref, "wl")
        scale_y = rows[2] * table(table_ref, "wj")
        for p in range(8):
            along_i = K[0][p] * field[0][c]
            for i in range(1, 8):
                along_i = along_i + K[i][p] * field[i][c]
            out[p][c] = scale_x * along_i + W[p] * (
                scale_z * along_j[8 * p : 8 * p + 8, :] + scale_y * along_l[8 * p : 8 * p + 8, :]
            )
    return out


def diagonal_parts(ref, base, column, table_ref):
    part_x = spread(metric_row(ref, base, 0, column)) * table(table_ref, "ww")
    part_rest = spread(metric_row(ref, base, 1, column)) * table(table_ref, "kw") + spread(
        metric_row(ref, base, 2, column)
    ) * table(table_ref, "wk")
    return part_x, part_rest


def diagonal_sum_x(rows_ref, left_ref, right_ref, column, table_ref):
    part_x, part_rest = diagonal_parts(rows_ref, 0, column, table_ref)
    out = []
    for i in range(8):
        sum_of_x, sum_of_rest = part_x, part_rest
        if i in (0, 7):
            side = left_ref if i == 0 else right_ref
            side_x, side_rest = diagonal_parts(side, Facross_refE_METRIC, column, table_ref)
            sum_of_x, sum_of_rest = part_x + side_x, part_rest + side_rest
        out.append(KD[i] * sum_of_x + W[i] * sum_of_rest)
    return out


class Faces:
    def __init__(self, across_ref, within_ref):
        self.odd = lax.rem(lax.axis_index("gx"), 2) == 1
        self.across, self.within = across_ref, within_ref

    def put(self, first, last, low, high):
        self.across[first:last, :] = jnp.where(self.odd, high, low)
        self.within[first:last, :] = jnp.where(self.odd, low, high)


class Side:
    def __init__(self, across_ref, within_ref, right):
        odd = lax.rem(lax.axis_index("gx"), 2) == 1
        self.across = odd if right else jnp.logical_not(odd)
        self.across_ref, self.within_ref = across_ref, within_ref

    def __getitem__(self, where):
        return jnp.where(self.across, self.across_ref[where], self.within_ref[where])


def sides(across_ref, within_ref):
    return Side(across_ref, within_ref, False), Side(across_ref, within_ref, True)


def write_x_faces(field, across_ref, within_ref):
    out = Faces(across_ref, within_ref)
    for c in range(len(field[0])):
        out.put(8 * c, 8 * c + 8, field[0][c], field[7][c])


def faces(ref, count):
    return [ref[8 * c : 8 * c + 8, :] for c in range(count)]


def pack(load_ref, metric_ref, near_ref, up_ref, down_ref):
    element = lax.broadcasted_iota(jnp.int32, (16, 128), 0)
    lane = lax.broadcasted_iota(jnp.int32, (16, 128), 1)
    expand = jnp.where(element == lane // 8, 1.0, 0.0)
    for ref, start in ((near_ref, 128), (up_ref, 72), (down_ref, 72)):
        ref[start + 6 : start + 8, :] = jnp.zeros((2, 128), F32)
    for m in range(3):
        expanded = jnp.dot(
            metric_ref[m, 0], expand, precision=HIGHEST, preferred_element_type=F32
        )
        for ref, start in ((near_ref, 128), (up_ref, 72), (down_ref, 72)):
            ref[start + 2 * m : start + 2 * m + 2, :] = expanded
    for i in range(8):
        for z in range(2):
            near_ref[8 * (2 * i + z) : 8 * (2 * i + z) + 8, :] = load_ref[0, i, z]
        up_ref[8 * i : 8 * i + 8, :] = load_ref[0, i, 1]
        up_ref[64 + i : 65 + i, :] = load_ref[0, i, 0, 7:8, :]
        down_ref[8 * i : 8 * i + 8, :] = load_ref[0, i, 0]
        down_ref[64 + i : 65 + i, :] = load_ref[0, i, 1, 0:1, :]


Facross_refE_METRIC = 72
Facross_refE_ROWS = 104


def gather(
    near_ref, below_ref, far_below_ref, above_ref, far_above_ref,
    load_ref, edge_ref, rows_ref, low_ref, high_ref,
):
    for i in range(8):
        load_ref[i, 0] = far_below_ref[8 * i : 8 * i + 8, :]
        load_ref[i, 7] = far_above_ref[8 * i : 8 * i + 8, :]
        for z in range(2):
            start = 8 * (2 * i + z)
            load_ref[i, 1 + z] = below_ref[start : start + 8, :]
            load_ref[i, 3 + z] = near_ref[start : start + 8, :]
            load_ref[i, 5 + z] = above_ref[start : start + 8, :]
    edge_ref[0:8, :] = far_below_ref[64:72, :]
    edge_ref[8:16, :] = far_above_ref[64:72, :]
    sources = (
        (far_below_ref, 72), (below_ref, 128), (near_ref, 128), (above_ref, 128), (far_above_ref, 72),
    )
    for index, (source, start) in enumerate(sources):
        for m in range(3):
            row = ROWS * m + 2 * index
            rows_ref[row : row + 2, :] = source[start + 2 * m : start + 2 * m + 2, :]
    rows_ref[30:32, :] = jnp.zeros((2, 128), F32)
    rows = rows_ref[...]
    out = Faces(low_ref, high_ref)
    for c in range(8):
        out.put(8 * c, 8 * c + 8, load_ref[0, c], load_ref[7, c])
    for row, ref in ((64, far_below_ref), (65, far_above_ref)):
        out.put(row, row + 1, ref[64:65, :], ref[71:72, :])
    for ref in (low_ref, high_ref):
        ref[66:72, :] = jnp.zeros((6, 128), F32)
        ref[Facross_refE_METRIC:Facross_refE_ROWS, :] = rows


def send_along_x(field, extra, send_ref):
    here = lax.axis_index("gx")
    above = lax.rem(here + 1, N_GX)
    for chunk in range(N_GX):
        for z in range(2):
            send_ref[chunk, 8 * z : 8 * z + 8, :] = jnp.where(
                above == chunk, field[7][z], field[0][z]
            )
        send_ref[chunk, 16:24, :] = extra


def write_z_faces(field, low_ref, high_ref):
    for i in range(8):
        low_ref[i : i + 1, :] = field[i][0][0:1, :]
        high_ref[i : i + 1, :] = field[i][-1][7:8, :]


def begin(
    load_ref, edge_ref, rows_ref, across_ref, within_ref, factor_ref, table_ref,
    rhs_ref, inverse_ref, smooth_ref, applied_ref, across_out, within_out, send_ref,
):
    left_ref, right_ref = sides(across_ref, within_ref)

    def edge(which):
        start = 8 * which

        def row(i):
            value = edge_ref[start + i : start + i + 1, :]
            if i == 0:
                value = value + left_ref[64 + which : 65 + which, :]
            if i == 7:
                value = value + right_ref[64 + which : 65 + which, :]
            return value

        return row

    load = sum_x(read(load_ref, 0, 8), faces(left_ref, 8), faces(right_ref, 8))
    rhs = each(wall, sum_y(sum_z(load, edge(0), edge(1))))
    columns = [
        diagonal_sum_x(rows_ref, left_ref, right_ref, column, table_ref) for column in range(-4, 6)
    ]
    diagonal = sum_z([[columns[c][i] for c in range(10)] for i in range(8)])
    inverse = each(lambda d: wall(1.0 / d), sum_y(diagonal))
    smooth = each(lambda d, r: d * r / THETA, inverse, rhs)
    write(rhs_ref, [row[1:7] for row in rhs])
    write(inverse_ref, [row[1:7] for row in inverse])
    write(smooth_ref, [row[1:7] for row in smooth])
    applied = element_apply(smooth, -3, rows_ref, table_ref)
    write(applied_ref, applied)
    write_x_faces(applied, across_out, within_out)

    mult = table(table_ref, "mult")
    weighted = [[rhs[i][3 + z] * (mult * float(EDGE[i])) for z in range(2)] for i in range(8)]
    parts = []
    for a in range(2):
        along_x = []
        for z in range(2):
            total = float(ALONG_X[a, 0]) * weighted[0][z]
            for i in range(1, 8):
                total = total + float(ALONG_X[a, i]) * weighted[i][z]
            along_x.append(total)
        for b in range(2):
            both = (
                table(table_ref, f"bz{b}0") * along_x[0] + table(table_ref, f"bz{b}1") * along_x[1]
            )
            parts.append(jnp.sum(both, axis=0, keepdims=True))
    node = lax.broadcasted_iota(jnp.int32, (8, 128), 0)
    stacked = jnp.zeros((8, 128), F32)
    for index, part in enumerate(parts):
        stacked = jnp.where(node == index, spread(part), stacked)
    modes = lax.dot_general(
        stacked, table(table_ref, "modes"), (((1,), (1,)), ((), ())),
        precision=HIGHEST, preferred_element_type=F32,
    )
    owner = lax.broadcasted_iota(jnp.int32, (8, 32), 1) // 8
    row = lax.broadcasted_iota(jnp.int32, (8, 32), 0)
    coarse_rhs = jnp.sum(jnp.where(owner == row, modes, 0.0), axis=0, keepdims=True)
    own = jnp.dot(
        jnp.broadcast_to(coarse_rhs, (8, 32)), factor_ref[...],
        precision=HIGHEST, preferred_element_type=F32,
    )
    for chunk in range(N_GZ):
        send_ref[chunk, 0:1, :] = own[0:1, 0:128]
        send_ref[chunk, 1:2, :] = own[0:1, 128:256]


def level_of_lane(first):
    return first + lax.broadcasted_iota(jnp.int32, (1, 128), 1) // 16


def tree_sum(rows_of, count, here, shift):
    total = jnp.zeros((1, 128), F32)
    mine = lax.shift_right_logical(jnp.full((1, 128), here, jnp.int32), shift)
    for e in range(count):
        other = lax.shift_right_logical(jnp.full((1, 128), e, jnp.int32), shift)
        total = total + jnp.where(other == mine, rows_of(e), 0.0)
    return total


def neighbours(axis, count):
    here = lax.axis_index(axis)
    return lax.rem(here + count - 1, count), lax.rem(here + 1, count)


def lower_tree(received_ref, send_ref):
    here = lax.axis_index("gz")
    for row in range(2):
        total = tree_sum(
            lambda e: received_ref[e, row : row + 1, :], N_GZ, here, level_of_lane(8 * row)
        )
        for chunk in range(N_GX):
            send_ref[chunk, row : row + 1, :] = total


def x_faces_received(received_ref):
    below, above = neighbours("gx", N_GX)
    left = [received_ref[below, 8 * z : 8 * z + 8, :] for z in range(2)]
    right = [received_ref[above, 8 * z : 8 * z + 8, :] for z in range(2)]
    return left, right


def relax(step, count, applied_ref, across_ref, within_ref, rhs_ref, inverse_ref, smooth_ref, update_ref):
    left_ref, right_ref = sides(across_ref, within_ref)
    field = sum_x(
        read(applied_ref, 0, count + 2), faces(left_ref, count + 2), faces(right_ref, count + 2)
    )
    image = each(wall, sum_y(sum_z(field)))
    first, second = STEPS[step]
    inset = (6 - count) // 2
    shift = 1 if step else 0
    update = each(
        lambda u, d, r, a: first * u + (second * d) * (r - a),
        read(update_ref, shift, count), read(inverse_ref, inset, count), read(rhs_ref, inset, count),
        image,
    )
    return each(lambda s, u: s + u, read(smooth_ref, shift, count), update), update


def sweep(
    applied_ref, across_ref, within_ref, rhs_ref, inverse_ref, smooth_ref, update_ref, rows_ref, table_ref,
    next_ref, next_update_ref, out_ref, low_ref, high_ref, *, step, count,
):
    smooth, update = relax(
        step, count, applied_ref, across_ref, within_ref, rhs_ref, inverse_ref, smooth_ref, update_ref
    )
    write(next_ref, smooth)
    write(next_update_ref, update)
    applied = element_apply(smooth, 1 - count // 2, rows_ref, table_ref)
    write(out_ref, applied)
    write_x_faces(applied, low_ref, high_ref)


def coarse_field(received_ref, factor_ref, table_ref):
    here = lax.axis_index("gx")
    first = tree_sum(
        lambda e: received_ref[e, 0:1, :], N_GX, here, jnp.maximum(level_of_lane(0) - 4, 0)
    )
    second = tree_sum(lambda e: received_ref[e, 1:2, :], N_GX, here, level_of_lane(8) - 4)
    columns = jnp.broadcast_to(jnp.concatenate([first, second], axis=1), (8, 256))
    coarse = lax.dot_general(
        columns, factor_ref[...], (((1,), (1,)), ((), ())),
        precision=HIGHEST, preferred_element_type=F32,
    )
    owner = lax.broadcasted_iota(jnp.int32, (8, 32), 1) // 8
    row = lax.broadcasted_iota(jnp.int32, (8, 32), 0)
    across = jnp.dot(
        jnp.where(owner == row, coarse, 0.0), table(table_ref, "modes"),
        precision=HIGHEST, preferred_element_type=F32,
    )
    out = [[None, None] for i in range(8)]
    for z in range(2):
        along_z = []
        for a in range(2):
            along_z.append(
                table(table_ref, f"bz0{z}") * spread(across[2 * a : 2 * a + 1, :])
                + table(table_ref, f"bz1{z}") * spread(across[2 * a + 1 : 2 * a + 2, :])
            )
        for i in range(8):
            out[i][z] = wall(float(ALONG_X[0, i]) * along_z[0] + float(ALONG_X[1, i]) * along_z[1])
    return out


def last_sweep(
    applied_ref, across_ref, within_ref, rhs_ref, inverse_ref, smooth_ref, update_ref, rows_ref,
    tree_ref, factor_ref, near_ref, table_ref,
    precond_ref, out_ref, send_ref,
):
    smooth, update = relax(
        2, 2, applied_ref, across_ref, within_ref, rhs_ref, inverse_ref, smooth_ref, update_ref
    )
    coarse = coarse_field(tree_ref, factor_ref, table_ref)
    precond = each(lambda s, c: s + c, smooth, coarse)
    write(precond_ref, precond)
    applied = element_apply(precond, 0, rows_ref, table_ref)
    write(out_ref, applied)
    first = jnp.zeros((8, 128), F32)
    second = jnp.zeros((8, 128), F32)
    for i in range(8):
        for z in range(2):
            start = 8 * (2 * i + z)
            first = first + near_ref[start : start + 8, :] * precond[i][z]
            second = second + applied[i][z] * precond[i][z]
    first = first + pltpu.roll(first, 64, 1)
    second = second + pltpu.roll(second, 64, 1)
    both = jnp.where(lane_iota() < 64, first, second)
    send_along_x(applied, spread(jnp.sum(both, axis=0, keepdims=True)), send_ref)


def middle(applied_ref, received_ref, summed_ref, low_ref, high_ref, send_ref):
    field = sum_x(read(applied_ref), *x_faces_received(received_ref))
    write(summed_ref, field)
    write_z_faces(field, low_ref, high_ref)
    total = received_ref[0, 16:24, :]
    for e in range(1, N_GX):
        total = total + received_ref[e, 16:24, :]
    send_ref[0:8, :] = total
    send_ref[8:16, :] = total


def finish(
    summed_ref, before_ref, after_ref, received_ref, precond_ref, rhs_ref, solution_ref, residual_ref
):
    field = sum_z(
        read(summed_ref), lambda i: before_ref[i : i + 1, :], lambda i: after_ref[i : i + 1, :]
    )
    image = each(wall, sum_y(field))
    total = jnp.sum(received_ref[0:8, :] + received_ref[8:16, :], axis=0, keepdims=True)
    lane = lax.broadcasted_iota(jnp.int32, (1, 128), 1)
    product = jnp.sum(jnp.where(lane < 64, total, 0.0), axis=1, keepdims=True)
    curvature = jnp.sum(jnp.where(lane < 64, 0.0, total), axis=1, keepdims=True)
    alpha = spread(product / curvature)
    write(solution_ref, each(lambda p: alpha * p, read(precond_ref)))
    write(residual_ref, each(lambda r, a: r - alpha * a, read(rhs_ref, 2, 2), image))


def field_shape(count):
    return (8, count, 8, 128)


def run(kernel, shapes, *operands, last=False):
    spec = pl.BlockSpec(memory_space=pltpu.VMEM)
    outs = [
        jax.ShapeDtypeStruct(shape, F32) if last else pltpu.VMEM(shape, F32) for shape in shapes
    ]
    operands = [pltpu.with_memory_space_constraint(value, pltpu.VMEM) for value in operands]
    return pl.pallas_call(
        kernel, out_shape=outs, in_specs=[spec] * len(operands), out_specs=[spec] * len(outs)
    )(*operands)


def shifted(value, axis, distance):
    count = lax.axis_size(axis)
    return lax.ppermute(value, axis, [(i, (i + distance) % count) for i in range(count)])


def swap_x(across, within):
    count = lax.axis_size("gx")
    over = [(i, (((i - 1) % count) ^ 1) + 1) for i in range(count)]
    over = [(i, target % count) for i, target in over]
    inside = [(i, i ^ 1) for i in range(count)]
    return lax.ppermute(across, "gx", over), lax.ppermute(within, "gx", inside)


def per_device(element_rhs_load, metric, coarse_factor):
    constants = jnp.asarray(TABLE)
    factor = coarse_factor.reshape(10, 32, 16).transpose(1, 0, 2).reshape(32, 160)
    factor = jnp.pad(factor, ((0, 0), (0, 96)))
    near, up, down = run(
        pack, [(136, 128), (80, 128), (80, 128)], element_rhs_load, metric
    )
    below, far_below = shifted(near, "gz", 1), shifted(up, "gz", 2)
    above, far_above = shifted(near, "gz", -1), shifted(down, "gz", -2)
    wide, edge, rows, low, high = run(
        gather, [field_shape(8), (16, 128), (32, 128)] + [(Facross_refE_ROWS, 128)] * 2,
        near, below, far_below, above, far_above,
    )
    left, right = swap_x(low, high)
    rhs, inverse, smooth, applied, low, high, send = run(
        begin, [field_shape(6)] * 3 + [field_shape(8)] + [(64, 128)] * 2 + [(N_GZ, 2, 128)],
        wide, edge, rows, left, right, factor, constants,
    )
    tree = lax.all_to_all(send, "gz", 0, 0, tiled=True)
    left, right = swap_x(low, high)
    update = smooth
    for step, count in ((0, 6), (1, 4)):

        def stage(*refs, step=step, count=count):
            sweep(*refs, step=step, count=count)

        smooth, update, applied, low, high = run(
            stage, [field_shape(count)] * 3 + [(8 * count, 128)] * 2,
            applied, left, right, rhs, inverse, smooth, update, rows, constants,
        )
        left, right = swap_x(low, high)
        if step == 0:
            (send,) = run(lower_tree, [(N_GX, 2, 128)], tree)
            tree = lax.all_to_all(send, "gx", 0, 0, tiled=True)
    precond, applied, send = run(
        last_sweep, [field_shape(2)] * 2 + [(N_GX, 24, 128)],
        applied, left, right, rhs, inverse, smooth, update, rows, tree, factor, near, constants,
    )
    received = lax.all_to_all(send, "gx", 0, 0, tiled=True)
    summed, low, high, send = run(
        middle, [field_shape(2)] + [(8, 128)] * 2 + [(N_GZ, 128)], applied, received
    )
    received = lax.all_to_all(send.reshape(N_GZ, 1, 128), "gz", 0, 0, tiled=True)
    before, after = shifted(high, "gz", 1), shifted(low, "gz", -1)
    solution_field, residual = run(
        finish, [field_shape(2)] * 2,
        summed, before, after, received.reshape(N_GZ, 128), precond, rhs, last=True,
    )
    shape = element_rhs_load.shape
    return solution_field.reshape(shape), residual.reshape(shape)


def solution(mesh):
    placed = (
        P("gx", None, "gz", None, None),
        P(None, "gx", "gz", None),
        P("gx", "gz", None, None, None),
    )
    return jax.shard_map(
        per_device,
        mesh=mesh,
        in_specs=placed,
        out_specs=(P("gx", None, "gz", None, None), P("gx", None, "gz", None, None)),
        check_vma=False,
    )
```

```python
import jax
import jax.numpy as jnp
import numpy as np
from jax import lax
from jax.experimental import pallas as pl
from jax.experimental.pallas import tpu as pltpu
from jax.sharding import PartitionSpec as P

CHEB = 4
N_GX = 32
N_GZ = 16
F32 = jnp.float32
HIGHEST = lax.Precision.HIGHEST

cheb_high = 2.0
cheb_low = 0.1
gll_inner = (
    -0.8717401485096066,
    -0.5917001814331423,
    -0.2092992179024789,
    0.2092992179024789,
    0.5917001814331423,
    0.8717401485096066,
)


def legendre_seven(points):
    before = np.ones(points.shape[0])
    current = points.copy()
    for degree in range(1, 7):
        following = ((2.0 * degree + 1.0) * points * current - degree * before) / (degree + 1.0)
        before = current
        current = following
    return current


def gll_tables():
    order = 7
    points = np.concatenate([[-1.0], np.array(gll_inner), [1.0]])
    values = legendre_seven(points)
    weights = 2.0 / (order * (order + 1) * values**2)
    count = order + 1
    deriv = np.zeros((count, count))
    for row_index in range(count):
        for col_index in range(count):
            if row_index != col_index:
                deriv[row_index, col_index] = values[row_index] / (
                    values[col_index] * (points[row_index] - points[col_index])
                )
    deriv[0, 0] = -order * (order + 1) / 4.0
    deriv[-1, -1] = order * (order + 1) / 4.0
    stiff = deriv.T @ (weights[:, None] * deriv)
    return (points, weights, stiff)


POINTS, WEIGHTS, STIFF = gll_tables()
KDIAG = np.diag(STIFF)
W = [float(v) for v in WEIGHTS]
KD = [float(v) for v in KDIAG]
K = [[float(v) for v in row] for row in STIFF]


def positions(count):
    return ((np.arange(count)[:, None] + (1.0 + POINTS[None, :]) / 2.0) / count).reshape(-1)


ALONG_X = np.stack([np.sin(np.pi * mode * positions(1)) for mode in (1, 2)])
ALONG_Z = np.stack([np.sin(np.pi * mode * positions(2)) for mode in (1, 2)])
ALONG_Y = np.stack([np.sin(np.pi * mode * positions(16)) for mode in range(1, 9)])


def build_tables():
    w_l = np.tile(WEIGHTS, 16)[None, :]
    k_l = np.tile(KDIAG, 16)[None, :]
    w_j = WEIGHTS[:, None]
    k_j = KDIAG[:, None]
    ones = np.ones((1, 128))
    pieces = {
        "stiff": np.kron(np.eye(16), STIFF),
        "ww": w_j * w_l,
        "kw": k_j * w_l,
        "wk": w_j * k_l,
        "wl": np.ones((8, 1)) * w_l,
        "wj": w_j * ones,
        "modes": np.tile(ALONG_Y, (4, 1)),
    }
    for b in range(2):
        for z in range(2):
            pieces[f"bz{b}{z}"] = ALONG_Z[b, 8 * z : 8 * z + 8, None] * ones
    offsets = {}
    rows = []
    start = 0
    for name, piece in pieces.items():
        offsets[name] = (start, start + piece.shape[0])
        rows.append(piece)
        start += piece.shape[0]
    return np.concatenate(rows).astype(np.float32), offsets


TABLE, OFFSETS = build_tables()


def chebyshev_steps():
    theta = 0.5 * (cheb_high + cheb_low)
    delta = 0.5 * (cheb_high - cheb_low)
    sigma = theta / delta
    rho = 1.0 / sigma
    steps = []
    for sweep in range(CHEB - 1):
        rho_next = 1.0 / (2.0 * sigma - rho)
        steps.append((rho_next * rho, 2.0 * rho_next / delta))
        rho = rho_next
    return theta, steps


THETA, STEPS = chebyshev_steps()


def table(table_ref, name):
    low, high = OFFSETS[name]
    return table_ref[low:high, :]


def lane_iota():
    return lax.broadcasted_iota(jnp.int32, (8, 128), 1)


def read(ref, first=0, count=2):
    return [[ref[i, c] for c in range(first, first + count)] for i in range(8)]


def write(ref, field):
    for i in range(8):
        for c, value in enumerate(field[i]):
            ref[i, c] = value


def spread(row):
    return jnp.broadcast_to(row, (8, 128))


def sum_x(field, left, right):
    out = [list(row) for row in field]
    for c in range(len(field[0])):
        out[0][c] = field[0][c] + left[c]
        out[7][c] = field[7][c] + right[c]
    return out


def sum_z(field, before=None, after=None):
    node = lax.broadcasted_iota(jnp.int32, (8, 128), 0)
    count = len(field[0])
    out = []
    for i in range(8):
        lows = [None] + [field[i][c][7:8, :] for c in range(count - 1)]
        highs = [field[i][c][0:1, :] for c in range(1, count)] + [None]
        if before is not None:
            lows[0], highs[-1] = before(i), after(i)
        out.append(
            [
                field[i][c]
                + jnp.where(node == 0, spread(lows[c]), jnp.where(node == 7, spread(highs[c]), 0.0))
                for c in range(count)
                if lows[c] is not None and highs[c] is not None
            ]
        )
    return out


def sum_y(field):
    lane = lane_iota()
    first = (lane % 8 == 0) & (lane > 0)
    last = (lane % 8 == 7) & (lane < 127)
    return each(
        lambda value: value
        + jnp.where(last, pltpu.roll(value, 127, 1), jnp.where(first, pltpu.roll(value, 1, 1), 0.0)),
        field,
    )


def wall(value):
    lane = lane_iota()
    return jnp.where((lane == 0) | (lane == 127), 0.0, value)


def each(function, *fields):
    return [[function(*values) for values in zip(*rows)] for rows in zip(*fields)]


ROWS = 10


def metric_row(ref, base, m, column):
    row = base + ROWS * m + 4 + column
    return ref[row : row + 1, :]


def element_apply(field, first, metric_ref, table_ref):
    count = len(field[0])
    stiff = table(table_ref, "stiff")
    out = [[None] * count for i in range(8)]
    for c in range(count):
        stacked = jnp.concatenate([field[i][c] for i in range(8)], axis=0)
        along_l = jnp.dot(stacked, stiff, precision=HIGHEST, preferred_element_type=F32)
        along_j = jnp.dot(
            stiff[0:64, 0:64], stacked, precision=HIGHEST, preferred_element_type=F32
        )
        rows = [spread(metric_row(metric_ref, 0, m, first + c)) for m in range(3)]
        scale_x = rows[0] * table(table_ref, "ww")
        scale_z = rows[1] * table(table_ref, "wl")
        scale_y = rows[2] * table(table_ref, "wj")
        for p in range(8):
            along_i = K[0][p] * field[0][c]
            for i in range(1, 8):
                along_i = along_i + K[i][p] * field[i][c]
            out[p][c] = scale_x * along_i + W[p] * (
                scale_z * along_j[8 * p : 8 * p + 8, :] + scale_y * along_l[8 * p : 8 * p + 8, :]
            )
    return out


def diagonal_parts(ref, base, column, table_ref):
    part_x = spread(metric_row(ref, base, 0, column)) * table(table_ref, "ww")
    part_rest = spread(metric_row(ref, base, 1, column)) * table(table_ref, "kw") + spread(
        metric_row(ref, base, 2, column)
    ) * table(table_ref, "wk")
    return part_x, part_rest


def diagonal_sum_x(rows_ref, left_ref, right_ref, column, table_ref):
    part_x, part_rest = diagonal_parts(rows_ref, 0, column, table_ref)
    out = []
    for i in range(8):
        sum_of_x, sum_of_rest = part_x, part_rest
        if i in (0, 7):
            side = left_ref if i == 0 else right_ref
            side_x, side_rest = diagonal_parts(side, Facross_refE_METRIC, column, table_ref)
            sum_of_x, sum_of_rest = part_x + side_x, part_rest + side_rest
        out.append(KD[i] * sum_of_x + W[i] * sum_of_rest)
    return out


class Faces:
    def __init__(self, across_ref, within_ref):
        self.odd = lax.rem(lax.axis_index("gx"), 2) == 1
        self.across, self.within = across_ref, within_ref

    def put(self, first, last, low, high):
        self.across[first:last, :] = jnp.where(self.odd, high, low)
        self.within[first:last, :] = jnp.where(self.odd, low, high)


class Side:
    def __init__(self, across_ref, within_ref, right):
        odd = lax.rem(lax.axis_index("gx"), 2) == 1
        self.across = odd if right else jnp.logical_not(odd)
        self.across_ref, self.within_ref = across_ref, within_ref

    def __getitem__(self, where):
        return jnp.where(self.across, self.across_ref[where], self.within_ref[where])


def sides(across_ref, within_ref):
    return Side(across_ref, within_ref, False), Side(across_ref, within_ref, True)


def write_x_faces(field, across_ref, within_ref):
    out = Faces(across_ref, within_ref)
    for c in range(len(field[0])):
        out.put(8 * c, 8 * c + 8, field[0][c], field[7][c])


def faces(ref, count):
    return [ref[8 * c : 8 * c + 8, :] for c in range(count)]


def pack(load_ref, metric_ref, near_ref, up_ref, down_ref):
    element = lax.broadcasted_iota(jnp.int32, (16, 128), 0)
    lane = lax.broadcasted_iota(jnp.int32, (16, 128), 1)
    expand = jnp.where(element == lane // 8, 1.0, 0.0)
    for ref, start in ((near_ref, 128), (up_ref, 72), (down_ref, 72)):
        ref[start + 6 : start + 8, :] = jnp.zeros((2, 128), F32)
    for m in range(3):
        expanded = jnp.dot(
            metric_ref[m, 0], expand, precision=HIGHEST, preferred_element_type=F32
        )
        for ref, start in ((near_ref, 128), (up_ref, 72), (down_ref, 72)):
            ref[start + 2 * m : start + 2 * m + 2, :] = expanded
    for i in range(8):
        for z in range(2):
            near_ref[8 * (2 * i + z) : 8 * (2 * i + z) + 8, :] = load_ref[0, i, z]
        up_ref[8 * i : 8 * i + 8, :] = load_ref[0, i, 1]
        up_ref[64 + i : 65 + i, :] = load_ref[0, i, 0, 7:8, :]
        down_ref[8 * i : 8 * i + 8, :] = load_ref[0, i, 0]
        down_ref[64 + i : 65 + i, :] = load_ref[0, i, 1, 0:1, :]


Facross_refE_METRIC = 72
Facross_refE_ROWS = 104


def gather(
    near_ref, below_ref, far_below_ref, above_ref, far_above_ref,
    load_ref, edge_ref, rows_ref, low_ref, high_ref,
):
    for i in range(8):
        load_ref[i, 0] = far_below_ref[8 * i : 8 * i + 8, :]
        load_ref[i, 7] = far_above_ref[8 * i : 8 * i + 8, :]
        for z in range(2):
            start = 8 * (2 * i + z)
            load_ref[i, 1 + z] = below_ref[start : start + 8, :]
            load_ref[i, 3 + z] = near_ref[start : start + 8, :]
            load_ref[i, 5 + z] = above_ref[start : start + 8, :]
    edge_ref[0:8, :] = far_below_ref[64:72, :]
    edge_ref[8:16, :] = far_above_ref[64:72, :]
    sources = (
        (far_below_ref, 72), (below_ref, 128), (near_ref, 128), (above_ref, 128), (far_above_ref, 72),
    )
    for index, (source, start) in enumerate(sources):
        for m in range(3):
            row = ROWS * m + 2 * index
            rows_ref[row : row + 2, :] = source[start + 2 * m : start + 2 * m + 2, :]
    rows_ref[30:32, :] = jnp.zeros((2, 128), F32)
    rows = rows_ref[...]
    out = Faces(low_ref, high_ref)
    for c in range(8):
        out.put(8 * c, 8 * c + 8, load_ref[0, c], load_ref[7, c])
    for row, ref in ((64, far_below_ref), (65, far_above_ref)):
        out.put(row, row + 1, ref[64:65, :], ref[71:72, :])
    for ref in (low_ref, high_ref):
        ref[66:72, :] = jnp.zeros((6, 128), F32)
        ref[Facross_refE_METRIC:Facross_refE_ROWS, :] = rows


def with_sums(face, first, second):
    lane = lane_iota()
    return jnp.where(lane == 0, first, jnp.where(lane == 127, second, face))


def send_along_x(field, first, second, send_ref):
    here = lax.axis_index("gx")
    above = lax.rem(here + 1, N_GX)
    low = [with_sums(field[0][0], first, second), field[0][1]]
    high = [with_sums(field[7][0], first, second), field[7][1]]
    for chunk in range(N_GX):
        for z in range(2):
            send_ref[chunk, 8 * z : 8 * z + 8, :] = jnp.where(above == chunk, high[z], low[z])


def send_along_z(field, sums, send_ref):
    here = lax.axis_index("gz")
    above = lax.rem(here + 1, N_GZ)
    node = lax.broadcasted_iota(jnp.int32, (8, 128), 0)
    low = high = jnp.zeros((8, 128), F32)
    for i in range(8):
        low = jnp.where(node == i, spread(field[i][0][0:1, :]), low)
        high = jnp.where(node == i, spread(field[i][1][7:8, :]), high)
    low, high = with_sums(low, sums, sums), with_sums(high, sums, sums)
    for chunk in range(N_GZ):
        send_ref[chunk] = jnp.where(above == chunk, high, low)


def coarse_start(load_ref, factor_ref, table_ref, send_ref):
    parts = []
    load = [[wall(load_ref[0, i, z]) for z in range(2)] for i in range(8)]
    for a in range(2):
        along_x = []
        for z in range(2):
            total = float(ALONG_X[a, 0]) * load[0][z]
            for i in range(1, 8):
                total = total + float(ALONG_X[a, i]) * load[i][z]
            along_x.append(total)
        for b in range(2):
            both = (
                table(table_ref, f"bz{b}0") * along_x[0] + table(table_ref, f"bz{b}1") * along_x[1]
            )
            parts.append(jnp.sum(both, axis=0, keepdims=True))
    node = lax.broadcasted_iota(jnp.int32, (8, 128), 0)
    stacked = jnp.zeros((8, 128), F32)
    for index, part in enumerate(parts):
        stacked = jnp.where(node == index, spread(part), stacked)
    modes = lax.dot_general(
        stacked, table(table_ref, "modes"), (((1,), (1,)), ((), ())),
        precision=HIGHEST, preferred_element_type=F32,
    )
    owner = lax.broadcasted_iota(jnp.int32, (8, 32), 1) // 8
    row = lax.broadcasted_iota(jnp.int32, (8, 32), 0)
    coarse_rhs = jnp.sum(jnp.where(owner == row, modes, 0.0), axis=0, keepdims=True)
    own = jnp.dot(
        jnp.broadcast_to(coarse_rhs, (8, 32)), factor_ref[...],
        precision=HIGHEST, preferred_element_type=F32,
    )
    for chunk in range(N_GZ):
        send_ref[chunk, 0:1, :] = own[0:1, 0:128]
        send_ref[chunk, 1:2, :] = own[0:1, 128:256]


def begin(
    load_ref, edge_ref, rows_ref, across_ref, within_ref, table_ref,
    rhs_ref, inverse_ref, smooth_ref, applied_ref, across_out, within_out,
):
    left_ref, right_ref = sides(across_ref, within_ref)

    def edge(which):
        start = 8 * which

        def row(i):
            value = edge_ref[start + i : start + i + 1, :]
            if i == 0:
                value = value + left_ref[64 + which : 65 + which, :]
            if i == 7:
                value = value + right_ref[64 + which : 65 + which, :]
            return value

        return row

    load = sum_x(read(load_ref, 0, 8), faces(left_ref, 8), faces(right_ref, 8))
    rhs = each(wall, sum_y(sum_z(load, edge(0), edge(1))))
    columns = [
        diagonal_sum_x(rows_ref, left_ref, right_ref, column, table_ref) for column in range(-4, 6)
    ]
    diagonal = sum_z([[columns[c][i] for c in range(10)] for i in range(8)])
    inverse = each(lambda d: wall(1.0 / d), sum_y(diagonal))
    smooth = each(lambda d, r: d * r / THETA, inverse, rhs)
    write(rhs_ref, [row[1:7] for row in rhs])
    write(inverse_ref, [row[1:7] for row in inverse])
    write(smooth_ref, [row[1:7] for row in smooth])
    applied = element_apply(smooth, -3, rows_ref, table_ref)
    write(applied_ref, applied)
    write_x_faces(applied, across_out, within_out)


def level_of_lane(first):
    return first + lax.broadcasted_iota(jnp.int32, (1, 128), 1) // 16


def tree_sum(rows_of, count, here, shift):
    total = jnp.zeros((1, 128), F32)
    mine = lax.shift_right_logical(jnp.full((1, 128), here, jnp.int32), shift)
    for e in range(count):
        other = lax.shift_right_logical(jnp.full((1, 128), e, jnp.int32), shift)
        total = total + jnp.where(other == mine, rows_of(e), 0.0)
    return total


def neighbours(axis, count):
    here = lax.axis_index(axis)
    return lax.rem(here + count - 1, count), lax.rem(here + 1, count)


def lower_tree(received_ref, send_ref):
    here = lax.axis_index("gz")
    for row in range(2):
        total = tree_sum(
            lambda e: received_ref[e, row : row + 1, :], N_GZ, here, level_of_lane(8 * row)
        )
        for chunk in range(N_GX):
            send_ref[chunk, row : row + 1, :] = total


def x_faces_received(received_ref):
    below, above = neighbours("gx", N_GX)
    left = [received_ref[below, 8 * z : 8 * z + 8, :] for z in range(2)]
    right = [received_ref[above, 8 * z : 8 * z + 8, :] for z in range(2)]
    return left, right


def relax(step, count, applied_ref, across_ref, within_ref, rhs_ref, inverse_ref, smooth_ref, update_ref):
    left_ref, right_ref = sides(across_ref, within_ref)
    field = sum_x(
        read(applied_ref, 0, count + 2), faces(left_ref, count + 2), faces(right_ref, count + 2)
    )
    image = each(wall, sum_y(sum_z(field)))
    first, second = STEPS[step]
    inset = (6 - count) // 2
    shift = 1 if step else 0
    update = each(
        lambda u, d, r, a: first * u + (second * d) * (r - a),
        read(update_ref, shift, count), read(inverse_ref, inset, count), read(rhs_ref, inset, count),
        image,
    )
    return each(lambda s, u: s + u, read(smooth_ref, shift, count), update), update


def sweep(
    applied_ref, across_ref, within_ref, rhs_ref, inverse_ref, smooth_ref, update_ref, rows_ref, table_ref,
    next_ref, next_update_ref, out_ref, low_ref, high_ref, *, step, count,
):
    smooth, update = relax(
        step, count, applied_ref, across_ref, within_ref, rhs_ref, inverse_ref, smooth_ref, update_ref
    )
    write(next_ref, smooth)
    write(next_update_ref, update)
    applied = element_apply(smooth, 1 - count // 2, rows_ref, table_ref)
    write(out_ref, applied)
    write_x_faces(applied, low_ref, high_ref)


def coarse_field(received_ref, factor_ref, table_ref):
    here = lax.axis_index("gx")
    first = tree_sum(
        lambda e: received_ref[e, 0:1, :], N_GX, here, jnp.maximum(level_of_lane(0) - 4, 0)
    )
    second = tree_sum(lambda e: received_ref[e, 1:2, :], N_GX, here, level_of_lane(8) - 4)
    columns = jnp.broadcast_to(jnp.concatenate([first, second], axis=1), (8, 256))
    coarse = lax.dot_general(
        columns, factor_ref[...], (((1,), (1,)), ((), ())),
        precision=HIGHEST, preferred_element_type=F32,
    )
    owner = lax.broadcasted_iota(jnp.int32, (8, 32), 1) // 8
    row = lax.broadcasted_iota(jnp.int32, (8, 32), 0)
    across = jnp.dot(
        jnp.where(owner == row, coarse, 0.0), table(table_ref, "modes"),
        precision=HIGHEST, preferred_element_type=F32,
    )
    out = [[None, None] for i in range(8)]
    for z in range(2):
        along_z = []
        for a in range(2):
            along_z.append(
                table(table_ref, f"bz0{z}") * spread(across[2 * a : 2 * a + 1, :])
                + table(table_ref, f"bz1{z}") * spread(across[2 * a + 1 : 2 * a + 2, :])
            )
        for i in range(8):
            out[i][z] = wall(float(ALONG_X[0, i]) * along_z[0] + float(ALONG_X[1, i]) * along_z[1])
    return out


def last_sweep(
    applied_ref, across_ref, within_ref, rhs_ref, inverse_ref, smooth_ref, update_ref, rows_ref,
    tree_ref, factor_ref, near_ref, table_ref,
    precond_ref, out_ref, send_ref,
):
    smooth, update = relax(
        2, 2, applied_ref, across_ref, within_ref, rhs_ref, inverse_ref, smooth_ref, update_ref
    )
    coarse = coarse_field(tree_ref, factor_ref, table_ref)
    precond = each(lambda s, c: s + c, smooth, coarse)
    write(precond_ref, precond)
    applied = element_apply(precond, 0, rows_ref, table_ref)
    write(out_ref, applied)
    first = jnp.zeros((8, 128), F32)
    second = jnp.zeros((8, 128), F32)
    for i in range(8):
        for z in range(2):
            start = 8 * (2 * i + z)
            first = first + near_ref[start : start + 8, :] * precond[i][z]
            second = second + applied[i][z] * precond[i][z]
    send_along_x(
        applied,
        jnp.sum(first, axis=1, keepdims=True),
        jnp.sum(second, axis=1, keepdims=True),
        send_ref,
    )


def middle(applied_ref, received_ref, summed_ref, send_ref):
    field = sum_x(read(applied_ref), *x_faces_received(received_ref))
    write(summed_ref, field)
    sums = received_ref[0, 0:8, :]
    for e in range(1, N_GX):
        sums = sums + received_ref[e, 0:8, :]
    send_along_z(field, sums, send_ref)


def finish(summed_ref, received_ref, precond_ref, rhs_ref, solution_ref, residual_ref):
    below, above = neighbours("gz", N_GZ)
    field = sum_z(
        read(summed_ref),
        lambda i: received_ref[below, i : i + 1, :],
        lambda i: received_ref[above, i : i + 1, :],
    )
    image = each(wall, sum_y(field))
    sums = received_ref[0]
    for e in range(1, N_GZ):
        sums = sums + received_ref[e]
    sums = jnp.sum(sums, axis=0, keepdims=True)
    alpha = spread(sums[:, 0:1] / sums[:, 127:128])
    write(solution_ref, each(lambda p: alpha * p, read(precond_ref)))
    write(residual_ref, each(lambda r, a: r - alpha * a, read(rhs_ref, 2, 2), image))


def field_shape(count):
    return (8, count, 8, 128)


def run(kernel, shapes, *operands, last=False):
    spec = pl.BlockSpec(memory_space=pltpu.VMEM)
    outs = [
        jax.ShapeDtypeStruct(shape, F32) if last else pltpu.VMEM(shape, F32) for shape in shapes
    ]
    operands = [pltpu.with_memory_space_constraint(value, pltpu.VMEM) for value in operands]
    return pl.pallas_call(
        kernel, out_shape=outs, in_specs=[spec] * len(operands), out_specs=[spec] * len(outs)
    )(*operands)


def shifted(value, axis, distance):
    count = lax.axis_size(axis)
    return lax.ppermute(value, axis, [(i, (i + distance) % count) for i in range(count)])


def swap_x(across, within):
    count = lax.axis_size("gx")
    over = [(i, (((i - 1) % count) ^ 1) + 1) for i in range(count)]
    over = [(i, target % count) for i, target in over]
    inside = [(i, i ^ 1) for i in range(count)]
    return lax.ppermute(across, "gx", over), lax.ppermute(within, "gx", inside)


def per_device(element_rhs_load, metric, coarse_factor):
    constants = jnp.asarray(TABLE)
    factor = coarse_factor.reshape(10, 32, 16).transpose(1, 0, 2).reshape(32, 160)
    factor = jnp.pad(factor, ((0, 0), (0, 96)))
    (send,) = run(coarse_start, [(N_GZ, 2, 128)], element_rhs_load, factor, constants)
    tree = lax.all_to_all(send, "gz", 0, 0, tiled=True)
    near, up, down = run(
        pack, [(136, 128), (80, 128), (80, 128)], element_rhs_load, metric
    )
    below, far_below = shifted(near, "gz", 1), shifted(up, "gz", 2)
    above, far_above = shifted(near, "gz", -1), shifted(down, "gz", -2)
    wide, edge, rows, low, high = run(
        gather, [field_shape(8), (16, 128), (32, 128)] + [(Facross_refE_ROWS, 128)] * 2,
        near, below, far_below, above, far_above,
    )
    left, right = swap_x(low, high)
    rhs, inverse, smooth, applied, low, high = run(
        begin, [field_shape(6)] * 3 + [field_shape(8)] + [(64, 128)] * 2,
        wide, edge, rows, left, right, constants,
    )
    left, right = swap_x(low, high)
    (send,) = run(lower_tree, [(N_GX, 2, 128)], tree)
    tree = lax.all_to_all(send, "gx", 0, 0, tiled=True)
    update = smooth
    for step, count in ((0, 6), (1, 4)):

        def stage(*refs, step=step, count=count):
            sweep(*refs, step=step, count=count)

        smooth, update, applied, low, high = run(
            stage, [field_shape(count)] * 3 + [(8 * count, 128)] * 2,
            applied, left, right, rhs, inverse, smooth, update, rows, constants,
        )
        left, right = swap_x(low, high)
    precond, applied, send = run(
        last_sweep, [field_shape(2)] * 2 + [(N_GX, 16, 128)],
        applied, left, right, rhs, inverse, smooth, update, rows, tree, factor, near, constants,
    )
    received = lax.all_to_all(send, "gx", 0, 0, tiled=True)
    summed, send = run(middle, [field_shape(2), (N_GZ, 8, 128)], applied, received)
    received = lax.all_to_all(send, "gz", 0, 0, tiled=True)
    solution_field, residual = run(
        finish, [field_shape(2)] * 2, summed, received, precond, rhs, last=True
    )
    shape = element_rhs_load.shape
    return solution_field.reshape(shape), residual.reshape(shape)


def solution(mesh):
    placed = (
        P("gx", None, "gz", None, None),
        P(None, "gx", "gz", None),
        P("gx", "gz", None, None, None),
    )
    return jax.shard_map(
        per_device,
        mesh=mesh,
        in_specs=placed,
        out_specs=(P("gx", None, "gz", None, None), P("gx", None, "gz", None, None)),
        check_vma=False,
    )
```

```python
import jax
import jax.numpy as jnp
import numpy as np
from jax import lax
from jax.experimental import pallas as pl
from jax.experimental.pallas import tpu as pltpu
from jax.sharding import PartitionSpec as P

CHEB = 4
N_GX = 32
N_GZ = 16
F32 = jnp.float32
HIGHEST = lax.Precision.HIGHEST
TREE_Z, TREE_X = 0, 0
END_Z, END_X = 9, 20

cheb_high = 2.0
cheb_low = 0.1
gll_inner = (
    -0.8717401485096066,
    -0.5917001814331423,
    -0.2092992179024789,
    0.2092992179024789,
    0.5917001814331423,
    0.8717401485096066,
)


def legendre_seven(points):
    before = np.ones(points.shape[0])
    current = points.copy()
    for degree in range(1, 7):
        following = ((2.0 * degree + 1.0) * points * current - degree * before) / (degree + 1.0)
        before = current
        current = following
    return current


def gll_tables():
    order = 7
    points = np.concatenate([[-1.0], np.array(gll_inner), [1.0]])
    values = legendre_seven(points)
    weights = 2.0 / (order * (order + 1) * values**2)
    count = order + 1
    deriv = np.zeros((count, count))
    for row_index in range(count):
        for col_index in range(count):
            if row_index != col_index:
                deriv[row_index, col_index] = values[row_index] / (
                    values[col_index] * (points[row_index] - points[col_index])
                )
    deriv[0, 0] = -order * (order + 1) / 4.0
    deriv[-1, -1] = order * (order + 1) / 4.0
    stiff = deriv.T @ (weights[:, None] * deriv)
    return (points, weights, stiff)


POINTS, WEIGHTS, STIFF = gll_tables()
KDIAG = np.diag(STIFF)
W = [float(v) for v in WEIGHTS]
KD = [float(v) for v in KDIAG]
K = [[float(v) for v in row] for row in STIFF]


def positions(count):
    return ((np.arange(count)[:, None] + (1.0 + POINTS[None, :]) / 2.0) / count).reshape(-1)


ALONG_X = np.stack([np.sin(np.pi * mode * positions(1)) for mode in (1, 2)])
ALONG_Z = np.stack([np.sin(np.pi * mode * positions(2)) for mode in (1, 2)])
ALONG_Y = np.stack([np.sin(np.pi * mode * positions(16)) for mode in range(1, 9)])


def build_tables():
    w_l = np.tile(WEIGHTS, 16)[None, :]
    k_l = np.tile(KDIAG, 16)[None, :]
    w_j = WEIGHTS[:, None]
    k_j = KDIAG[:, None]
    ones = np.ones((1, 128))
    pieces = {
        "stiff": np.kron(np.eye(16), STIFF),
        "ww": w_j * w_l,
        "kw": k_j * w_l,
        "wk": w_j * k_l,
        "wl": np.ones((8, 1)) * w_l,
        "wj": w_j * ones,
        "modes": np.tile(ALONG_Y, (4, 1)),
    }
    for b in range(2):
        for z in range(2):
            pieces[f"bz{b}{z}"] = ALONG_Z[b, 8 * z : 8 * z + 8, None] * ones
    offsets = {}
    rows = []
    start = 0
    for name, piece in pieces.items():
        offsets[name] = (start, start + piece.shape[0])
        rows.append(piece)
        start += piece.shape[0]
    return np.concatenate(rows).astype(np.float32), offsets


TABLE, OFFSETS = build_tables()


def chebyshev_steps():
    theta = 0.5 * (cheb_high + cheb_low)
    delta = 0.5 * (cheb_high - cheb_low)
    sigma = theta / delta
    rho = 1.0 / sigma
    steps = []
    for sweep in range(CHEB - 1):
        rho_next = 1.0 / (2.0 * sigma - rho)
        steps.append((rho_next * rho, 2.0 * rho_next / delta))
        rho = rho_next
    return theta, steps


THETA, STEPS = chebyshev_steps()


def table(table_ref, name):
    low, high = OFFSETS[name]
    return table_ref[low:high, :]


def lane_iota():
    return lax.broadcasted_iota(jnp.int32, (8, 128), 1)


def read(ref, first=0, count=2):
    return [[ref[i, c] for c in range(first, first + count)] for i in range(8)]


def write(ref, field):
    for i in range(8):
        for c, value in enumerate(field[i]):
            ref[i, c] = value


def spread(row):
    return jnp.broadcast_to(row, (8, 128))


def sum_x(field, left, right):
    out = [list(row) for row in field]
    for c in range(len(field[0])):
        out[0][c] = field[0][c] + left[c]
        out[7][c] = field[7][c] + right[c]
    return out


def sum_z(field, before=None, after=None):
    node = lax.broadcasted_iota(jnp.int32, (8, 128), 0)
    count = len(field[0])
    out = []
    for i in range(8):
        lows = [None] + [field[i][c][7:8, :] for c in range(count - 1)]
        highs = [field[i][c][0:1, :] for c in range(1, count)] + [None]
        if before is not None:
            lows[0], highs[-1] = before(i), after(i)
        out.append(
            [
                field[i][c]
                + jnp.where(node == 0, spread(lows[c]), jnp.where(node == 7, spread(highs[c]), 0.0))
                for c in range(count)
                if lows[c] is not None and highs[c] is not None
            ]
        )
    return out


def sum_y(field):
    lane = lane_iota()
    first = (lane % 8 == 0) & (lane > 0)
    last = (lane % 8 == 7) & (lane < 127)
    return each(
        lambda value: value
        + jnp.where(last, pltpu.roll(value, 127, 1), jnp.where(first, pltpu.roll(value, 1, 1), 0.0)),
        field,
    )


def wall(value):
    lane = lane_iota()
    return jnp.where((lane == 0) | (lane == 127), 0.0, value)


def each(function, *fields):
    return [[function(*values) for values in zip(*rows)] for rows in zip(*fields)]


ROWS = 10


def metric_row(ref, base, m, column):
    row = base + ROWS * m + 4 + column
    return ref[row : row + 1, :]


def element_apply(field, first, metric_ref, table_ref):
    count = len(field[0])
    stiff = table(table_ref, "stiff")
    out = [[None] * count for i in range(8)]
    for c in range(count):
        stacked = jnp.concatenate([field[i][c] for i in range(8)], axis=0)
        along_l = jnp.dot(stacked, stiff, precision=HIGHEST, preferred_element_type=F32)
        along_j = jnp.dot(
            stiff[0:64, 0:64], stacked, precision=HIGHEST, preferred_element_type=F32
        )
        rows = [spread(metric_row(metric_ref, 0, m, first + c)) for m in range(3)]
        scale_x = rows[0] * table(table_ref, "ww")
        scale_z = rows[1] * table(table_ref, "wl")
        scale_y = rows[2] * table(table_ref, "wj")
        for p in range(8):
            along_i = K[0][p] * field[0][c]
            for i in range(1, 8):
                along_i = along_i + K[i][p] * field[i][c]
            out[p][c] = scale_x * along_i + W[p] * (
                scale_z * along_j[8 * p : 8 * p + 8, :] + scale_y * along_l[8 * p : 8 * p + 8, :]
            )
    return out


def diagonal_parts(ref, base, column, table_ref):
    part_x = spread(metric_row(ref, base, 0, column)) * table(table_ref, "ww")
    part_rest = spread(metric_row(ref, base, 1, column)) * table(table_ref, "kw") + spread(
        metric_row(ref, base, 2, column)
    ) * table(table_ref, "wk")
    return part_x, part_rest


def diagonal_sum_x(rows_ref, left_ref, right_ref, column, table_ref):
    part_x, part_rest = diagonal_parts(rows_ref, 0, column, table_ref)
    out = []
    for i in range(8):
        sum_of_x, sum_of_rest = part_x, part_rest
        if i in (0, 7):
            side = left_ref if i == 0 else right_ref
            side_x, side_rest = diagonal_parts(side, Facross_refE_METRIC, column, table_ref)
            sum_of_x, sum_of_rest = part_x + side_x, part_rest + side_rest
        out.append(KD[i] * sum_of_x + W[i] * sum_of_rest)
    return out


class Faces:
    def __init__(self, across_ref, within_ref):
        self.odd = lax.rem(lax.axis_index("gx"), 2) == 1
        self.across, self.within = across_ref, within_ref

    def put(self, first, last, low, high):
        self.across[first:last, :] = jnp.where(self.odd, high, low)
        self.within[first:last, :] = jnp.where(self.odd, low, high)


class Side:
    def __init__(self, across_ref, within_ref, right):
        odd = lax.rem(lax.axis_index("gx"), 2) == 1
        self.across = odd if right else jnp.logical_not(odd)
        self.across_ref, self.within_ref = across_ref, within_ref

    def __getitem__(self, where):
        return jnp.where(self.across, self.across_ref[where], self.within_ref[where])


def sides(across_ref, within_ref):
    return Side(across_ref, within_ref, False), Side(across_ref, within_ref, True)


def write_x_faces(field, across_ref, within_ref):
    out = Faces(across_ref, within_ref)
    for c in range(len(field[0])):
        out.put(8 * c, 8 * c + 8, field[0][c], field[7][c])


def faces(ref, count):
    return [ref[8 * c : 8 * c + 8, :] for c in range(count)]


def pack(load_ref, metric_ref, near_ref, up_ref, down_ref):
    element = lax.broadcasted_iota(jnp.int32, (16, 128), 0)
    lane = lax.broadcasted_iota(jnp.int32, (16, 128), 1)
    expand = jnp.where(element == lane // 8, 1.0, 0.0)
    for ref, start in ((near_ref, 128), (up_ref, 72), (down_ref, 72)):
        ref[start + 6 : start + 8, :] = jnp.zeros((2, 128), F32)
    for m in range(3):
        expanded = jnp.dot(
            metric_ref[m, 0], expand, precision=HIGHEST, preferred_element_type=F32
        )
        for ref, start in ((near_ref, 128), (up_ref, 72), (down_ref, 72)):
            ref[start + 2 * m : start + 2 * m + 2, :] = expanded
    for i in range(8):
        for z in range(2):
            near_ref[8 * (2 * i + z) : 8 * (2 * i + z) + 8, :] = load_ref[0, i, z]
        up_ref[8 * i : 8 * i + 8, :] = load_ref[0, i, 1]
        up_ref[64 + i : 65 + i, :] = load_ref[0, i, 0, 7:8, :]
        down_ref[8 * i : 8 * i + 8, :] = load_ref[0, i, 0]
        down_ref[64 + i : 65 + i, :] = load_ref[0, i, 1, 0:1, :]


Facross_refE_METRIC = 72
Facross_refE_ROWS = 104


def gather(
    near_ref, below_ref, far_below_ref, above_ref, far_above_ref,
    load_ref, edge_ref, rows_ref, low_ref, high_ref,
):
    for i in range(8):
        load_ref[i, 0] = far_below_ref[8 * i : 8 * i + 8, :]
        load_ref[i, 7] = far_above_ref[8 * i : 8 * i + 8, :]
        for z in range(2):
            start = 8 * (2 * i + z)
            load_ref[i, 1 + z] = below_ref[start : start + 8, :]
            load_ref[i, 3 + z] = near_ref[start : start + 8, :]
            load_ref[i, 5 + z] = above_ref[start : start + 8, :]
    edge_ref[0:8, :] = far_below_ref[64:72, :]
    edge_ref[8:16, :] = far_above_ref[64:72, :]
    sources = (
        (far_below_ref, 72), (below_ref, 128), (near_ref, 128), (above_ref, 128), (far_above_ref, 72),
    )
    for index, (source, start) in enumerate(sources):
        for m in range(3):
            row = ROWS * m + 2 * index
            rows_ref[row : row + 2, :] = source[start + 2 * m : start + 2 * m + 2, :]
    rows_ref[30:32, :] = jnp.zeros((2, 128), F32)
    rows = rows_ref[...]
    out = Faces(low_ref, high_ref)
    for c in range(8):
        out.put(8 * c, 8 * c + 8, load_ref[0, c], load_ref[7, c])
    for row, ref in ((64, far_below_ref), (65, far_above_ref)):
        out.put(row, row + 1, ref[64:65, :], ref[71:72, :])
    for ref in (low_ref, high_ref):
        ref[66:72, :] = jnp.zeros((6, 128), F32)
        ref[Facross_refE_METRIC:Facross_refE_ROWS, :] = rows


def with_sums(face, first, second):
    lane = lane_iota()
    return jnp.where(lane == 0, first, jnp.where(lane == 127, second, face))


def send_along_x(field, first, second, send_ref):
    here = lax.axis_index("gx")
    above = lax.rem(here + 1, N_GX)
    low = [with_sums(field[0][0], first, second), field[0][1]]
    high = [with_sums(field[7][0], first, second), field[7][1]]
    for chunk in range(N_GX):
        for z in range(2):
            send_ref[chunk, 8 * z : 8 * z + 8, :] = jnp.where(
                above == (chunk + END_X) % N_GX, high[z], low[z]
            )


def send_along_z(field, sums, send_ref):
    here = lax.axis_index("gz")
    above = lax.rem(here + 1, N_GZ)
    node = lax.broadcasted_iota(jnp.int32, (8, 128), 0)
    low = high = jnp.zeros((8, 128), F32)
    for i in range(8):
        low = jnp.where(node == i, spread(field[i][0][0:1, :]), low)
        high = jnp.where(node == i, spread(field[i][1][7:8, :]), high)
    low, high = with_sums(low, sums, sums), with_sums(high, sums, sums)
    for chunk in range(N_GZ):
        send_ref[chunk] = jnp.where(above == (chunk + END_Z) % N_GZ, high, low)


def coarse_start(load_ref, factor_ref, table_ref, send_ref):
    parts = []
    load = [[wall(load_ref[0, i, z]) for z in range(2)] for i in range(8)]
    for a in range(2):
        along_x = []
        for z in range(2):
            total = float(ALONG_X[a, 0]) * load[0][z]
            for i in range(1, 8):
                total = total + float(ALONG_X[a, i]) * load[i][z]
            along_x.append(total)
        for b in range(2):
            both = (
                table(table_ref, f"bz{b}0") * along_x[0] + table(table_ref, f"bz{b}1") * along_x[1]
            )
            parts.append(jnp.sum(both, axis=0, keepdims=True))
    node = lax.broadcasted_iota(jnp.int32, (8, 128), 0)
    stacked = jnp.zeros((8, 128), F32)
    for index, part in enumerate(parts):
        stacked = jnp.where(node == index, spread(part), stacked)
    modes = lax.dot_general(
        stacked, table(table_ref, "modes"), (((1,), (1,)), ((), ())),
        precision=HIGHEST, preferred_element_type=F32,
    )
    owner = lax.broadcasted_iota(jnp.int32, (8, 32), 1) // 8
    row = lax.broadcasted_iota(jnp.int32, (8, 32), 0)
    coarse_rhs = jnp.sum(jnp.where(owner == row, modes, 0.0), axis=0, keepdims=True)
    own = jnp.dot(
        jnp.broadcast_to(coarse_rhs, (8, 32)), factor_ref[...],
        precision=HIGHEST, preferred_element_type=F32,
    )
    write_pairs(send_ref, own[0:1, 0:128], own[0:1, 128:256])


def begin(
    load_ref, edge_ref, rows_ref, across_ref, within_ref, table_ref,
    rhs_ref, inverse_ref, smooth_ref, applied_ref, across_out, within_out,
):
    left_ref, right_ref = sides(across_ref, within_ref)

    def edge(which):
        start = 8 * which

        def row(i):
            value = edge_ref[start + i : start + i + 1, :]
            if i == 0:
                value = value + left_ref[64 + which : 65 + which, :]
            if i == 7:
                value = value + right_ref[64 + which : 65 + which, :]
            return value

        return row

    load = sum_x(read(load_ref, 0, 8), faces(left_ref, 8), faces(right_ref, 8))
    rhs = each(wall, sum_y(sum_z(load, edge(0), edge(1))))
    columns = [
        diagonal_sum_x(rows_ref, left_ref, right_ref, column, table_ref) for column in range(-4, 6)
    ]
    diagonal = sum_z([[columns[c][i] for c in range(10)] for i in range(8)])
    inverse = each(lambda d: wall(1.0 / d), sum_y(diagonal))
    smooth = each(lambda d, r: d * r / THETA, inverse, rhs)
    write(rhs_ref, [row[1:7] for row in rhs])
    write(inverse_ref, [row[1:7] for row in inverse])
    write(smooth_ref, [row[1:7] for row in smooth])
    applied = element_apply(smooth, -3, rows_ref, table_ref)
    write(applied_ref, applied)
    write_x_faces(applied, across_out, within_out)


def write_pairs(ref, first, second):
    row = lax.broadcasted_iota(jnp.int32, (8, 128), 0)
    pairs = jnp.where(row % 2 == 0, spread(first), spread(second))
    for start in range(0, ref.shape[0], 8):
        ref[start : start + 8, :] = pairs


def tree_sums(ref, here, skipped, head):
    row = lax.broadcasted_iota(jnp.int32, (8, 128), 0)
    level = (row % 2) * 8 + lane_iota() // 16
    shift = jnp.maximum(level - skipped, 0)
    mine = lax.shift_right_logical(jnp.full((8, 128), here, jnp.int32), shift)
    total = jnp.zeros((8, 128), F32)
    for start in range(0, ref.shape[0], 8):
        device = (head + start // 2 + row // 2) % (ref.shape[0] // 2)
        other = lax.shift_right_logical(device, shift)
        total = total + jnp.where(other == mine, ref[start : start + 8, :], 0.0)
    first = jnp.sum(jnp.where(row % 2 == 0, total, 0.0), axis=0, keepdims=True)
    second = jnp.sum(jnp.where(row % 2 == 1, total, 0.0), axis=0, keepdims=True)
    return first, second


def neighbours(axis, count, head):
    here = lax.axis_index(axis) + count - head
    return lax.rem(here + count - 1, count), lax.rem(here + 1, count)


def lower_tree(received_ref, send_ref):
    write_pairs(send_ref, *tree_sums(received_ref, lax.axis_index("gz"), 0, TREE_Z))


def x_faces_received(received_ref):
    below, above = neighbours("gx", N_GX, END_X)
    left = [received_ref[below, 8 * z : 8 * z + 8, :] for z in range(2)]
    right = [received_ref[above, 8 * z : 8 * z + 8, :] for z in range(2)]
    return left, right


def relax(step, count, applied_ref, across_ref, within_ref, rhs_ref, inverse_ref, smooth_ref, update_ref):
    left_ref, right_ref = sides(across_ref, within_ref)
    field = sum_x(
        read(applied_ref, 0, count + 2), faces(left_ref, count + 2), faces(right_ref, count + 2)
    )
    image = each(wall, sum_y(sum_z(field)))
    first, second = STEPS[step]
    inset = (6 - count) // 2
    shift = 1 if step else 0
    update = each(
        lambda u, d, r, a: first * u + (second * d) * (r - a),
        read(update_ref, shift, count), read(inverse_ref, inset, count), read(rhs_ref, inset, count),
        image,
    )
    return each(lambda s, u: s + u, read(smooth_ref, shift, count), update), update


def sweep(
    applied_ref, across_ref, within_ref, rhs_ref, inverse_ref, smooth_ref, update_ref, rows_ref, table_ref,
    next_ref, next_update_ref, out_ref, low_ref, high_ref, *, step, count,
):
    smooth, update = relax(
        step, count, applied_ref, across_ref, within_ref, rhs_ref, inverse_ref, smooth_ref, update_ref
    )
    write(next_ref, smooth)
    write(next_update_ref, update)
    applied = element_apply(smooth, 1 - count // 2, rows_ref, table_ref)
    write(out_ref, applied)
    write_x_faces(applied, low_ref, high_ref)


def coarse_field(received_ref, factor_ref, table_ref):
    first, second = tree_sums(received_ref, lax.axis_index("gx"), 4, TREE_X)
    columns = jnp.broadcast_to(jnp.concatenate([first, second], axis=1), (8, 256))
    coarse = lax.dot_general(
        columns, factor_ref[...], (((1,), (1,)), ((), ())),
        precision=HIGHEST, preferred_element_type=F32,
    )
    owner = lax.broadcasted_iota(jnp.int32, (8, 32), 1) // 8
    row = lax.broadcasted_iota(jnp.int32, (8, 32), 0)
    across = jnp.dot(
        jnp.where(owner == row, coarse, 0.0), table(table_ref, "modes"),
        precision=HIGHEST, preferred_element_type=F32,
    )
    out = [[None, None] for i in range(8)]
    for z in range(2):
        along_z = []
        for a in range(2):
            along_z.append(
                table(table_ref, f"bz0{z}") * spread(across[2 * a : 2 * a + 1, :])
                + table(table_ref, f"bz1{z}") * spread(across[2 * a + 1 : 2 * a + 2, :])
            )
        for i in range(8):
            out[i][z] = wall(float(ALONG_X[0, i]) * along_z[0] + float(ALONG_X[1, i]) * along_z[1])
    return out


def last_sweep(
    applied_ref, across_ref, within_ref, rhs_ref, inverse_ref, smooth_ref, update_ref, rows_ref,
    tree_ref, factor_ref, near_ref, table_ref,
    precond_ref, out_ref, send_ref,
):
    smooth, update = relax(
        2, 2, applied_ref, across_ref, within_ref, rhs_ref, inverse_ref, smooth_ref, update_ref
    )
    coarse = coarse_field(tree_ref, factor_ref, table_ref)
    precond = each(lambda s, c: s + c, smooth, coarse)
    write(precond_ref, precond)
    applied = element_apply(precond, 0, rows_ref, table_ref)
    write(out_ref, applied)
    first = jnp.zeros((8, 128), F32)
    second = jnp.zeros((8, 128), F32)
    for i in range(8):
        for z in range(2):
            start = 8 * (2 * i + z)
            first = first + near_ref[start : start + 8, :] * precond[i][z]
            second = second + applied[i][z] * precond[i][z]
    send_along_x(
        applied,
        jnp.sum(first, axis=1, keepdims=True),
        jnp.sum(second, axis=1, keepdims=True),
        send_ref,
    )


def middle(applied_ref, received_ref, summed_ref, send_ref):
    field = sum_x(read(applied_ref), *x_faces_received(received_ref))
    write(summed_ref, field)
    sums = received_ref[0, 0:8, :]
    for e in range(1, N_GX):
        sums = sums + received_ref[e, 0:8, :]
    send_along_z(field, sums, send_ref)


def finish(summed_ref, received_ref, precond_ref, rhs_ref, solution_ref, residual_ref):
    below, above = neighbours("gz", N_GZ, END_Z)
    field = sum_z(
        read(summed_ref),
        lambda i: received_ref[below, i : i + 1, :],
        lambda i: received_ref[above, i : i + 1, :],
    )
    image = each(wall, sum_y(field))
    sums = received_ref[0]
    for e in range(1, N_GZ):
        sums = sums + received_ref[e]
    sums = jnp.sum(sums, axis=0, keepdims=True)
    alpha = spread(sums[:, 0:1] / sums[:, 127:128])
    write(solution_ref, each(lambda p: alpha * p, read(precond_ref)))
    write(residual_ref, each(lambda r, a: r - alpha * a, read(rhs_ref, 2, 2), image))


def field_shape(count):
    return (8, count, 8, 128)


def run(kernel, shapes, *operands, first=False, last=False):
    spec = pl.BlockSpec(memory_space=pltpu.VMEM)
    outs = [
        jax.ShapeDtypeStruct(shape, F32) if last else pltpu.VMEM(shape, F32) for shape in shapes
    ]
    if not first:
        operands = [pltpu.with_memory_space_constraint(value, pltpu.VMEM) for value in operands]
    return pl.pallas_call(
        kernel, out_shape=outs, in_specs=[spec] * len(operands), out_specs=[spec] * len(outs)
    )(*operands)


def shifted(value, axis, distance):
    count = lax.axis_size(axis)
    return lax.ppermute(value, axis, [(i, (i + distance) % count) for i in range(count)])


def swap_x(across, within):
    count = lax.axis_size("gx")
    over = [(i, (((i - 1) % count) ^ 1) + 1) for i in range(count)]
    over = [(i, target % count) for i, target in over]
    inside = [(i, i ^ 1) for i in range(count)]
    return lax.ppermute(across, "gx", over), lax.ppermute(within, "gx", inside)


def send_chunks(chunks, axis, head):
    count = lax.axis_size(axis)
    group = [(head + k) % count for k in range(count)]
    return lax.all_to_all(chunks, axis, 0, 0, tiled=True, axis_index_groups=[group])


def send_pairs(pairs, axis, head):
    return send_chunks(pairs.reshape(-1, 2, 128), axis, head).reshape(pairs.shape)


def per_device(element_rhs_load, metric, coarse_factor):
    constants = jnp.asarray(TABLE)
    factor = coarse_factor.reshape(10, 32, 16).transpose(1, 0, 2).reshape(32, 160)
    factor = jnp.pad(factor, ((0, 0), (0, 96)))
    near, up, down = run(
        pack, [(136, 128), (80, 128), (80, 128)], element_rhs_load, metric, first=True
    )
    below, far_below = shifted(near, "gz", 1), shifted(up, "gz", 2)
    above, far_above = shifted(near, "gz", -1), shifted(down, "gz", -2)
    wide, edge, rows, low, high = run(
        gather, [field_shape(8), (16, 128), (32, 128)] + [(Facross_refE_ROWS, 128)] * 2,
        near, below, far_below, above, far_above,
    )
    left, right = swap_x(low, high)
    rhs, inverse, smooth, applied, low, high = run(
        begin, [field_shape(6)] * 3 + [field_shape(8)] + [(64, 128)] * 2,
        wide, edge, rows, left, right, constants,
    )
    left, right = swap_x(low, high)
    (send,) = run(coarse_start, [(2 * N_GZ, 128)], element_rhs_load, factor, constants)
    tree = send_pairs(send, "gz", TREE_Z)
    (send,) = run(lower_tree, [(2 * N_GX, 128)], tree)
    tree = send_pairs(send, "gx", TREE_X)
    update = smooth
    for step, count in ((0, 6), (1, 4)):

        def stage(*refs, step=step, count=count):
            sweep(*refs, step=step, count=count)

        smooth, update, applied, low, high = run(
            stage, [field_shape(count)] * 3 + [(8 * count, 128)] * 2,
            applied, left, right, rhs, inverse, smooth, update, rows, constants,
        )
        left, right = swap_x(low, high)
    precond, applied, send = run(
        last_sweep, [field_shape(2)] * 2 + [(N_GX, 16, 128)],
        applied, left, right, rhs, inverse, smooth, update, rows, tree, factor, near, constants,
    )
    received = send_chunks(send, "gx", END_X)
    summed, send = run(middle, [field_shape(2), (N_GZ, 8, 128)], applied, received)
    received = send_chunks(send, "gz", END_Z)
    solution_field, residual = run(
        finish, [field_shape(2)] * 2, summed, received, precond, rhs, last=True
    )
    shape = element_rhs_load.shape
    return solution_field.reshape(shape), residual.reshape(shape)


def solution(mesh):
    placed = (
        P("gx", None, "gz", None, None),
        P(None, "gx", "gz", None),
        P("gx", "gz", None, None, None),
    )
    return jax.shard_map(
        per_device,
        mesh=mesh,
        in_specs=placed,
        out_specs=(P("gx", None, "gz", None, None), P("gx", None, "gz", None, None)),
        check_vma=False,
    )
```

```python
import jax
import jax.numpy as jnp
import numpy as np
from jax import lax
from jax.experimental import pallas as pl
from jax.experimental.pallas import tpu as pltpu
from jax.sharding import PartitionSpec as P

CHEB = 4
N_GX = 32
N_GZ = 16
F32 = jnp.float32
HIGHEST = lax.Precision.HIGHEST
TREE_Z, TREE_X = 0, 0
END_Z, END_X = 9, 20

cheb_high = 2.0
cheb_low = 0.1
gll_inner = (
    -0.8717401485096066,
    -0.5917001814331423,
    -0.2092992179024789,
    0.2092992179024789,
    0.5917001814331423,
    0.8717401485096066,
)


def legendre_seven(points):
    before = np.ones(points.shape[0])
    current = points.copy()
    for degree in range(1, 7):
        following = ((2.0 * degree + 1.0) * points * current - degree * before) / (degree + 1.0)
        before = current
        current = following
    return current


def gll_tables():
    order = 7
    points = np.concatenate([[-1.0], np.array(gll_inner), [1.0]])
    values = legendre_seven(points)
    weights = 2.0 / (order * (order + 1) * values**2)
    count = order + 1
    deriv = np.zeros((count, count))
    for row_index in range(count):
        for col_index in range(count):
            if row_index != col_index:
                deriv[row_index, col_index] = values[row_index] / (
                    values[col_index] * (points[row_index] - points[col_index])
                )
    deriv[0, 0] = -order * (order + 1) / 4.0
    deriv[-1, -1] = order * (order + 1) / 4.0
    stiff = deriv.T @ (weights[:, None] * deriv)
    return (points, weights, stiff)


POINTS, WEIGHTS, STIFF = gll_tables()
KDIAG = np.diag(STIFF)
W = [float(v) for v in WEIGHTS]
KD = [float(v) for v in KDIAG]
K = [[float(v) for v in row] for row in STIFF]


def positions(count):
    return ((np.arange(count)[:, None] + (1.0 + POINTS[None, :]) / 2.0) / count).reshape(-1)


ALONG_X = np.stack([np.sin(np.pi * mode * positions(1)) for mode in (1, 2)])
ALONG_Z = np.stack([np.sin(np.pi * mode * positions(2)) for mode in (1, 2)])
ALONG_Y = np.stack([np.sin(np.pi * mode * positions(16)) for mode in range(1, 9)])


def build_tables():
    w_l = np.tile(WEIGHTS, 16)[None, :]
    k_l = np.tile(KDIAG, 16)[None, :]
    w_j = WEIGHTS[:, None]
    k_j = KDIAG[:, None]
    ones = np.ones((1, 128))
    pieces = {
        "stiff": np.kron(np.eye(16), STIFF),
        "ww": w_j * w_l,
        "kw": k_j * w_l,
        "wk": w_j * k_l,
        "wl": np.ones((8, 1)) * w_l,
        "wj": w_j * ones,
        "modes": np.tile(ALONG_Y, (4, 1)),
    }
    for b in range(2):
        for z in range(2):
            pieces[f"bz{b}{z}"] = ALONG_Z[b, 8 * z : 8 * z + 8, None] * ones
    offsets = {}
    rows = []
    start = 0
    for name, piece in pieces.items():
        offsets[name] = (start, start + piece.shape[0])
        rows.append(piece)
        start += piece.shape[0]
    return np.concatenate(rows).astype(np.float32), offsets


TABLE, OFFSETS = build_tables()


def chebyshev_steps():
    theta = 0.5 * (cheb_high + cheb_low)
    delta = 0.5 * (cheb_high - cheb_low)
    sigma = theta / delta
    rho = 1.0 / sigma
    steps = []
    for sweep in range(CHEB - 1):
        rho_next = 1.0 / (2.0 * sigma - rho)
        steps.append((rho_next * rho, 2.0 * rho_next / delta))
        rho = rho_next
    return theta, steps


THETA, STEPS = chebyshev_steps()


def table(table_ref, name):
    low, high = OFFSETS[name]
    return table_ref[low:high, :]


def lane_iota():
    return lax.broadcasted_iota(jnp.int32, (8, 128), 1)


def read(ref, first=0, count=2):
    return [[ref[i, c] for c in range(first, first + count)] for i in range(8)]


def write(ref, field):
    for i in range(8):
        for c, value in enumerate(field[i]):
            ref[i, c] = value


def spread(row):
    return jnp.broadcast_to(row, (8, 128))


def sum_x(field, left, right):
    out = [list(row) for row in field]
    for c in range(len(field[0])):
        out[0][c] = field[0][c] + left[c]
        out[7][c] = field[7][c] + right[c]
    return out


def sum_z(field, before=None, after=None):
    node = lax.broadcasted_iota(jnp.int32, (8, 128), 0)
    count = len(field[0])
    out = []
    for i in range(8):
        lows = [None] + [field[i][c][7:8, :] for c in range(count - 1)]
        highs = [field[i][c][0:1, :] for c in range(1, count)] + [None]
        if before is not None:
            lows[0], highs[-1] = before(i), after(i)
        out.append(
            [
                field[i][c]
                + jnp.where(node == 0, spread(lows[c]), jnp.where(node == 7, spread(highs[c]), 0.0))
                for c in range(count)
                if lows[c] is not None and highs[c] is not None
            ]
        )
    return out


def sum_y(field):
    lane = lane_iota()
    first = (lane % 8 == 0) & (lane > 0)
    last = (lane % 8 == 7) & (lane < 127)
    return each(
        lambda value: value
        + jnp.where(last, pltpu.roll(value, 127, 1), jnp.where(first, pltpu.roll(value, 1, 1), 0.0)),
        field,
    )


def wall(value):
    lane = lane_iota()
    return jnp.where((lane == 0) | (lane == 127), 0.0, value)


def each(function, *fields):
    return [[function(*values) for values in zip(*rows)] for rows in zip(*fields)]


ROWS = 10


def metric_row(ref, base, m, column):
    row = base + ROWS * m + 4 + column
    return ref[row : row + 1, :]


def element_apply(field, first, metric_ref, table_ref):
    count = len(field[0])
    stiff = table(table_ref, "stiff")
    out = [[None] * count for i in range(8)]
    columns = [jnp.concatenate([field[i][c] for i in range(8)], axis=0) for c in range(count)]
    along_y = jnp.dot(
        jnp.concatenate(columns, axis=0), stiff, precision=HIGHEST, preferred_element_type=F32
    )
    for c in range(count):
        stacked = columns[c]
        along_l = along_y[64 * c : 64 * c + 64, :]
        along_j = jnp.dot(
            stiff[0:64, 0:64], stacked, precision=HIGHEST, preferred_element_type=F32
        )
        rows = [spread(metric_row(metric_ref, 0, m, first + c)) for m in range(3)]
        scale_x = rows[0] * table(table_ref, "ww")
        scale_z = rows[1] * table(table_ref, "wl")
        scale_y = rows[2] * table(table_ref, "wj")
        for p in range(8):
            along_i = K[0][p] * field[0][c]
            for i in range(1, 8):
                along_i = along_i + K[i][p] * field[i][c]
            out[p][c] = scale_x * along_i + W[p] * (
                scale_z * along_j[8 * p : 8 * p + 8, :] + scale_y * along_l[8 * p : 8 * p + 8, :]
            )
    return out


def diagonal_parts(ref, base, column, table_ref):
    part_x = spread(metric_row(ref, base, 0, column)) * table(table_ref, "ww")
    part_rest = spread(metric_row(ref, base, 1, column)) * table(table_ref, "kw") + spread(
        metric_row(ref, base, 2, column)
    ) * table(table_ref, "wk")
    return part_x, part_rest


def diagonal_sum_x(rows_ref, left_ref, right_ref, column, table_ref):
    part_x, part_rest = diagonal_parts(rows_ref, 0, column, table_ref)
    out = []
    for i in range(8):
        sum_of_x, sum_of_rest = part_x, part_rest
        if i in (0, 7):
            side = left_ref if i == 0 else right_ref
            side_x, side_rest = diagonal_parts(side, Facross_refE_METRIC, column, table_ref)
            sum_of_x, sum_of_rest = part_x + side_x, part_rest + side_rest
        out.append(KD[i] * sum_of_x + W[i] * sum_of_rest)
    return out


class Faces:
    def __init__(self, across_ref, within_ref):
        self.odd = lax.rem(lax.axis_index("gx"), 2) == 1
        self.across, self.within = across_ref, within_ref

    def put(self, first, last, low, high):
        self.across[first:last, :] = jnp.where(self.odd, high, low)
        self.within[first:last, :] = jnp.where(self.odd, low, high)


class Either:
    def __init__(self, first, first_ref, second_ref):
        self.first, self.first_ref, self.second_ref = first, first_ref, second_ref

    def __getitem__(self, where):
        return jnp.where(self.first, self.first_ref[where], self.second_ref[where])


class Side:
    def __init__(self, across_ref, within_ref, right):
        odd = lax.rem(lax.axis_index("gx"), 2) == 1
        self.across = odd if right else jnp.logical_not(odd)
        self.across_ref, self.within_ref = across_ref, within_ref

    def __getitem__(self, where):
        return jnp.where(self.across, self.across_ref[where], self.within_ref[where])


def sides(across_ref, within_ref):
    return Side(across_ref, within_ref, False), Side(across_ref, within_ref, True)


def write_x_faces(field, across_ref, within_ref):
    out = Faces(across_ref, within_ref)
    for c in range(len(field[0])):
        out.put(8 * c, 8 * c + 8, field[0][c], field[7][c])


def faces(ref, count):
    return [ref[8 * c : 8 * c + 8, :] for c in range(count)]


def pack(load_ref, metric_ref, near_ref, inner_ref, outer_ref):
    begins = lax.rem(lax.axis_index("gz"), 4) < 2
    element = lax.broadcasted_iota(jnp.int32, (16, 128), 0)
    lane = lax.broadcasted_iota(jnp.int32, (16, 128), 1)
    expand = jnp.where(element == lane // 8, 1.0, 0.0)
    for ref, start in ((near_ref, 128), (inner_ref, 72), (outer_ref, 72)):
        ref[start + 6 : start + 8, :] = jnp.zeros((2, 128), F32)
    for m in range(3):
        expanded = jnp.dot(
            metric_ref[m, 0], expand, precision=HIGHEST, preferred_element_type=F32
        )
        for ref, start in ((near_ref, 128), (inner_ref, 72), (outer_ref, 72)):
            ref[start + 2 * m : start + 2 * m + 2, :] = expanded
    for i in range(8):
        for z in range(2):
            near_ref[8 * (2 * i + z) : 8 * (2 * i + z) + 8, :] = load_ref[0, i, z]
        rows = slice(8 * i, 8 * i + 8)
        inner_ref[rows, :] = jnp.where(begins, load_ref[0, i, 1], load_ref[0, i, 0])
        outer_ref[rows, :] = jnp.where(begins, load_ref[0, i, 0], load_ref[0, i, 1])
        up, down = load_ref[0, i, 0, 7:8, :], load_ref[0, i, 1, 0:1, :]
        inner_ref[64 + i : 65 + i, :] = jnp.where(begins, up, down)
        outer_ref[64 + i : 65 + i, :] = jnp.where(begins, down, up)


Facross_refE_METRIC = 72
Facross_refE_ROWS = 104


def gather(
    near_ref, even_ref, odd_ref, inner_ref, outer_ref, earlier_ref,
    load_ref, edge_ref, rows_ref, low_ref, high_ref,
):
    place = lax.axis_index("gz")
    above_ref = Either(lax.rem(place, 2) == 0, even_ref, odd_ref)
    below_ref = Either(lax.rem(place, 2) == 1, even_ref, odd_ref)
    far_above_ref = Either(lax.rem(place, 4) < 2, inner_ref, outer_ref)
    far_below_ref = Either(lax.rem(place, 4) >= 2, inner_ref, outer_ref)
    for i in range(8):
        load_ref[i, 0] = far_below_ref[8 * i : 8 * i + 8, :]
        load_ref[i, 7] = far_above_ref[8 * i : 8 * i + 8, :]
        for z in range(2):
            start = 8 * (2 * i + z)
            load_ref[i, 1 + z] = below_ref[start : start + 8, :]
            load_ref[i, 3 + z] = near_ref[start : start + 8, :]
            load_ref[i, 5 + z] = above_ref[start : start + 8, :]
    edge_ref[0:8, :] = far_below_ref[64:72, :]
    edge_ref[8:16, :] = far_above_ref[64:72, :]
    sources = (
        (far_below_ref, 72), (below_ref, 128), (near_ref, 128), (above_ref, 128), (far_above_ref, 72),
    )
    for index, (source, start) in enumerate(sources):
        for m in range(3):
            row = ROWS * m + 2 * index
            rows_ref[row : row + 2, :] = source[start + 2 * m : start + 2 * m + 2, :]
    rows_ref[30:32, :] = jnp.zeros((2, 128), F32)
    rows = rows_ref[...]
    out = Faces(low_ref, high_ref)
    for c in range(8):
        out.put(8 * c, 8 * c + 8, load_ref[0, c], load_ref[7, c])
    for row, ref in ((64, far_below_ref), (65, far_above_ref)):
        out.put(row, row + 1, ref[64:65, :], ref[71:72, :])
    for ref in (low_ref, high_ref):
        ref[66:72, :] = jnp.zeros((6, 128), F32)
        ref[Facross_refE_METRIC:Facross_refE_ROWS, :] = rows


def with_sums(face, first, second):
    lane = lane_iota()
    return jnp.where(lane == 0, first, jnp.where(lane == 127, second, face))


def send_along_x(field, first, second, send_ref):
    here = lax.axis_index("gx")
    above = lax.rem(here + 1, N_GX)
    low = [with_sums(field[0][0], first, second), field[0][1]]
    high = [with_sums(field[7][0], first, second), field[7][1]]
    for chunk in range(N_GX):
        for z in range(2):
            send_ref[chunk, 8 * z : 8 * z + 8, :] = jnp.where(
                above == (chunk + END_X) % N_GX, high[z], low[z]
            )


def send_along_z(field, sums, send_ref):
    here = lax.axis_index("gz")
    above = lax.rem(here + 1, N_GZ)
    node = lax.broadcasted_iota(jnp.int32, (8, 128), 0)
    low = high = jnp.zeros((8, 128), F32)
    for i in range(8):
        low = jnp.where(node == i, spread(field[i][0][0:1, :]), low)
        high = jnp.where(node == i, spread(field[i][1][7:8, :]), high)
    low, high = with_sums(low, sums, sums), with_sums(high, sums, sums)
    for chunk in range(N_GZ):
        send_ref[chunk] = jnp.where(above == (chunk + END_Z) % N_GZ, high, low)


def near_rows(near_ref, i, z):
    start = 8 * (2 * i + z)
    return near_ref[start : start + 8, :]


def coarse_start(near_ref, factor_ref, table_ref, send_ref):
    parts = []
    load = [[wall(near_rows(near_ref, i, z)) for z in range(2)] for i in range(8)]
    for a in range(2):
        along_x = []
        for z in range(2):
            total = float(ALONG_X[a, 0]) * load[0][z]
            for i in range(1, 8):
                total = total + float(ALONG_X[a, i]) * load[i][z]
            along_x.append(total)
        for b in range(2):
            both = (
                table(table_ref, f"bz{b}0") * along_x[0] + table(table_ref, f"bz{b}1") * along_x[1]
            )
            parts.append(jnp.sum(both, axis=0, keepdims=True))
    node = lax.broadcasted_iota(jnp.int32, (8, 128), 0)
    stacked = jnp.zeros((8, 128), F32)
    for index, part in enumerate(parts):
        stacked = jnp.where(node == index, spread(part), stacked)
    modes = lax.dot_general(
        stacked, table(table_ref, "modes"), (((1,), (1,)), ((), ())),
        precision=HIGHEST, preferred_element_type=F32,
    )
    owner = lax.broadcasted_iota(jnp.int32, (8, 32), 1) // 8
    row = lax.broadcasted_iota(jnp.int32, (8, 32), 0)
    coarse_rhs = jnp.sum(jnp.where(owner == row, modes, 0.0), axis=0, keepdims=True)
    own = jnp.dot(
        jnp.broadcast_to(coarse_rhs, (8, 32)), factor_ref[...],
        precision=HIGHEST, preferred_element_type=F32,
    )
    write_pairs(send_ref, own[0:1, 0:128], own[0:1, 128:256])


def begin(
    load_ref, edge_ref, rows_ref, across_ref, within_ref, table_ref,
    rhs_ref, inverse_ref, smooth_ref, applied_ref, across_out, within_out,
):
    left_ref, right_ref = sides(across_ref, within_ref)

    def edge(which):
        start = 8 * which

        def row(i):
            value = edge_ref[start + i : start + i + 1, :]
            if i == 0:
                value = value + left_ref[64 + which : 65 + which, :]
            if i == 7:
                value = value + right_ref[64 + which : 65 + which, :]
            return value

        return row

    load = sum_x(read(load_ref, 0, 8), faces(left_ref, 8), faces(right_ref, 8))
    rhs = each(wall, sum_y(sum_z(load, edge(0), edge(1))))
    columns = [
        diagonal_sum_x(rows_ref, left_ref, right_ref, column, table_ref) for column in range(-4, 6)
    ]
    diagonal = sum_z([[columns[c][i] for c in range(10)] for i in range(8)])
    inverse = each(lambda d: wall(1.0 / d), sum_y(diagonal))
    smooth = each(lambda d, r: d * r / THETA, inverse, rhs)
    write(rhs_ref, [row[1:7] for row in rhs])
    write(inverse_ref, [row[1:7] for row in inverse])
    write(smooth_ref, [row[1:7] for row in smooth])
    applied = element_apply(smooth, -3, rows_ref, table_ref)
    write(applied_ref, applied)
    write_x_faces(applied, across_out, within_out)


def write_pairs(ref, first, second):
    row = lax.broadcasted_iota(jnp.int32, (8, 128), 0)
    pairs = jnp.where(row % 2 == 0, spread(first), spread(second))
    for start in range(0, ref.shape[0], 8):
        ref[start : start + 8, :] = pairs


def tree_sums(ref, here, skipped, head):
    row = lax.broadcasted_iota(jnp.int32, (8, 128), 0)
    level = (row % 2) * 8 + lane_iota() // 16
    shift = jnp.maximum(level - skipped, 0)
    mine = lax.shift_right_logical(jnp.full((8, 128), here, jnp.int32), shift)
    total = jnp.zeros((8, 128), F32)
    for start in range(0, ref.shape[0], 8):
        device = (head + start // 2 + row // 2) % (ref.shape[0] // 2)
        other = lax.shift_right_logical(device, shift)
        total = total + jnp.where(other == mine, ref[start : start + 8, :], 0.0)
    first = jnp.sum(jnp.where(row % 2 == 0, total, 0.0), axis=0, keepdims=True)
    second = jnp.sum(jnp.where(row % 2 == 1, total, 0.0), axis=0, keepdims=True)
    return first, second


def neighbours(axis, count, head):
    here = lax.axis_index(axis) + count - head
    return lax.rem(here + count - 1, count), lax.rem(here + 1, count)


def lower_tree(received_ref, send_ref):
    write_pairs(send_ref, *tree_sums(received_ref, lax.axis_index("gz"), 0, TREE_Z))


def x_faces_received(received_ref):
    below, above = neighbours("gx", N_GX, END_X)
    left = [received_ref[below, 8 * z : 8 * z + 8, :] for z in range(2)]
    right = [received_ref[above, 8 * z : 8 * z + 8, :] for z in range(2)]
    return left, right


def relax(step, count, applied_ref, across_ref, within_ref, rhs_ref, inverse_ref, smooth_ref, update_ref):
    left_ref, right_ref = sides(across_ref, within_ref)
    field = sum_x(
        read(applied_ref, 0, count + 2), faces(left_ref, count + 2), faces(right_ref, count + 2)
    )
    image = each(wall, sum_y(sum_z(field)))
    first, second = STEPS[step]
    inset = (6 - count) // 2
    shift = 1 if step else 0
    update = each(
        lambda u, d, r, a: first * u + (second * d) * (r - a),
        read(update_ref, shift, count), read(inverse_ref, inset, count), read(rhs_ref, inset, count),
        image,
    )
    return each(lambda s, u: s + u, read(smooth_ref, shift, count), update), update


def sweep(
    applied_ref, across_ref, within_ref, rhs_ref, inverse_ref, smooth_ref, update_ref, rows_ref, table_ref,
    next_ref, next_update_ref, out_ref, low_ref, high_ref, *, step, count,
):
    smooth, update = relax(
        step, count, applied_ref, across_ref, within_ref, rhs_ref, inverse_ref, smooth_ref, update_ref
    )
    write(next_ref, smooth)
    write(next_update_ref, update)
    applied = element_apply(smooth, 1 - count // 2, rows_ref, table_ref)
    write(out_ref, applied)
    write_x_faces(applied, low_ref, high_ref)


def coarse_field(received_ref, factor_ref, table_ref):
    first, second = tree_sums(received_ref, lax.axis_index("gx"), 4, TREE_X)
    columns = jnp.broadcast_to(jnp.concatenate([first, second], axis=1), (8, 256))
    coarse = lax.dot_general(
        columns, factor_ref[...], (((1,), (1,)), ((), ())),
        precision=HIGHEST, preferred_element_type=F32,
    )
    owner = lax.broadcasted_iota(jnp.int32, (8, 32), 1) // 8
    row = lax.broadcasted_iota(jnp.int32, (8, 32), 0)
    across = jnp.dot(
        jnp.where(owner == row, coarse, 0.0), table(table_ref, "modes"),
        precision=HIGHEST, preferred_element_type=F32,
    )
    out = [[None, None] for i in range(8)]
    for z in range(2):
        along_z = []
        for a in range(2):
            along_z.append(
                table(table_ref, f"bz0{z}") * spread(across[2 * a : 2 * a + 1, :])
                + table(table_ref, f"bz1{z}") * spread(across[2 * a + 1 : 2 * a + 2, :])
            )
        for i in range(8):
            out[i][z] = wall(float(ALONG_X[0, i]) * along_z[0] + float(ALONG_X[1, i]) * along_z[1])
    return out


def last_sweep(
    applied_ref, across_ref, within_ref, rhs_ref, inverse_ref, smooth_ref, update_ref, rows_ref,
    tree_ref, factor_ref, near_ref, table_ref,
    precond_ref, out_ref, send_ref,
):
    smooth, update = relax(
        2, 2, applied_ref, across_ref, within_ref, rhs_ref, inverse_ref, smooth_ref, update_ref
    )
    coarse = coarse_field(tree_ref, factor_ref, table_ref)
    precond = each(lambda s, c: s + c, smooth, coarse)
    write(precond_ref, precond)
    applied = element_apply(precond, 0, rows_ref, table_ref)
    write(out_ref, applied)
    first = jnp.zeros((8, 128), F32)
    second = jnp.zeros((8, 128), F32)
    for i in range(8):
        for z in range(2):
            first = first + near_rows(near_ref, i, z) * precond[i][z]
            second = second + applied[i][z] * precond[i][z]
    send_along_x(
        applied,
        jnp.sum(first, axis=1, keepdims=True),
        jnp.sum(second, axis=1, keepdims=True),
        send_ref,
    )


def middle(applied_ref, received_ref, summed_ref, send_ref):
    field = sum_x(read(applied_ref), *x_faces_received(received_ref))
    write(summed_ref, field)
    sums = received_ref[0, 0:8, :]
    for e in range(1, N_GX):
        sums = sums + received_ref[e, 0:8, :]
    send_along_z(field, sums, send_ref)


def finish(summed_ref, received_ref, precond_ref, rhs_ref, solution_ref, residual_ref):
    below, above = neighbours("gz", N_GZ, END_Z)
    field = sum_z(
        read(summed_ref),
        lambda i: received_ref[below, i : i + 1, :],
        lambda i: received_ref[above, i : i + 1, :],
    )
    image = each(wall, sum_y(field))
    sums = received_ref[0]
    for e in range(1, N_GZ):
        sums = sums + received_ref[e]
    sums = jnp.sum(sums, axis=0, keepdims=True)
    alpha = spread(sums[:, 0:1] / sums[:, 127:128])
    write(solution_ref, each(lambda p: alpha * p, read(precond_ref)))
    write(residual_ref, each(lambda r, a: r - alpha * a, read(rhs_ref, 2, 2), image))


def field_shape(count):
    return (8, count, 8, 128)


def run(kernel, shapes, *operands, first=False, last=False):
    spec = pl.BlockSpec(memory_space=pltpu.VMEM)
    outs = [
        jax.ShapeDtypeStruct(shape, F32) if last else pltpu.VMEM(shape, F32) for shape in shapes
    ]
    if not first:
        operands = [pltpu.with_memory_space_constraint(value, pltpu.VMEM) for value in operands]
    return pl.pallas_call(
        kernel, out_shape=outs, in_specs=[spec] * len(operands), out_specs=[spec] * len(outs)
    )(*operands)


def swap_z(value, distance, first=0):
    count = lax.axis_size("gz")
    pairs = [(i, (((i - first) % count ^ distance) + first) % count) for i in range(count)]
    return lax.ppermute(value, "gz", pairs)


def swap_x(across, within):
    count = lax.axis_size("gx")
    over = [(i, (((i - 1) % count) ^ 1) + 1) for i in range(count)]
    over = [(i, target % count) for i, target in over]
    inside = [(i, i ^ 1) for i in range(count)]
    return lax.ppermute(across, "gx", over), lax.ppermute(within, "gx", inside)


def send_chunks(chunks, axis, head):
    count = lax.axis_size(axis)
    group = [(head + k) % count for k in range(count)]
    return lax.all_to_all(chunks, axis, 0, 0, tiled=True, axis_index_groups=[group])


def send_pairs(pairs, axis, head):
    return send_chunks(pairs.reshape(-1, 2, 128), axis, head).reshape(pairs.shape)


def per_device(element_rhs_load, metric, coarse_factor):
    constants = jnp.asarray(TABLE)
    factor = coarse_factor.reshape(10, 32, 16).transpose(1, 0, 2).reshape(32, 160)
    factor = jnp.pad(factor, ((0, 0), (0, 96)))
    near, inner, outer = run(
        pack, [(136, 128), (80, 128), (80, 128)], element_rhs_load, metric, first=True
    )
    near_even, near_odd = swap_z(near, 1), swap_z(near, 1, 1)
    far_inner, far_outer = swap_z(inner, 2), swap_z(outer, 2, 2)
    (send,) = run(coarse_start, [(2 * N_GZ, 128)], near, factor, constants)
    tree = send_pairs(send, "gz", TREE_Z)
    wide, edge, rows, low, high = run(
        gather, [field_shape(8), (16, 128), (32, 128)] + [(Facross_refE_ROWS, 128)] * 2,
        near, near_even, near_odd, far_inner, far_outer, send,
    )
    left, right = swap_x(low, high)
    rhs, inverse, smooth, applied, low, high = run(
        begin, [field_shape(6)] * 3 + [field_shape(8)] + [(64, 128)] * 2,
        wide, edge, rows, left, right, constants,
    )
    left, right = swap_x(low, high)
    (send,) = run(lower_tree, [(2 * N_GX, 128)], tree)
    tree = send_pairs(send, "gx", TREE_X)
    update = smooth
    for step, count in ((0, 6), (1, 4)):

        def stage(*refs, step=step, count=count):
            sweep(*refs, step=step, count=count)

        smooth, update, applied, low, high = run(
            stage, [field_shape(count)] * 3 + [(8 * count, 128)] * 2,
            applied, left, right, rhs, inverse, smooth, update, rows, constants,
        )
        left, right = swap_x(low, high)
    precond, applied, send = run(
        last_sweep, [field_shape(2)] * 2 + [(N_GX, 16, 128)],
        applied, left, right, rhs, inverse, smooth, update, rows, tree, factor, near, constants,
    )
    received = send_chunks(send, "gx", END_X)
    summed, send = run(middle, [field_shape(2), (N_GZ, 8, 128)], applied, received)
    received = send_chunks(send, "gz", END_Z)
    solution_field, residual = run(
        finish, [field_shape(2)] * 2, summed, received, precond, rhs, last=True
    )
    shape = element_rhs_load.shape
    return solution_field.reshape(shape), residual.reshape(shape)


def solution(mesh):
    placed = (
        P("gx", None, "gz", None, None),
        P(None, "gx", "gz", None),
        P("gx", "gz", None, None, None),
    )
    return jax.shard_map(
        per_device,
        mesh=mesh,
        in_specs=placed,
        out_specs=(P("gx", None, "gz", None, None), P("gx", None, "gz", None, None)),
        check_vma=False,
    )
```

```python
import jax
import jax.numpy as jnp
import numpy as np
from jax import lax
from jax.experimental import pallas as pl
from jax.experimental.pallas import tpu as pltpu
from jax.sharding import PartitionSpec as P

CHEB = 4
N_GX = 32
N_GZ = 16
F32 = jnp.float32
HIGHEST = lax.Precision.HIGHEST
TREE_Z, TREE_X = 0, 7
END_Z, END_X = 9, 20

cheb_high = 2.0
cheb_low = 0.1
gll_inner = (
    -0.8717401485096066,
    -0.5917001814331423,
    -0.2092992179024789,
    0.2092992179024789,
    0.5917001814331423,
    0.8717401485096066,
)


def legendre_seven(points):
    before = np.ones(points.shape[0])
    current = points.copy()
    for degree in range(1, 7):
        following = ((2.0 * degree + 1.0) * points * current - degree * before) / (degree + 1.0)
        before = current
        current = following
    return current


def gll_tables():
    order = 7
    points = np.concatenate([[-1.0], np.array(gll_inner), [1.0]])
    values = legendre_seven(points)
    weights = 2.0 / (order * (order + 1) * values**2)
    count = order + 1
    deriv = np.zeros((count, count))
    for row_index in range(count):
        for col_index in range(count):
            if row_index != col_index:
                deriv[row_index, col_index] = values[row_index] / (
                    values[col_index] * (points[row_index] - points[col_index])
                )
    deriv[0, 0] = -order * (order + 1) / 4.0
    deriv[-1, -1] = order * (order + 1) / 4.0
    stiff = deriv.T @ (weights[:, None] * deriv)
    return (points, weights, stiff)


POINTS, WEIGHTS, STIFF = gll_tables()
KDIAG = np.diag(STIFF)
W = [float(v) for v in WEIGHTS]
KD = [float(v) for v in KDIAG]
K = [[float(v) for v in row] for row in STIFF]


def positions(count):
    return ((np.arange(count)[:, None] + (1.0 + POINTS[None, :]) / 2.0) / count).reshape(-1)


ALONG_X = np.stack([np.sin(np.pi * mode * positions(1)) for mode in (1, 2)])
ALONG_Z = np.stack([np.sin(np.pi * mode * positions(2)) for mode in (1, 2)])
ALONG_Y = np.stack([np.sin(np.pi * mode * positions(16)) for mode in range(1, 9)])


def build_tables():
    w_l = np.tile(WEIGHTS, 16)[None, :]
    k_l = np.tile(KDIAG, 16)[None, :]
    w_j = WEIGHTS[:, None]
    k_j = KDIAG[:, None]
    ones = np.ones((1, 128))
    pieces = {
        "stiff": np.kron(np.eye(16), STIFF),
        "ww": w_j * w_l,
        "kw": k_j * w_l,
        "wk": w_j * k_l,
        "wl": np.ones((8, 1)) * w_l,
        "wj": w_j * ones,
        "modes": np.tile(ALONG_Y, (4, 1)),
    }
    for b in range(2):
        for z in range(2):
            pieces[f"bz{b}{z}"] = ALONG_Z[b, 8 * z : 8 * z + 8, None] * ones
    offsets = {}
    rows = []
    start = 0
    for name, piece in pieces.items():
        offsets[name] = (start, start + piece.shape[0])
        rows.append(piece)
        start += piece.shape[0]
    return np.concatenate(rows).astype(np.float32), offsets


TABLE, OFFSETS = build_tables()


def chebyshev_steps():
    theta = 0.5 * (cheb_high + cheb_low)
    delta = 0.5 * (cheb_high - cheb_low)
    sigma = theta / delta
    rho = 1.0 / sigma
    steps = []
    for sweep in range(CHEB - 1):
        rho_next = 1.0 / (2.0 * sigma - rho)
        steps.append((rho_next * rho, 2.0 * rho_next / delta))
        rho = rho_next
    return theta, steps


THETA, STEPS = chebyshev_steps()


def table(table_ref, name):
    low, high = OFFSETS[name]
    return table_ref[low:high, :]


def lane_iota():
    return lax.broadcasted_iota(jnp.int32, (8, 128), 1)


def read(ref, first=0, count=2):
    return [[ref[i, c] for c in range(first, first + count)] for i in range(8)]


def write(ref, field):
    for i in range(8):
        for c, value in enumerate(field[i]):
            ref[i, c] = value


def spread(row):
    return jnp.broadcast_to(row, (8, 128))


def sum_x(field, left, right):
    out = [list(row) for row in field]
    for c in range(len(field[0])):
        out[0][c] = field[0][c] + left[c]
        out[7][c] = field[7][c] + right[c]
    return out


def sum_z(field, before=None, after=None):
    node = lax.broadcasted_iota(jnp.int32, (8, 128), 0)
    count = len(field[0])
    out = []
    for i in range(8):
        lows = [None] + [field[i][c][7:8, :] for c in range(count - 1)]
        highs = [field[i][c][0:1, :] for c in range(1, count)] + [None]
        if before is not None:
            lows[0], highs[-1] = before(i), after(i)
        out.append(
            [
                field[i][c]
                + jnp.where(node == 0, spread(lows[c]), jnp.where(node == 7, spread(highs[c]), 0.0))
                for c in range(count)
                if lows[c] is not None and highs[c] is not None
            ]
        )
    return out


def sum_y(field):
    lane = lane_iota()
    first = ((lane & 7) == 0) & (lane > 0)
    last = ((lane & 7) == 7) & (lane < 127)
    return each(
        lambda value: value
        + jnp.where(last, pltpu.roll(value, 127, 1), jnp.where(first, pltpu.roll(value, 1, 1), 0.0)),
        field,
    )


def wall(value):
    lane = lane_iota()
    return jnp.where((lane == 0) | (lane == 127), 0.0, value)


def each(function, *fields):
    return [[function(*values) for values in zip(*rows)] for rows in zip(*fields)]


ROWS = 10


def metric_row(ref, base, m, column):
    row = base + ROWS * m + 4 + column
    return ref[row : row + 1, :]


def element_apply(field, first, metric_ref, table_ref):
    count = len(field[0])
    stiff = table(table_ref, "stiff")
    out = [[None] * count for i in range(8)]
    columns = [jnp.concatenate([field[i][c] for i in range(8)], axis=0) for c in range(count)]
    along_y = jnp.dot(
        jnp.concatenate(columns, axis=0), stiff, precision=HIGHEST, preferred_element_type=F32
    )
    for c in range(count):
        stacked = columns[c]
        along_l = along_y[64 * c : 64 * c + 64, :]
        along_j = jnp.dot(
            stiff[0:64, 0:64], stacked, precision=HIGHEST, preferred_element_type=F32
        )
        rows = [spread(metric_row(metric_ref, 0, m, first + c)) for m in range(3)]
        scale_x = rows[0] * table(table_ref, "ww")
        scale_z = rows[1] * table(table_ref, "wl")
        scale_y = rows[2] * table(table_ref, "wj")
        for p in range(8):
            along_i = K[0][p] * field[0][c]
            for i in range(1, 8):
                along_i = along_i + K[i][p] * field[i][c]
            out[p][c] = scale_x * along_i + W[p] * (
                scale_z * along_j[8 * p : 8 * p + 8, :] + scale_y * along_l[8 * p : 8 * p + 8, :]
            )
    return out


def diagonal_parts(ref, base, column, table_ref):
    part_x = spread(metric_row(ref, base, 0, column)) * table(table_ref, "ww")
    part_rest = spread(metric_row(ref, base, 1, column)) * table(table_ref, "kw") + spread(
        metric_row(ref, base, 2, column)
    ) * table(table_ref, "wk")
    return part_x, part_rest


def diagonal_sum_x(rows_ref, left_ref, right_ref, column, table_ref):
    part_x, part_rest = diagonal_parts(rows_ref, 0, column, table_ref)
    out = []
    for i in range(8):
        sum_of_x, sum_of_rest = part_x, part_rest
        if i in (0, 7):
            side = left_ref if i == 0 else right_ref
            side_x, side_rest = diagonal_parts(side, FACE_METRIC, column, table_ref)
            sum_of_x, sum_of_rest = part_x + side_x, part_rest + side_rest
        out.append(KD[i] * sum_of_x + W[i] * sum_of_rest)
    return out


class Faces:
    def __init__(self, across_ref, within_ref):
        self.odd = lax.rem(lax.axis_index("gx"), 2) == 1
        self.across, self.within = across_ref, within_ref

    def put(self, first, last, low, high):
        self.across[first:last, :] = jnp.where(self.odd, high, low)
        self.within[first:last, :] = jnp.where(self.odd, low, high)


class Either:
    def __init__(self, first, first_ref, second_ref):
        self.first, self.first_ref, self.second_ref = first, first_ref, second_ref

    def __getitem__(self, where):
        return jnp.where(self.first, self.first_ref[where], self.second_ref[where])


class Side:
    def __init__(self, across_ref, within_ref, right):
        odd = lax.rem(lax.axis_index("gx"), 2) == 1
        self.across = odd if right else jnp.logical_not(odd)
        self.across_ref, self.within_ref = across_ref, within_ref

    def __getitem__(self, where):
        return jnp.where(self.across, self.across_ref[where], self.within_ref[where])


def sides(across_ref, within_ref):
    return Side(across_ref, within_ref, False), Side(across_ref, within_ref, True)


def write_x_faces(field, across_ref, within_ref):
    out = Faces(across_ref, within_ref)
    for c in range(len(field[0])):
        out.put(8 * c, 8 * c + 8, field[0][c], field[7][c])


def faces(ref, count):
    return [ref[8 * c : 8 * c + 8, :] for c in range(count)]


def pack(load_ref, metric_ref, near_ref, inner_ref, outer_ref):
    begins = lax.rem(lax.axis_index("gz"), 4) < 2
    element = lax.broadcasted_iota(jnp.int32, (16, 128), 0)
    lane = lax.broadcasted_iota(jnp.int32, (16, 128), 1)
    expand = jnp.where(element == (lane >> 3), 1.0, 0.0)
    for ref, start in ((near_ref, 128), (inner_ref, 72), (outer_ref, 72)):
        ref[start + 6 : start + 8, :] = jnp.zeros((2, 128), F32)
    for m in range(3):
        expanded = jnp.dot(
            metric_ref[m, 0], expand, precision=HIGHEST, preferred_element_type=F32
        )
        for ref, start in ((near_ref, 128), (inner_ref, 72), (outer_ref, 72)):
            ref[start + 2 * m : start + 2 * m + 2, :] = expanded
    for i in range(8):
        for z in range(2):
            near_ref[8 * (2 * i + z) : 8 * (2 * i + z) + 8, :] = load_ref[0, i, z]
        rows = slice(8 * i, 8 * i + 8)
        inner_ref[rows, :] = jnp.where(begins, load_ref[0, i, 1], load_ref[0, i, 0])
        outer_ref[rows, :] = jnp.where(begins, load_ref[0, i, 0], load_ref[0, i, 1])
        up, down = load_ref[0, i, 0, 7:8, :], load_ref[0, i, 1, 0:1, :]
        inner_ref[64 + i : 65 + i, :] = jnp.where(begins, up, down)
        outer_ref[64 + i : 65 + i, :] = jnp.where(begins, down, up)


FACE_METRIC = 72
FACE_ROWS = 104


def neighbours_z(even_ref, odd_ref, inner_ref, outer_ref):
    place = lax.axis_index("gz")
    return (
        Either(lax.rem(place, 4) >= 2, inner_ref, outer_ref),
        Either(lax.rem(place, 2) == 1, even_ref, odd_ref),
        Either(lax.rem(place, 2) == 0, even_ref, odd_ref),
        Either(lax.rem(place, 4) < 2, inner_ref, outer_ref),
    )


def wide_load(near_ref, far_below_ref, below_ref, above_ref, far_above_ref, i):
    far = slice(8 * i, 8 * i + 8)
    pair = [slice(8 * (2 * i + z), 8 * (2 * i + z) + 8) for z in range(2)]
    return (
        [far_below_ref[far, :]]
        + [ref[rows, :] for ref in (below_ref, near_ref, above_ref) for rows in pair]
        + [far_above_ref[far, :]]
    )


def gather(
    near_ref, even_ref, odd_ref, inner_ref, outer_ref, earlier_ref, rows_ref, across_ref, within_ref
):
    messages = neighbours_z(even_ref, odd_ref, inner_ref, outer_ref)
    far_below_ref, below_ref, above_ref, far_above_ref = messages
    sources = (
        (far_below_ref, 72), (below_ref, 128), (near_ref, 128), (above_ref, 128), (far_above_ref, 72),
    )
    for index, (source, start) in enumerate(sources):
        for m in range(3):
            row = ROWS * m + 2 * index
            rows_ref[row : row + 2, :] = source[start + 2 * m : start + 2 * m + 2, :]
    rows_ref[30:32, :] = jnp.zeros((2, 128), F32)
    rows = rows_ref[...]
    out = Faces(across_ref, within_ref)
    lows, highs = wide_load(near_ref, *messages, 0), wide_load(near_ref, *messages, 7)
    for c in range(8):
        out.put(8 * c, 8 * c + 8, lows[c], highs[c])
    for row, ref in ((64, far_below_ref), (65, far_above_ref)):
        out.put(row, row + 1, ref[64:65, :], ref[71:72, :])
    for ref in (across_ref, within_ref):
        ref[66:72, :] = jnp.zeros((6, 128), F32)
        ref[FACE_METRIC:FACE_ROWS, :] = rows


def with_sums(face, first, second):
    lane = lane_iota()
    return jnp.where(lane == 0, first, jnp.where(lane == 127, second, face))


def send_along_x(field, first, second, send_ref):
    here = lax.axis_index("gx")
    above = lax.rem(here + 1, N_GX)
    low = [with_sums(field[0][0], first, second), field[0][1]]
    high = [with_sums(field[7][0], first, second), field[7][1]]
    for chunk in range(N_GX):
        for z in range(2):
            send_ref[chunk, 8 * z : 8 * z + 8, :] = jnp.where(
                above == (chunk + END_X) % N_GX, high[z], low[z]
            )


def send_along_z(field, sums, send_ref):
    here = lax.axis_index("gz")
    above = lax.rem(here + 1, N_GZ)
    node = lax.broadcasted_iota(jnp.int32, (8, 128), 0)
    low = high = jnp.zeros((8, 128), F32)
    for i in range(8):
        low = jnp.where(node == i, spread(field[i][0][0:1, :]), low)
        high = jnp.where(node == i, spread(field[i][1][7:8, :]), high)
    low, high = with_sums(low, sums, sums), with_sums(high, sums, sums)
    for chunk in range(N_GZ):
        send_ref[chunk] = jnp.where(above == (chunk + END_Z) % N_GZ, high, low)


def near_rows(near_ref, i, z):
    start = 8 * (2 * i + z)
    return near_ref[start : start + 8, :]


def coarse_start(near_ref, factor_ref, table_ref, send_ref):
    parts = []
    load = [[wall(near_rows(near_ref, i, z)) for z in range(2)] for i in range(8)]
    for a in range(2):
        along_x = []
        for z in range(2):
            total = float(ALONG_X[a, 0]) * load[0][z]
            for i in range(1, 8):
                total = total + float(ALONG_X[a, i]) * load[i][z]
            along_x.append(total)
        for b in range(2):
            both = (
                table(table_ref, f"bz{b}0") * along_x[0] + table(table_ref, f"bz{b}1") * along_x[1]
            )
            parts.append(jnp.sum(both, axis=0, keepdims=True))
    node = lax.broadcasted_iota(jnp.int32, (8, 128), 0)
    stacked = jnp.zeros((8, 128), F32)
    for index, part in enumerate(parts):
        stacked = jnp.where(node == index, spread(part), stacked)
    modes = lax.dot_general(
        stacked, table(table_ref, "modes"), (((1,), (1,)), ((), ())),
        precision=HIGHEST, preferred_element_type=F32,
    )
    owner = lax.broadcasted_iota(jnp.int32, (8, 32), 1) >> 3
    row = lax.broadcasted_iota(jnp.int32, (8, 32), 0)
    coarse_rhs = jnp.sum(jnp.where(owner == row, modes, 0.0), axis=0, keepdims=True)
    own = jnp.dot(
        jnp.broadcast_to(coarse_rhs, (8, 32)), factor_ref[...],
        precision=HIGHEST, preferred_element_type=F32,
    )
    write_pairs(send_ref, own[0:1, 0:128], own[0:1, 128:256])


def begin(
    near_ref, even_ref, odd_ref, inner_ref, outer_ref, rows_ref, across_ref, within_ref, table_ref,
    rhs_ref, inverse_ref, smooth_ref, applied_ref, across_out, within_out,
):
    left_ref, right_ref = sides(across_ref, within_ref)

    messages = neighbours_z(even_ref, odd_ref, inner_ref, outer_ref)

    def edge(which):
        def row(i):
            value = messages[3 * which][64 + i : 65 + i, :]
            if i == 0:
                value = value + left_ref[64 + which : 65 + which, :]
            if i == 7:
                value = value + right_ref[64 + which : 65 + which, :]
            return value

        return row

    load = [wide_load(near_ref, *messages, i) for i in range(8)]
    load = sum_x(load, faces(left_ref, 8), faces(right_ref, 8))
    rhs = each(wall, sum_y(sum_z(load, edge(0), edge(1))))
    columns = [
        diagonal_sum_x(rows_ref, left_ref, right_ref, column, table_ref) for column in range(-4, 6)
    ]
    diagonal = sum_z([[columns[c][i] for c in range(10)] for i in range(8)])
    inverse = each(lambda d: wall(1.0 / d), sum_y(diagonal))
    smooth = each(lambda d, r: d * r / THETA, inverse, rhs)
    write(rhs_ref, [row[1:7] for row in rhs])
    write(inverse_ref, [row[1:7] for row in inverse])
    write(smooth_ref, [row[1:7] for row in smooth])
    applied = element_apply(smooth, -3, rows_ref, table_ref)
    write(applied_ref, applied)
    write_x_faces(applied, across_out, within_out)


def write_pairs(ref, first, second):
    row = lax.broadcasted_iota(jnp.int32, (8, 128), 0)
    pairs = jnp.where((row & 1) == 0, spread(first), spread(second))
    for start in range(0, ref.shape[0], 8):
        ref[start : start + 8, :] = pairs


def tree_sums(ref, here, skipped, head):
    row = lax.broadcasted_iota(jnp.int32, (8, 128), 0)
    level = (row & 1) * 8 + (lane_iota() >> 4)
    shift = jnp.maximum(level - skipped, 0)
    mine = lax.shift_right_logical(jnp.full((8, 128), here, jnp.int32), shift)
    total = jnp.zeros((8, 128), F32)
    for start in range(0, ref.shape[0], 8):
        device = (head + start // 2 + (row >> 1)) & (ref.shape[0] // 2 - 1)
        other = lax.shift_right_logical(device, shift)
        total = total + jnp.where(other == mine, ref[start : start + 8, :], 0.0)
    first = jnp.sum(jnp.where((row & 1) == 0, total, 0.0), axis=0, keepdims=True)
    second = jnp.sum(jnp.where((row & 1) == 1, total, 0.0), axis=0, keepdims=True)
    return first, second


def neighbours(axis, count, head):
    here = lax.axis_index(axis) + count - head
    return lax.rem(here + count - 1, count), lax.rem(here + 1, count)


def lower_tree(received_ref, send_ref):
    write_pairs(send_ref, *tree_sums(received_ref, lax.axis_index("gz"), 0, TREE_Z))


def x_faces_received(received_ref):
    below, above = neighbours("gx", N_GX, END_X)
    left = [received_ref[below, 8 * z : 8 * z + 8, :] for z in range(2)]
    right = [received_ref[above, 8 * z : 8 * z + 8, :] for z in range(2)]
    return left, right


def relax(step, count, applied_ref, across_ref, within_ref, rhs_ref, inverse_ref, smooth_ref, update_ref):
    left_ref, right_ref = sides(across_ref, within_ref)
    field = sum_x(
        read(applied_ref, 0, count + 2), faces(left_ref, count + 2), faces(right_ref, count + 2)
    )
    image = each(wall, sum_y(sum_z(field)))
    first, second = STEPS[step]
    inset = (6 - count) // 2
    shift = 1 if step else 0
    update = each(
        lambda u, d, r, a: first * u + (second * d) * (r - a),
        read(update_ref, shift, count), read(inverse_ref, inset, count), read(rhs_ref, inset, count),
        image,
    )
    return each(lambda s, u: s + u, read(smooth_ref, shift, count), update), update


def sweep(
    applied_ref, across_ref, within_ref, rhs_ref, inverse_ref, smooth_ref, update_ref, rows_ref, table_ref,
    next_ref, next_update_ref, out_ref, low_ref, high_ref, *, step, count,
):
    smooth, update = relax(
        step, count, applied_ref, across_ref, within_ref, rhs_ref, inverse_ref, smooth_ref, update_ref
    )
    write(next_ref, smooth)
    write(next_update_ref, update)
    applied = element_apply(smooth, 1 - count // 2, rows_ref, table_ref)
    write(out_ref, applied)
    write_x_faces(applied, low_ref, high_ref)


def coarse_field(received_ref, factor_ref, table_ref):
    first, second = tree_sums(received_ref, lax.axis_index("gx"), 4, TREE_X)
    columns = jnp.broadcast_to(jnp.concatenate([first, second], axis=1), (8, 256))
    coarse = lax.dot_general(
        columns, factor_ref[...], (((1,), (1,)), ((), ())),
        precision=HIGHEST, preferred_element_type=F32,
    )
    owner = lax.broadcasted_iota(jnp.int32, (8, 32), 1) >> 3
    row = lax.broadcasted_iota(jnp.int32, (8, 32), 0)
    across = jnp.dot(
        jnp.where(owner == row, coarse, 0.0), table(table_ref, "modes"),
        precision=HIGHEST, preferred_element_type=F32,
    )
    out = [[None, None] for i in range(8)]
    for z in range(2):
        along_z = []
        for a in range(2):
            along_z.append(
                table(table_ref, f"bz0{z}") * spread(across[2 * a : 2 * a + 1, :])
                + table(table_ref, f"bz1{z}") * spread(across[2 * a + 1 : 2 * a + 2, :])
            )
        for i in range(8):
            out[i][z] = wall(float(ALONG_X[0, i]) * along_z[0] + float(ALONG_X[1, i]) * along_z[1])
    return out


def last_sweep(
    applied_ref, across_ref, within_ref, rhs_ref, inverse_ref, smooth_ref, update_ref, rows_ref,
    tree_ref, factor_ref, near_ref, table_ref,
    precond_ref, out_ref, send_ref,
):
    smooth, update = relax(
        2, 2, applied_ref, across_ref, within_ref, rhs_ref, inverse_ref, smooth_ref, update_ref
    )
    coarse = coarse_field(tree_ref, factor_ref, table_ref)
    precond = each(lambda s, c: s + c, smooth, coarse)
    write(precond_ref, precond)
    applied = element_apply(precond, 0, rows_ref, table_ref)
    write(out_ref, applied)
    first = jnp.zeros((8, 128), F32)
    second = jnp.zeros((8, 128), F32)
    for i in range(8):
        for z in range(2):
            first = first + near_rows(near_ref, i, z) * precond[i][z]
            second = second + applied[i][z] * precond[i][z]
    send_along_x(
        applied,
        jnp.sum(first, axis=1, keepdims=True),
        jnp.sum(second, axis=1, keepdims=True),
        send_ref,
    )


def middle(applied_ref, received_ref, summed_ref, send_ref):
    field = sum_x(read(applied_ref), *x_faces_received(received_ref))
    write(summed_ref, field)
    sums = received_ref[0, 0:8, :]
    for e in range(1, N_GX):
        sums = sums + received_ref[e, 0:8, :]
    send_along_z(field, sums, send_ref)


def finish(summed_ref, received_ref, precond_ref, rhs_ref, solution_ref, residual_ref):
    below, above = neighbours("gz", N_GZ, END_Z)
    field = sum_z(
        read(summed_ref),
        lambda i: received_ref[below, i : i + 1, :],
        lambda i: received_ref[above, i : i + 1, :],
    )
    image = each(wall, sum_y(field))
    sums = received_ref[0]
    for e in range(1, N_GZ):
        sums = sums + received_ref[e]
    sums = jnp.sum(sums, axis=0, keepdims=True)
    alpha = spread(sums[:, 0:1] / sums[:, 127:128])
    write(solution_ref, each(lambda p: alpha * p, read(precond_ref)))
    write(residual_ref, each(lambda r, a: r - alpha * a, read(rhs_ref, 2, 2), image))


def field_shape(count):
    return (8, count, 8, 128)


def run(kernel, shapes, *operands, first=False, last=False, after=None):
    spec = pl.BlockSpec(memory_space=pltpu.VMEM)
    outs = [
        jax.ShapeDtypeStruct(shape, F32) if last else pltpu.VMEM(shape, F32) for shape in shapes
    ]
    if not first:
        operands = [pltpu.with_memory_space_constraint(value, pltpu.VMEM) for value in operands]
    specs = [spec] * len(operands)
    if after is not None:
        operands, specs = [*operands, after], [*specs, pl.BlockSpec(memory_space=pl.ANY)]
    return pl.pallas_call(
        kernel, out_shape=outs, in_specs=specs, out_specs=[spec] * len(outs)
    )(*operands)


def swap_z(value, distance, first=0):
    count = lax.axis_size("gz")
    pairs = [(i, (((i - first) % count ^ distance) + first) % count) for i in range(count)]
    return lax.ppermute(value, "gz", pairs)


def swap_x(across, within):
    count = lax.axis_size("gx")
    over = [(i, (((i - 1) % count) ^ 1) + 1) for i in range(count)]
    over = [(i, target % count) for i, target in over]
    inside = [(i, i ^ 1) for i in range(count)]
    return lax.ppermute(across, "gx", over), lax.ppermute(within, "gx", inside)


def send_chunks(chunks, axis, head):
    count = lax.axis_size(axis)
    group = [(head + k) % count for k in range(count)]
    return lax.all_to_all(chunks, axis, 0, 0, tiled=True, axis_index_groups=[group])


def send_pairs(pairs, axis, head):
    return send_chunks(pairs.reshape(-1, 2, 128), axis, head).reshape(pairs.shape)


def per_device(element_rhs_load, metric, coarse_factor):
    constants = jnp.asarray(TABLE)
    factor = coarse_factor.reshape(10, 32, 16).transpose(1, 0, 2).reshape(32, 160)
    factor = jnp.pad(factor, ((0, 0), (0, 96)))
    near, inner, outer = run(
        pack, [(136, 128), (80, 128), (80, 128)], element_rhs_load, metric, first=True
    )
    near_even, near_odd = swap_z(near, 1), swap_z(near, 1, 1)
    far_inner, far_outer = swap_z(inner, 2), swap_z(outer, 2, 2)
    (send,) = run(coarse_start, [(2 * N_GZ, 128)], near, factor, constants)
    tree = send_pairs(send, "gz", TREE_Z)
    rows, low, high = run(
        gather, [(32, 128)] + [(FACE_ROWS, 128)] * 2,
        near, near_even, near_odd, far_inner, far_outer, after=send,
    )
    left, right = swap_x(low, high)
    rhs, inverse, smooth, applied, low, high = run(
        begin, [field_shape(6)] * 3 + [field_shape(8)] + [(64, 128)] * 2,
        near, near_even, near_odd, far_inner, far_outer, rows, left, right, constants,
    )
    left, right = swap_x(low, high)
    (send,) = run(lower_tree, [(2 * N_GX, 128)], tree)
    tree = send_pairs(send, "gx", TREE_X)
    update = smooth
    for step, count in ((0, 6), (1, 4)):

        def stage(*refs, step=step, count=count):
            sweep(*refs, step=step, count=count)

        smooth, update, applied, low, high = run(
            stage, [field_shape(count)] * 3 + [(8 * count, 128)] * 2,
            applied, left, right, rhs, inverse, smooth, update, rows, constants,
        )
        left, right = swap_x(low, high)
    precond, applied, send = run(
        last_sweep, [field_shape(2)] * 2 + [(N_GX, 16, 128)],
        applied, left, right, rhs, inverse, smooth, update, rows, tree, factor, near, constants,
    )
    received = send_chunks(send, "gx", END_X)
    summed, send = run(middle, [field_shape(2), (N_GZ, 8, 128)], applied, received)
    received = send_chunks(send, "gz", END_Z)
    solution_field, residual = run(
        finish, [field_shape(2)] * 2, summed, received, precond, rhs, last=True
    )
    shape = element_rhs_load.shape
    return solution_field.reshape(shape), residual.reshape(shape)


def solution(mesh):
    placed = (
        P("gx", None, "gz", None, None),
        P(None, "gx", "gz", None),
        P("gx", "gz", None, None, None),
    )
    return jax.shard_map(
        per_device,
        mesh=mesh,
        in_specs=placed,
        out_specs=(P("gx", None, "gz", None, None), P("gx", None, "gz", None, None)),
        check_vma=False,
    )
```

```python
import jax
import jax.numpy as jnp
import numpy as np
from jax import lax
from jax.experimental import pallas as pl
from jax.experimental.pallas import tpu as pltpu
from jax.sharding import PartitionSpec as P

CHEB = 4
N_GX = 32
N_GZ = 16
F32 = jnp.float32
HIGHEST = lax.Precision.HIGHEST
TREE_Z, TREE_X = 0, 7
END_Z, END_X = 9, 20

cheb_high = 2.0
cheb_low = 0.1
gll_inner = (
    -0.8717401485096066,
    -0.5917001814331423,
    -0.2092992179024789,
    0.2092992179024789,
    0.5917001814331423,
    0.8717401485096066,
)


def legendre_seven(points):
    before = np.ones(points.shape[0])
    current = points.copy()
    for degree in range(1, 7):
        following = ((2.0 * degree + 1.0) * points * current - degree * before) / (degree + 1.0)
        before = current
        current = following
    return current


def gll_tables():
    order = 7
    points = np.concatenate([[-1.0], np.array(gll_inner), [1.0]])
    values = legendre_seven(points)
    weights = 2.0 / (order * (order + 1) * values**2)
    count = order + 1
    deriv = np.zeros((count, count))
    for row_index in range(count):
        for col_index in range(count):
            if row_index != col_index:
                deriv[row_index, col_index] = values[row_index] / (
                    values[col_index] * (points[row_index] - points[col_index])
                )
    deriv[0, 0] = -order * (order + 1) / 4.0
    deriv[-1, -1] = order * (order + 1) / 4.0
    stiff = deriv.T @ (weights[:, None] * deriv)
    return (points, weights, stiff)


POINTS, WEIGHTS, STIFF = gll_tables()
KDIAG = np.diag(STIFF)
W = [float(v) for v in WEIGHTS]
KD = [float(v) for v in KDIAG]
K = [[float(v) for v in row] for row in STIFF]


def positions(count):
    return ((np.arange(count)[:, None] + (1.0 + POINTS[None, :]) / 2.0) / count).reshape(-1)


ALONG_X = np.stack([np.sin(np.pi * mode * positions(1)) for mode in (1, 2)])
ALONG_Z = np.stack([np.sin(np.pi * mode * positions(2)) for mode in (1, 2)])
ALONG_Y = np.stack([np.sin(np.pi * mode * positions(16)) for mode in range(1, 9)])


def build_tables():
    w_l = np.tile(WEIGHTS, 16)[None, :]
    k_l = np.tile(KDIAG, 16)[None, :]
    w_j = WEIGHTS[:, None]
    k_j = KDIAG[:, None]
    ones = np.ones((1, 128))
    pieces = {
        "stiff": np.kron(np.eye(16), STIFF),
        "ww": w_j * w_l,
        "kw": k_j * w_l,
        "wk": w_j * k_l,
        "wl": np.ones((8, 1)) * w_l,
        "wj": w_j * ones,
        "modes": np.tile(ALONG_Y, (4, 1)),
    }
    for b in range(2):
        for z in range(2):
            pieces[f"bz{b}{z}"] = ALONG_Z[b, 8 * z : 8 * z + 8, None] * ones
    offsets = {}
    rows = []
    start = 0
    for name, piece in pieces.items():
        offsets[name] = (start, start + piece.shape[0])
        rows.append(piece)
        start += piece.shape[0]
    return np.concatenate(rows).astype(np.float32), offsets


TABLE, OFFSETS = build_tables()


def chebyshev_steps():
    theta = 0.5 * (cheb_high + cheb_low)
    delta = 0.5 * (cheb_high - cheb_low)
    sigma = theta / delta
    rho = 1.0 / sigma
    steps = []
    for sweep in range(CHEB - 1):
        rho_next = 1.0 / (2.0 * sigma - rho)
        steps.append((rho_next * rho, 2.0 * rho_next / delta))
        rho = rho_next
    return theta, steps


THETA, STEPS = chebyshev_steps()


def table(table_ref, name):
    low, high = OFFSETS[name]
    return table_ref[low:high, :]


def lane_iota():
    return lax.broadcasted_iota(jnp.int32, (8, 128), 1)


def read(ref, first=0, count=2):
    return [[ref[i, c] for c in range(first, first + count)] for i in range(8)]


def write(ref, field):
    for i in range(8):
        for c, value in enumerate(field[i]):
            ref[i, c] = value


def spread(row):
    return jnp.broadcast_to(row, (8, 128))


def sum_x(field, left, right):
    out = [list(row) for row in field]
    for c in range(len(field[0])):
        out[0][c] = field[0][c] + left[c]
        out[7][c] = field[7][c] + right[c]
    return out


def sum_z(field, before=None, after=None):
    node = lax.broadcasted_iota(jnp.int32, (8, 128), 0)
    count = len(field[0])
    out = []
    for i in range(8):
        lows = [None] + [field[i][c][7:8, :] for c in range(count - 1)]
        highs = [field[i][c][0:1, :] for c in range(1, count)] + [None]
        if before is not None:
            lows[0], highs[-1] = before(i), after(i)
        out.append(
            [
                field[i][c]
                + jnp.where(node == 0, spread(lows[c]), jnp.where(node == 7, spread(highs[c]), 0.0))
                for c in range(count)
                if lows[c] is not None and highs[c] is not None
            ]
        )
    return out


def sum_y(field):
    lane = lane_iota()
    first = ((lane & 7) == 0) & (lane > 0)
    last = ((lane & 7) == 7) & (lane < 127)
    return each(
        lambda value: value
        + jnp.where(last, pltpu.roll(value, 127, 1), jnp.where(first, pltpu.roll(value, 1, 1), 0.0)),
        field,
    )


def wall(value):
    lane = lane_iota()
    return jnp.where((lane == 0) | (lane == 127), 0.0, value)


def each(function, *fields):
    return [[function(*values) for values in zip(*rows)] for rows in zip(*fields)]


ROWS = 10


def metric_row(ref, base, m, column):
    row = base + ROWS * m + 4 + column
    return ref[row : row + 1, :]


def element_apply(field, first, metric_ref, table_ref):
    count = len(field[0])
    stiff = table(table_ref, "stiff")
    out = [[None] * count for i in range(8)]
    columns = [jnp.concatenate([field[i][c] for i in range(8)], axis=0) for c in range(count)]
    along_y = jnp.dot(
        jnp.concatenate(columns, axis=0), stiff, precision=HIGHEST, preferred_element_type=F32
    )
    for c in range(count):
        stacked = columns[c]
        along_l = along_y[64 * c : 64 * c + 64, :]
        along_j = jnp.dot(
            stiff[0:64, 0:64], stacked, precision=HIGHEST, preferred_element_type=F32
        )
        rows = [spread(metric_row(metric_ref, 0, m, first + c)) for m in range(3)]
        scale_x = rows[0] * table(table_ref, "ww")
        scale_z = rows[1] * table(table_ref, "wl")
        scale_y = rows[2] * table(table_ref, "wj")
        for p in range(8):
            along_i = K[0][p] * field[0][c]
            for i in range(1, 8):
                along_i = along_i + K[i][p] * field[i][c]
            out[p][c] = scale_x * along_i + W[p] * (
                scale_z * along_j[8 * p : 8 * p + 8, :] + scale_y * along_l[8 * p : 8 * p + 8, :]
            )
    return out


def diagonal_parts(ref, base, column, table_ref):
    part_x = spread(metric_row(ref, base, 0, column)) * table(table_ref, "ww")
    part_rest = spread(metric_row(ref, base, 1, column)) * table(table_ref, "kw") + spread(
        metric_row(ref, base, 2, column)
    ) * table(table_ref, "wk")
    return part_x, part_rest


def diagonal_sum_x(rows_ref, left_ref, right_ref, column, table_ref):
    part_x, part_rest = diagonal_parts(rows_ref, 0, column, table_ref)
    out = []
    for i in range(8):
        sum_of_x, sum_of_rest = part_x, part_rest
        if i in (0, 7):
            side = left_ref if i == 0 else right_ref
            side_x, side_rest = diagonal_parts(side, FACE_METRIC, column, table_ref)
            sum_of_x, sum_of_rest = part_x + side_x, part_rest + side_rest
        out.append(KD[i] * sum_of_x + W[i] * sum_of_rest)
    return out


class Faces:
    def __init__(self, across_ref, within_ref):
        self.odd = lax.rem(lax.axis_index("gx"), 2) == 1
        self.across, self.within = across_ref, within_ref

    def put(self, first, last, low, high):
        self.across[first:last, :] = jnp.where(self.odd, high, low)
        self.within[first:last, :] = jnp.where(self.odd, low, high)


class Either:
    def __init__(self, first, first_ref, second_ref):
        self.first, self.first_ref, self.second_ref = first, first_ref, second_ref

    def __getitem__(self, where):
        return jnp.where(self.first, self.first_ref[where], self.second_ref[where])


class Side:
    def __init__(self, across_ref, within_ref, right):
        odd = lax.rem(lax.axis_index("gx"), 2) == 1
        self.across = odd if right else jnp.logical_not(odd)
        self.across_ref, self.within_ref = across_ref, within_ref

    def __getitem__(self, where):
        return jnp.where(self.across, self.across_ref[where], self.within_ref[where])


def sides(across_ref, within_ref):
    return Side(across_ref, within_ref, False), Side(across_ref, within_ref, True)


def write_x_faces(field, across_ref, within_ref):
    out = Faces(across_ref, within_ref)
    for c in range(len(field[0])):
        out.put(8 * c, 8 * c + 8, field[0][c], field[7][c])


def faces(ref, count):
    return [ref[8 * c : 8 * c + 8, :] for c in range(count)]


def pack(load_ref, metric_ref, near_ref, inner_ref, outer_ref):
    begins = lax.rem(lax.axis_index("gz"), 4) < 2
    element = lax.broadcasted_iota(jnp.int32, (16, 128), 0)
    lane = lax.broadcasted_iota(jnp.int32, (16, 128), 1)
    expand = jnp.where(element == (lane >> 3), 1.0, 0.0)
    for ref, start in ((near_ref, 128), (inner_ref, 72), (outer_ref, 72)):
        ref[start + 6 : start + 8, :] = jnp.zeros((2, 128), F32)
    stacked = jnp.concatenate([metric_ref[m, 0] for m in range(3)], axis=0)
    expanded = jnp.dot(stacked, expand, precision=HIGHEST, preferred_element_type=F32)
    for ref, start in ((near_ref, 128), (inner_ref, 72), (outer_ref, 72)):
        ref[start : start + 6, :] = expanded
    for i in range(8):
        for z in range(2):
            near_ref[8 * (2 * i + z) : 8 * (2 * i + z) + 8, :] = load_ref[0, i, z]
        rows = slice(8 * i, 8 * i + 8)
        inner_ref[rows, :] = jnp.where(begins, load_ref[0, i, 1], load_ref[0, i, 0])
        outer_ref[rows, :] = jnp.where(begins, load_ref[0, i, 0], load_ref[0, i, 1])
        up, down = load_ref[0, i, 0, 7:8, :], load_ref[0, i, 1, 0:1, :]
        inner_ref[64 + i : 65 + i, :] = jnp.where(begins, up, down)
        outer_ref[64 + i : 65 + i, :] = jnp.where(begins, down, up)


FACE_METRIC = 72
FACE_ROWS = 104


def neighbours_z(even_ref, odd_ref, inner_ref, outer_ref):
    place = lax.axis_index("gz")
    return (
        Either(lax.rem(place, 4) >= 2, inner_ref, outer_ref),
        Either(lax.rem(place, 2) == 1, even_ref, odd_ref),
        Either(lax.rem(place, 2) == 0, even_ref, odd_ref),
        Either(lax.rem(place, 4) < 2, inner_ref, outer_ref),
    )


def wide_load(near_ref, far_below_ref, below_ref, above_ref, far_above_ref, i):
    far = slice(8 * i, 8 * i + 8)
    pair = [slice(8 * (2 * i + z), 8 * (2 * i + z) + 8) for z in range(2)]
    return (
        [far_below_ref[far, :]]
        + [ref[rows, :] for ref in (below_ref, near_ref, above_ref) for rows in pair]
        + [far_above_ref[far, :]]
    )


def gather(
    near_ref, even_ref, odd_ref, inner_ref, outer_ref, earlier_ref, rows_ref, across_ref, within_ref
):
    messages = neighbours_z(even_ref, odd_ref, inner_ref, outer_ref)
    far_below_ref, below_ref, above_ref, far_above_ref = messages
    sources = (
        (far_below_ref, 72), (below_ref, 128), (near_ref, 128), (above_ref, 128), (far_above_ref, 72),
    )
    for index, (source, start) in enumerate(sources):
        for m in range(3):
            row = ROWS * m + 2 * index
            rows_ref[row : row + 2, :] = source[start + 2 * m : start + 2 * m + 2, :]
    rows_ref[30:32, :] = jnp.zeros((2, 128), F32)
    rows = rows_ref[...]
    out = Faces(across_ref, within_ref)
    lows, highs = wide_load(near_ref, *messages, 0), wide_load(near_ref, *messages, 7)
    for c in range(8):
        out.put(8 * c, 8 * c + 8, lows[c], highs[c])
    for row, ref in ((64, far_below_ref), (65, far_above_ref)):
        out.put(row, row + 1, ref[64:65, :], ref[71:72, :])
    for ref in (across_ref, within_ref):
        ref[66:72, :] = jnp.zeros((6, 128), F32)
        ref[FACE_METRIC:FACE_ROWS, :] = rows


def with_sums(face, first, second):
    lane = lane_iota()
    return jnp.where(lane == 0, first, jnp.where(lane == 127, second, face))


def send_along_x(field, first, second, send_ref):
    here = lax.axis_index("gx")
    above = lax.rem(here + 1, N_GX)
    low = [with_sums(field[0][0], first, second), field[0][1]]
    high = [with_sums(field[7][0], first, second), field[7][1]]
    for chunk in range(N_GX):
        for z in range(2):
            send_ref[chunk, 8 * z : 8 * z + 8, :] = jnp.where(
                above == (chunk + END_X) % N_GX, high[z], low[z]
            )


def send_along_z(field, sums, send_ref):
    here = lax.axis_index("gz")
    above = lax.rem(here + 1, N_GZ)
    node = lax.broadcasted_iota(jnp.int32, (8, 128), 0)
    low = high = jnp.zeros((8, 128), F32)
    for i in range(8):
        low = jnp.where(node == i, spread(field[i][0][0:1, :]), low)
        high = jnp.where(node == i, spread(field[i][1][7:8, :]), high)
    low, high = with_sums(low, sums, sums), with_sums(high, sums, sums)
    for chunk in range(N_GZ):
        send_ref[chunk] = jnp.where(above == (chunk + END_Z) % N_GZ, high, low)


def near_rows(near_ref, i, z):
    start = 8 * (2 * i + z)
    return near_ref[start : start + 8, :]


def coarse_start(near_ref, factor_ref, table_ref, send_ref):
    parts = []
    load = [[wall(near_rows(near_ref, i, z)) for z in range(2)] for i in range(8)]
    for a in range(2):
        along_x = []
        for z in range(2):
            total = float(ALONG_X[a, 0]) * load[0][z]
            for i in range(1, 8):
                total = total + float(ALONG_X[a, i]) * load[i][z]
            along_x.append(total)
        for b in range(2):
            both = (
                table(table_ref, f"bz{b}0") * along_x[0] + table(table_ref, f"bz{b}1") * along_x[1]
            )
            parts.append(jnp.sum(both, axis=0, keepdims=True))
    node = lax.broadcasted_iota(jnp.int32, (8, 128), 0)
    stacked = jnp.zeros((8, 128), F32)
    for index, part in enumerate(parts):
        stacked = jnp.where(node == index, spread(part), stacked)
    modes = lax.dot_general(
        stacked, table(table_ref, "modes"), (((1,), (1,)), ((), ())),
        precision=HIGHEST, preferred_element_type=F32,
    )
    owner = lax.broadcasted_iota(jnp.int32, (8, 32), 1) >> 3
    row = lax.broadcasted_iota(jnp.int32, (8, 32), 0)
    coarse_rhs = jnp.sum(jnp.where(owner == row, modes, 0.0), axis=0, keepdims=True)
    own = jnp.dot(
        jnp.broadcast_to(coarse_rhs, (8, 32)), factor_ref[...],
        precision=HIGHEST, preferred_element_type=F32,
    )
    write_pairs(send_ref, own[0:1, 0:128], own[0:1, 128:256])


def begin(
    near_ref, even_ref, odd_ref, inner_ref, outer_ref, rows_ref, across_ref, within_ref, table_ref,
    rhs_ref, inverse_ref, smooth_ref, applied_ref, across_out, within_out,
):
    left_ref, right_ref = sides(across_ref, within_ref)

    messages = neighbours_z(even_ref, odd_ref, inner_ref, outer_ref)

    def edge(which):
        def row(i):
            value = messages[3 * which][64 + i : 65 + i, :]
            if i == 0:
                value = value + left_ref[64 + which : 65 + which, :]
            if i == 7:
                value = value + right_ref[64 + which : 65 + which, :]
            return value

        return row

    load = [wide_load(near_ref, *messages, i) for i in range(8)]
    load = sum_x(load, faces(left_ref, 8), faces(right_ref, 8))
    rhs = each(wall, sum_y(sum_z(load, edge(0), edge(1))))
    columns = [
        diagonal_sum_x(rows_ref, left_ref, right_ref, column, table_ref) for column in range(-4, 6)
    ]
    diagonal = sum_z([[columns[c][i] for c in range(10)] for i in range(8)])
    inverse = each(lambda d: wall(1.0 / d), sum_y(diagonal))
    smooth = each(lambda d, r: d * r / THETA, inverse, rhs)
    write(rhs_ref, [row[1:7] for row in rhs])
    write(inverse_ref, [row[1:7] for row in inverse])
    write(smooth_ref, [row[1:7] for row in smooth])
    applied = element_apply(smooth, -3, rows_ref, table_ref)
    write(applied_ref, applied)
    write_x_faces(applied, across_out, within_out)


def write_pairs(ref, first, second):
    row = lax.broadcasted_iota(jnp.int32, (8, 128), 0)
    pairs = jnp.where((row & 1) == 0, spread(first), spread(second))
    for start in range(0, ref.shape[0], 8):
        ref[start : start + 8, :] = pairs


def tree_sums(ref, here, skipped, head):
    row = lax.broadcasted_iota(jnp.int32, (8, 128), 0)
    level = (row & 1) * 8 + (lane_iota() >> 4)
    shift = jnp.maximum(level - skipped, 0)
    mine = lax.shift_right_logical(jnp.full((8, 128), here, jnp.int32), shift)
    total = jnp.zeros((8, 128), F32)
    for start in range(0, ref.shape[0], 8):
        device = (head + start // 2 + (row >> 1)) & (ref.shape[0] // 2 - 1)
        other = lax.shift_right_logical(device, shift)
        total = total + jnp.where(other == mine, ref[start : start + 8, :], 0.0)
    first = jnp.sum(jnp.where((row & 1) == 0, total, 0.0), axis=0, keepdims=True)
    second = jnp.sum(jnp.where((row & 1) == 1, total, 0.0), axis=0, keepdims=True)
    return first, second


def neighbours(axis, count, head):
    here = lax.axis_index(axis) + count - head
    return lax.rem(here + count - 1, count), lax.rem(here + 1, count)


def lower_tree(received_ref, send_ref):
    write_pairs(send_ref, *tree_sums(received_ref, lax.axis_index("gz"), 0, TREE_Z))


def x_faces_received(received_ref):
    below, above = neighbours("gx", N_GX, END_X)
    left = [received_ref[below, 8 * z : 8 * z + 8, :] for z in range(2)]
    right = [received_ref[above, 8 * z : 8 * z + 8, :] for z in range(2)]
    return left, right


def relax(step, count, applied_ref, across_ref, within_ref, rhs_ref, inverse_ref, smooth_ref, update_ref):
    left_ref, right_ref = sides(across_ref, within_ref)
    field = sum_x(
        read(applied_ref, 0, count + 2), faces(left_ref, count + 2), faces(right_ref, count + 2)
    )
    image = each(wall, sum_y(sum_z(field)))
    first, second = STEPS[step]
    inset = (6 - count) // 2
    shift = 1 if step else 0
    update = each(
        lambda u, d, r, a: first * u + (second * d) * (r - a),
        read(update_ref, shift, count), read(inverse_ref, inset, count), read(rhs_ref, inset, count),
        image,
    )
    return each(lambda s, u: s + u, read(smooth_ref, shift, count), update), update


def sweep(
    applied_ref, across_ref, within_ref, rhs_ref, inverse_ref, smooth_ref, update_ref, rows_ref, table_ref,
    next_ref, next_update_ref, out_ref, low_ref, high_ref, *, step, count,
):
    smooth, update = relax(
        step, count, applied_ref, across_ref, within_ref, rhs_ref, inverse_ref, smooth_ref, update_ref
    )
    write(next_ref, smooth)
    write(next_update_ref, update)
    applied = element_apply(smooth, 1 - count // 2, rows_ref, table_ref)
    write(out_ref, applied)
    write_x_faces(applied, low_ref, high_ref)


def coarse_field(received_ref, factor_ref, table_ref):
    first, second = tree_sums(received_ref, lax.axis_index("gx"), 4, TREE_X)
    columns = jnp.broadcast_to(jnp.concatenate([first, second], axis=1), (8, 256))
    coarse = lax.dot_general(
        columns, factor_ref[...], (((1,), (1,)), ((), ())),
        precision=HIGHEST, preferred_element_type=F32,
    )
    owner = lax.broadcasted_iota(jnp.int32, (8, 32), 1) >> 3
    row = lax.broadcasted_iota(jnp.int32, (8, 32), 0)
    across = jnp.dot(
        jnp.where(owner == row, coarse, 0.0), table(table_ref, "modes"),
        precision=HIGHEST, preferred_element_type=F32,
    )
    out = [[None, None] for i in range(8)]
    for z in range(2):
        along_z = []
        for a in range(2):
            along_z.append(
                table(table_ref, f"bz0{z}") * spread(across[2 * a : 2 * a + 1, :])
                + table(table_ref, f"bz1{z}") * spread(across[2 * a + 1 : 2 * a + 2, :])
            )
        for i in range(8):
            out[i][z] = wall(float(ALONG_X[0, i]) * along_z[0] + float(ALONG_X[1, i]) * along_z[1])
    return out


def coarse_stage(tree_ref, factor_ref, table_ref, coarse_ref, spare_ref):
    write(coarse_ref, coarse_field(tree_ref, factor_ref, table_ref))
    spare_ref[...] = jnp.zeros((8, 128), F32)


def last_sweep(
    applied_ref, across_ref, within_ref, rhs_ref, inverse_ref, smooth_ref, update_ref, rows_ref,
    coarse_ref, near_ref, table_ref,
    precond_ref, out_ref, send_ref,
):
    smooth, update = relax(
        2, 2, applied_ref, across_ref, within_ref, rhs_ref, inverse_ref, smooth_ref, update_ref
    )
    precond = each(lambda s, c: s + c, smooth, read(coarse_ref))
    write(precond_ref, precond)
    applied = element_apply(precond, 0, rows_ref, table_ref)
    write(out_ref, applied)
    first = jnp.zeros((8, 128), F32)
    second = jnp.zeros((8, 128), F32)
    for i in range(8):
        for z in range(2):
            first = first + near_rows(near_ref, i, z) * precond[i][z]
            second = second + applied[i][z] * precond[i][z]
    send_along_x(
        applied,
        jnp.sum(first, axis=1, keepdims=True),
        jnp.sum(second, axis=1, keepdims=True),
        send_ref,
    )


def middle(applied_ref, received_ref, summed_ref, send_ref):
    field = sum_x(read(applied_ref), *x_faces_received(received_ref))
    write(summed_ref, field)
    sums = received_ref[0, 0:8, :]
    for e in range(1, N_GX):
        sums = sums + received_ref[e, 0:8, :]
    send_along_z(field, sums, send_ref)


def finish(summed_ref, received_ref, precond_ref, rhs_ref, solution_ref, residual_ref):
    below, above = neighbours("gz", N_GZ, END_Z)
    field = sum_z(
        read(summed_ref),
        lambda i: received_ref[below, i : i + 1, :],
        lambda i: received_ref[above, i : i + 1, :],
    )
    image = each(wall, sum_y(field))
    sums = received_ref[0]
    for e in range(1, N_GZ):
        sums = sums + received_ref[e]
    sums = jnp.sum(sums, axis=0, keepdims=True)
    alpha = spread(sums[:, 0:1] / sums[:, 127:128])
    write(solution_ref, each(lambda p: alpha * p, read(precond_ref)))
    write(residual_ref, each(lambda r, a: r - alpha * a, read(rhs_ref, 2, 2), image))


def field_shape(count):
    return (8, count, 8, 128)


def run(kernel, shapes, *operands, first=False, last=False, after=None):
    spec = pl.BlockSpec(memory_space=pltpu.VMEM)
    outs = [
        jax.ShapeDtypeStruct(shape, F32) if last else pltpu.VMEM(shape, F32) for shape in shapes
    ]
    if not first:
        operands = [pltpu.with_memory_space_constraint(value, pltpu.VMEM) for value in operands]
    specs = [spec] * len(operands)
    if after is not None:
        operands, specs = [*operands, after], [*specs, pl.BlockSpec(memory_space=pl.ANY)]
    return pl.pallas_call(
        kernel, out_shape=outs, in_specs=specs, out_specs=[spec] * len(outs)
    )(*operands)


def swap_z(value, distance, first=0):
    count = lax.axis_size("gz")
    pairs = [(i, (((i - first) % count ^ distance) + first) % count) for i in range(count)]
    return lax.ppermute(value, "gz", pairs)


def swap_x(across, within):
    count = lax.axis_size("gx")
    over = [(i, (((i - 1) % count) ^ 1) + 1) for i in range(count)]
    over = [(i, target % count) for i, target in over]
    inside = [(i, i ^ 1) for i in range(count)]
    return lax.ppermute(across, "gx", over), lax.ppermute(within, "gx", inside)


def send_chunks(chunks, axis, head):
    count = lax.axis_size(axis)
    group = [(head + k) % count for k in range(count)]
    return lax.all_to_all(chunks, axis, 0, 0, tiled=True, axis_index_groups=[group])


def send_pairs(pairs, axis, head):
    return send_chunks(pairs.reshape(-1, 2, 128), axis, head).reshape(pairs.shape)


def per_device(element_rhs_load, metric, coarse_factor):
    constants = jnp.asarray(TABLE)
    factor = coarse_factor.reshape(10, 32, 16).transpose(1, 0, 2).reshape(32, 160)
    factor = jnp.pad(factor, ((0, 0), (0, 96)))
    near, inner, outer = run(
        pack, [(136, 128), (80, 128), (80, 128)], element_rhs_load, metric, first=True
    )
    near_even, near_odd = swap_z(near, 1), swap_z(near, 1, 1)
    far_inner, far_outer = swap_z(inner, 2), swap_z(outer, 2, 2)
    (send,) = run(coarse_start, [(2 * N_GZ, 128)], near, factor, constants)
    tree = send_pairs(send, "gz", TREE_Z)
    rows, low, high = run(
        gather, [(32, 128)] + [(FACE_ROWS, 128)] * 2,
        near, near_even, near_odd, far_inner, far_outer, after=send,
    )
    left, right = swap_x(low, high)
    rhs, inverse, smooth, applied, low, high = run(
        begin, [field_shape(6)] * 3 + [field_shape(8)] + [(64, 128)] * 2,
        near, near_even, near_odd, far_inner, far_outer, rows, left, right, constants,
    )
    left, right = swap_x(low, high)
    (send,) = run(lower_tree, [(2 * N_GX, 128)], tree)
    tree = send_pairs(send, "gx", TREE_X)
    update = smooth
    for step, count in ((0, 6), (1, 4)):

        def stage(*refs, step=step, count=count):
            sweep(*refs, step=step, count=count)

        smooth, update, applied, low, high = run(
            stage, [field_shape(count)] * 3 + [(8 * count, 128)] * 2,
            applied, left, right, rhs, inverse, smooth, update, rows, constants,
        )
        left, right = swap_x(low, high)
    coarse, _ = run(coarse_stage, [field_shape(2), (8, 128)], tree, factor, constants)
    precond, applied, send = run(
        last_sweep, [field_shape(2)] * 2 + [(N_GX, 16, 128)],
        applied, left, right, rhs, inverse, smooth, update, rows, coarse, near, constants,
    )
    received = send_chunks(send, "gx", END_X)
    summed, send = run(middle, [field_shape(2), (N_GZ, 8, 128)], applied, received)
    received = send_chunks(send, "gz", END_Z)
    solution_field, residual = run(
        finish, [field_shape(2)] * 2, summed, received, precond, rhs, last=True
    )
    shape = element_rhs_load.shape
    return solution_field.reshape(shape), residual.reshape(shape)


def solution(mesh):
    placed = (
        P("gx", None, "gz", None, None),
        P(None, "gx", "gz", None),
        P("gx", "gz", None, None, None),
    )
    return jax.shard_map(
        per_device,
        mesh=mesh,
        in_specs=placed,
        out_specs=(P("gx", None, "gz", None, None), P("gx", None, "gz", None, None)),
        check_vma=False,
    )
```

```python
import jax
import jax.numpy as jnp
import numpy as np
from jax import lax
from jax.experimental import pallas as pl
from jax.experimental.pallas import tpu as pltpu
from jax.sharding import PartitionSpec as P

CHEB = 4
N_GX = 32
N_GZ = 16
F32 = jnp.float32
HIGHEST = lax.Precision.HIGHEST
TREE_Z, TREE_X = 0, 7
END_Z, END_X = 9, 20

cheb_high = 2.0
cheb_low = 0.1
gll_inner = (
    -0.8717401485096066,
    -0.5917001814331423,
    -0.2092992179024789,
    0.2092992179024789,
    0.5917001814331423,
    0.8717401485096066,
)


def legendre_seven(points):
    before = np.ones(points.shape[0])
    current = points.copy()
    for degree in range(1, 7):
        following = ((2.0 * degree + 1.0) * points * current - degree * before) / (degree + 1.0)
        before = current
        current = following
    return current


def gll_tables():
    order = 7
    points = np.concatenate([[-1.0], np.array(gll_inner), [1.0]])
    values = legendre_seven(points)
    weights = 2.0 / (order * (order + 1) * values**2)
    count = order + 1
    deriv = np.zeros((count, count))
    for row_index in range(count):
        for col_index in range(count):
            if row_index != col_index:
                deriv[row_index, col_index] = values[row_index] / (
                    values[col_index] * (points[row_index] - points[col_index])
                )
    deriv[0, 0] = -order * (order + 1) / 4.0
    deriv[-1, -1] = order * (order + 1) / 4.0
    stiff = deriv.T @ (weights[:, None] * deriv)
    return (points, weights, stiff)


POINTS, WEIGHTS, STIFF = gll_tables()
KDIAG = np.diag(STIFF)
W = [float(v) for v in WEIGHTS]
KD = [float(v) for v in KDIAG]
K = [[float(v) for v in row] for row in STIFF]


def positions(count):
    return ((np.arange(count)[:, None] + (1.0 + POINTS[None, :]) / 2.0) / count).reshape(-1)


ALONG_X = np.stack([np.sin(np.pi * mode * positions(1)) for mode in (1, 2)])
ALONG_Z = np.stack([np.sin(np.pi * mode * positions(2)) for mode in (1, 2)])
ALONG_Y = np.stack([np.sin(np.pi * mode * positions(16)) for mode in range(1, 9)])


def build_tables():
    w_l = np.tile(WEIGHTS, 16)[None, :]
    k_l = np.tile(KDIAG, 16)[None, :]
    w_j = WEIGHTS[:, None]
    k_j = KDIAG[:, None]
    ones = np.ones((1, 128))
    pieces = {
        "stiff": np.kron(np.eye(16), STIFF),
        "ww": w_j * w_l,
        "kw": k_j * w_l,
        "wk": w_j * k_l,
        "wl": np.ones((8, 1)) * w_l,
        "wj": w_j * ones,
        "modes": np.tile(ALONG_Y, (4, 1)),
    }
    for b in range(2):
        for z in range(2):
            pieces[f"bz{b}{z}"] = ALONG_Z[b, 8 * z : 8 * z + 8, None] * ones
    offsets = {}
    rows = []
    start = 0
    for name, piece in pieces.items():
        offsets[name] = (start, start + piece.shape[0])
        rows.append(piece)
        start += piece.shape[0]
    return np.concatenate(rows).astype(np.float32), offsets


TABLE, OFFSETS = build_tables()


def chebyshev_steps():
    theta = 0.5 * (cheb_high + cheb_low)
    delta = 0.5 * (cheb_high - cheb_low)
    sigma = theta / delta
    rho = 1.0 / sigma
    steps = []
    for sweep in range(CHEB - 1):
        rho_next = 1.0 / (2.0 * sigma - rho)
        steps.append((rho_next * rho, 2.0 * rho_next / delta))
        rho = rho_next
    return theta, steps


THETA, STEPS = chebyshev_steps()


def table(table_ref, name):
    low, high = OFFSETS[name]
    return table_ref[low:high, :]


def lane_iota():
    return lax.broadcasted_iota(jnp.int32, (8, 128), 1)


def read(ref, first=0, count=2):
    return [[ref[i, c] for c in range(first, first + count)] for i in range(8)]


def write(ref, field):
    for i in range(8):
        for c, value in enumerate(field[i]):
            ref[i, c] = value


def spread(row):
    return jnp.broadcast_to(row, (8, 128))


def sum_x(field, left, right):
    out = [list(row) for row in field]
    for c in range(len(field[0])):
        out[0][c] = field[0][c] + left[c]
        out[7][c] = field[7][c] + right[c]
    return out


def sum_z(field, before=None, after=None):
    node = lax.broadcasted_iota(jnp.int32, (8, 128), 0)
    count = len(field[0])
    out = []
    for i in range(8):
        lows = [None] + [field[i][c][7:8, :] for c in range(count - 1)]
        highs = [field[i][c][0:1, :] for c in range(1, count)] + [None]
        if before is not None:
            lows[0], highs[-1] = before(i), after(i)
        out.append(
            [
                field[i][c]
                + jnp.where(node == 0, spread(lows[c]), jnp.where(node == 7, spread(highs[c]), 0.0))
                for c in range(count)
                if lows[c] is not None and highs[c] is not None
            ]
        )
    return out


def sum_y(field):
    lane = lane_iota()
    first = ((lane & 7) == 0) & (lane > 0)
    last = ((lane & 7) == 7) & (lane < 127)
    return each(
        lambda value: value
        + jnp.where(last, pltpu.roll(value, 127, 1), jnp.where(first, pltpu.roll(value, 1, 1), 0.0)),
        field,
    )


def wall(value):
    lane = lane_iota()
    return jnp.where((lane == 0) | (lane == 127), 0.0, value)


def each(function, *fields):
    return [[function(*values) for values in zip(*rows)] for rows in zip(*fields)]


ROWS = 10


def metric_row(ref, base, m, column):
    row = base + ROWS * m + 4 + column
    return ref[row : row + 1, :]


def element_apply(field, first, metric_ref, table_ref, nodes=range(8)):
    count = len(field[0])
    rows = 8 * len(nodes)
    stiff = table(table_ref, "stiff")
    out = [[None] * count for i in range(8)]
    columns = [jnp.concatenate([field[i][c] for i in nodes], axis=0) for c in range(count)]
    along_y = jnp.dot(
        jnp.concatenate(columns, axis=0), stiff, precision=HIGHEST, preferred_element_type=F32
    )
    for c in range(count):
        stacked = columns[c]
        along_l = along_y[rows * c : rows * c + rows, :]
        along_j = jnp.dot(
            stiff[0:rows, 0:rows], stacked, precision=HIGHEST, preferred_element_type=F32
        )
        factors = [spread(metric_row(metric_ref, 0, m, first + c)) for m in range(3)]
        scale_x = factors[0] * table(table_ref, "ww")
        scale_z = factors[1] * table(table_ref, "wl")
        scale_y = factors[2] * table(table_ref, "wj")
        for place, p in enumerate(nodes):
            along_i = K[0][p] * field[0][c]
            for i in range(1, 8):
                along_i = along_i + K[i][p] * field[i][c]
            out[p][c] = scale_x * along_i + W[p] * (
                scale_z * along_j[8 * place : 8 * place + 8, :] + scale_y * along_l[8 * place : 8 * place + 8, :]
            )
    return out


def diagonal_parts(ref, base, column, table_ref):
    part_x = spread(metric_row(ref, base, 0, column)) * table(table_ref, "ww")
    part_rest = spread(metric_row(ref, base, 1, column)) * table(table_ref, "kw") + spread(
        metric_row(ref, base, 2, column)
    ) * table(table_ref, "wk")
    return part_x, part_rest


def diagonal_sum_x(rows_ref, left_ref, right_ref, column, table_ref):
    part_x, part_rest = diagonal_parts(rows_ref, 0, column, table_ref)
    out = []
    for i in range(8):
        sum_of_x, sum_of_rest = part_x, part_rest
        if i in (0, 7):
            side = left_ref if i == 0 else right_ref
            side_x, side_rest = diagonal_parts(side, FACE_METRIC, column, table_ref)
            sum_of_x, sum_of_rest = part_x + side_x, part_rest + side_rest
        out.append(KD[i] * sum_of_x + W[i] * sum_of_rest)
    return out


class Faces:
    def __init__(self, across_ref, within_ref):
        self.odd = lax.rem(lax.axis_index("gx"), 2) == 1
        self.across, self.within = across_ref, within_ref

    def put(self, first, last, low, high):
        self.across[first:last, :] = jnp.where(self.odd, high, low)
        self.within[first:last, :] = jnp.where(self.odd, low, high)


class Either:
    def __init__(self, first, first_ref, second_ref):
        self.first, self.first_ref, self.second_ref = first, first_ref, second_ref

    def __getitem__(self, where):
        return jnp.where(self.first, self.first_ref[where], self.second_ref[where])


class Side:
    def __init__(self, across_ref, within_ref, right):
        odd = lax.rem(lax.axis_index("gx"), 2) == 1
        self.across = odd if right else jnp.logical_not(odd)
        self.across_ref, self.within_ref = across_ref, within_ref

    def __getitem__(self, where):
        return jnp.where(self.across, self.across_ref[where], self.within_ref[where])


def sides(across_ref, within_ref):
    return Side(across_ref, within_ref, False), Side(across_ref, within_ref, True)


def write_x_faces(field, across_ref, within_ref):
    out = Faces(across_ref, within_ref)
    for c in range(len(field[0])):
        out.put(8 * c, 8 * c + 8, field[0][c], field[7][c])


def faces(ref, count):
    return [ref[8 * c : 8 * c + 8, :] for c in range(count)]


def pack(load_ref, metric_ref, near_ref, inner_ref, outer_ref):
    begins = lax.rem(lax.axis_index("gz"), 4) < 2
    element = lax.broadcasted_iota(jnp.int32, (16, 128), 0)
    lane = lax.broadcasted_iota(jnp.int32, (16, 128), 1)
    expand = jnp.where(element == (lane >> 3), 1.0, 0.0)
    for ref, start in ((near_ref, 128), (inner_ref, 72), (outer_ref, 72)):
        ref[start + 6 : start + 8, :] = jnp.zeros((2, 128), F32)
    stacked = jnp.concatenate([metric_ref[m, 0] for m in range(3)], axis=0)
    expanded = jnp.dot(stacked, expand, precision=HIGHEST, preferred_element_type=F32)
    for ref, start in ((near_ref, 128), (inner_ref, 72), (outer_ref, 72)):
        ref[start : start + 6, :] = expanded
    for i in range(8):
        for z in range(2):
            near_ref[8 * (2 * i + z) : 8 * (2 * i + z) + 8, :] = load_ref[0, i, z]
        rows = slice(8 * i, 8 * i + 8)
        inner_ref[rows, :] = jnp.where(begins, load_ref[0, i, 1], load_ref[0, i, 0])
        outer_ref[rows, :] = jnp.where(begins, load_ref[0, i, 0], load_ref[0, i, 1])
        up, down = load_ref[0, i, 0, 7:8, :], load_ref[0, i, 1, 0:1, :]
        inner_ref[64 + i : 65 + i, :] = jnp.where(begins, up, down)
        outer_ref[64 + i : 65 + i, :] = jnp.where(begins, down, up)


FACE_METRIC = 72
FACE_ROWS = 104


def neighbours_z(even_ref, odd_ref, inner_ref, outer_ref):
    place = lax.axis_index("gz")
    return (
        Either(lax.rem(place, 4) >= 2, inner_ref, outer_ref),
        Either(lax.rem(place, 2) == 1, even_ref, odd_ref),
        Either(lax.rem(place, 2) == 0, even_ref, odd_ref),
        Either(lax.rem(place, 4) < 2, inner_ref, outer_ref),
    )


def wide_load(near_ref, far_below_ref, below_ref, above_ref, far_above_ref, i):
    far = slice(8 * i, 8 * i + 8)
    pair = [slice(8 * (2 * i + z), 8 * (2 * i + z) + 8) for z in range(2)]
    return (
        [far_below_ref[far, :]]
        + [ref[rows, :] for ref in (below_ref, near_ref, above_ref) for rows in pair]
        + [far_above_ref[far, :]]
    )


def gather(
    near_ref, even_ref, odd_ref, inner_ref, outer_ref, earlier_ref, rows_ref, across_ref, within_ref
):
    messages = neighbours_z(even_ref, odd_ref, inner_ref, outer_ref)
    far_below_ref, below_ref, above_ref, far_above_ref = messages
    sources = (
        (far_below_ref, 72), (below_ref, 128), (near_ref, 128), (above_ref, 128), (far_above_ref, 72),
    )
    for index, (source, start) in enumerate(sources):
        for m in range(3):
            row = ROWS * m + 2 * index
            rows_ref[row : row + 2, :] = source[start + 2 * m : start + 2 * m + 2, :]
    rows_ref[30:32, :] = jnp.zeros((2, 128), F32)
    rows = rows_ref[...]
    out = Faces(across_ref, within_ref)
    lows, highs = wide_load(near_ref, *messages, 0), wide_load(near_ref, *messages, 7)
    for c in range(8):
        out.put(8 * c, 8 * c + 8, lows[c], highs[c])
    for row, ref in ((64, far_below_ref), (65, far_above_ref)):
        out.put(row, row + 1, ref[64:65, :], ref[71:72, :])
    for ref in (across_ref, within_ref):
        ref[66:72, :] = jnp.zeros((6, 128), F32)
        ref[FACE_METRIC:FACE_ROWS, :] = rows


def with_sums(face, first, second):
    lane = lane_iota()
    return jnp.where(lane == 0, first, jnp.where(lane == 127, second, face))


def send_along_x(field, first, second, send_ref):
    here = lax.axis_index("gx")
    above = lax.rem(here + 1, N_GX)
    low = [with_sums(field[0][0], first, second), field[0][1]]
    high = [with_sums(field[7][0], first, second), field[7][1]]
    for chunk in range(N_GX):
        for z in range(2):
            send_ref[chunk, 8 * z : 8 * z + 8, :] = jnp.where(
                above == (chunk + END_X) % N_GX, high[z], low[z]
            )


def send_along_z(field, sums, send_ref):
    here = lax.axis_index("gz")
    above = lax.rem(here + 1, N_GZ)
    node = lax.broadcasted_iota(jnp.int32, (8, 128), 0)
    low = high = jnp.zeros((8, 128), F32)
    for i in range(8):
        low = jnp.where(node == i, spread(field[i][0][0:1, :]), low)
        high = jnp.where(node == i, spread(field[i][1][7:8, :]), high)
    low, high = with_sums(low, sums, sums), with_sums(high, sums, sums)
    for chunk in range(N_GZ):
        send_ref[chunk] = jnp.where(above == (chunk + END_Z) % N_GZ, high, low)


def near_rows(near_ref, i, z):
    start = 8 * (2 * i + z)
    return near_ref[start : start + 8, :]


def coarse_start(near_ref, factor_ref, table_ref, send_ref):
    parts = []
    load = [[wall(near_rows(near_ref, i, z)) for z in range(2)] for i in range(8)]
    for a in range(2):
        along_x = []
        for z in range(2):
            total = float(ALONG_X[a, 0]) * load[0][z]
            for i in range(1, 8):
                total = total + float(ALONG_X[a, i]) * load[i][z]
            along_x.append(total)
        for b in range(2):
            both = (
                table(table_ref, f"bz{b}0") * along_x[0] + table(table_ref, f"bz{b}1") * along_x[1]
            )
            parts.append(jnp.sum(both, axis=0, keepdims=True))
    node = lax.broadcasted_iota(jnp.int32, (8, 128), 0)
    stacked = jnp.zeros((8, 128), F32)
    for index, part in enumerate(parts):
        stacked = jnp.where(node == index, spread(part), stacked)
    modes = lax.dot_general(
        stacked, table(table_ref, "modes"), (((1,), (1,)), ((), ())),
        precision=HIGHEST, preferred_element_type=F32,
    )
    owner = lax.broadcasted_iota(jnp.int32, (8, 32), 1) >> 3
    row = lax.broadcasted_iota(jnp.int32, (8, 32), 0)
    coarse_rhs = jnp.sum(jnp.where(owner == row, modes, 0.0), axis=0, keepdims=True)
    own = jnp.dot(
        jnp.broadcast_to(coarse_rhs, (8, 32)), factor_ref[...],
        precision=HIGHEST, preferred_element_type=F32,
    )
    write_pairs(send_ref, own[0:1, 0:128], own[0:1, 128:256])


def begin(
    near_ref, even_ref, odd_ref, inner_ref, outer_ref, rows_ref, across_ref, within_ref, table_ref,
    rhs_ref, inverse_ref, smooth_ref, wide_ref, across_out, within_out,
):
    left_ref, right_ref = sides(across_ref, within_ref)

    messages = neighbours_z(even_ref, odd_ref, inner_ref, outer_ref)

    def edge(which):
        def row(i):
            value = messages[3 * which][64 + i : 65 + i, :]
            if i == 0:
                value = value + left_ref[64 + which : 65 + which, :]
            if i == 7:
                value = value + right_ref[64 + which : 65 + which, :]
            return value

        return row

    load = [wide_load(near_ref, *messages, i) for i in range(8)]
    load = sum_x(load, faces(left_ref, 8), faces(right_ref, 8))
    rhs = each(wall, sum_y(sum_z(load, edge(0), edge(1))))
    columns = [
        diagonal_sum_x(rows_ref, left_ref, right_ref, column, table_ref) for column in range(-4, 6)
    ]
    diagonal = sum_z([[columns[c][i] for c in range(10)] for i in range(8)])
    inverse = each(lambda d: wall(1.0 / d), sum_y(diagonal))
    smooth = each(lambda d, r: d * r / THETA, inverse, rhs)
    write(rhs_ref, [row[1:7] for row in rhs])
    write(inverse_ref, [row[1:7] for row in inverse])
    write(smooth_ref, [row[1:7] for row in smooth])
    write(wide_ref, smooth)
    applied = element_apply(smooth, -3, rows_ref, table_ref, (0, 7))
    write_x_faces(applied, across_out, within_out)


def write_pairs(ref, first, second):
    row = lax.broadcasted_iota(jnp.int32, (8, 128), 0)
    pairs = jnp.where((row & 1) == 0, spread(first), spread(second))
    for start in range(0, ref.shape[0], 8):
        ref[start : start + 8, :] = pairs


def tree_sums(ref, here, skipped, head):
    row = lax.broadcasted_iota(jnp.int32, (8, 128), 0)
    level = (row & 1) * 8 + (lane_iota() >> 4)
    shift = jnp.maximum(level - skipped, 0)
    mine = lax.shift_right_logical(jnp.full((8, 128), here, jnp.int32), shift)
    total = jnp.zeros((8, 128), F32)
    for start in range(0, ref.shape[0], 8):
        device = (head + start // 2 + (row >> 1)) & (ref.shape[0] // 2 - 1)
        other = lax.shift_right_logical(device, shift)
        total = total + jnp.where(other == mine, ref[start : start + 8, :], 0.0)
    first = jnp.sum(jnp.where((row & 1) == 0, total, 0.0), axis=0, keepdims=True)
    second = jnp.sum(jnp.where((row & 1) == 1, total, 0.0), axis=0, keepdims=True)
    return first, second


def neighbours(axis, count, head):
    here = lax.axis_index(axis) + count - head
    return lax.rem(here + count - 1, count), lax.rem(here + 1, count)


def lower_tree(received_ref, send_ref):
    write_pairs(send_ref, *tree_sums(received_ref, lax.axis_index("gz"), 0, TREE_Z))


def x_faces_received(received_ref):
    below, above = neighbours("gx", N_GX, END_X)
    left = [received_ref[below, 8 * z : 8 * z + 8, :] for z in range(2)]
    right = [received_ref[above, 8 * z : 8 * z + 8, :] for z in range(2)]
    return left, right


def relax(step, count, applied_ref, across_ref, within_ref, rhs_ref, inverse_ref, smooth_ref, update_ref):
    left_ref, right_ref = sides(across_ref, within_ref)
    field = sum_x(
        read(applied_ref, 0, count + 2), faces(left_ref, count + 2), faces(right_ref, count + 2)
    )
    image = each(wall, sum_y(sum_z(field)))
    first, second = STEPS[step]
    inset = (6 - count) // 2
    shift = 1 if step else 0
    update = each(
        lambda u, d, r, a: first * u + (second * d) * (r - a),
        read(update_ref, shift, count), read(inverse_ref, inset, count), read(rhs_ref, inset, count),
        image,
    )
    return each(lambda s, u: s + u, read(smooth_ref, shift, count), update), update


def sweep(
    applied_ref, across_ref, within_ref, rhs_ref, inverse_ref, smooth_ref, update_ref, rows_ref, table_ref,
    next_ref, next_update_ref, out_ref, low_ref, high_ref, *, step, count,
):
    smooth, update = relax(
        step, count, applied_ref, across_ref, within_ref, rhs_ref, inverse_ref, smooth_ref, update_ref
    )
    write(next_ref, smooth)
    write(next_update_ref, update)
    applied = element_apply(smooth, 1 - count // 2, rows_ref, table_ref)
    write(out_ref, applied)
    write_x_faces(applied, low_ref, high_ref)


def apply_wide(wide_ref, rows_ref, table_ref, applied_ref, spare_ref):
    write(applied_ref, element_apply(read(wide_ref, 0, 8), -3, rows_ref, table_ref))
    spare_ref[...] = jnp.zeros((8, 128), F32)


def coarse_field(received_ref, factor_ref, table_ref):
    first, second = tree_sums(received_ref, lax.axis_index("gx"), 4, TREE_X)
    columns = jnp.broadcast_to(jnp.concatenate([first, second], axis=1), (8, 256))
    coarse = lax.dot_general(
        columns, factor_ref[...], (((1,), (1,)), ((), ())),
        precision=HIGHEST, preferred_element_type=F32,
    )
    owner = lax.broadcasted_iota(jnp.int32, (8, 32), 1) >> 3
    row = lax.broadcasted_iota(jnp.int32, (8, 32), 0)
    across = jnp.dot(
        jnp.where(owner == row, coarse, 0.0), table(table_ref, "modes"),
        precision=HIGHEST, preferred_element_type=F32,
    )
    out = [[None, None] for i in range(8)]
    for z in range(2):
        along_z = []
        for a in range(2):
            along_z.append(
                table(table_ref, f"bz0{z}") * spread(across[2 * a : 2 * a + 1, :])
                + table(table_ref, f"bz1{z}") * spread(across[2 * a + 1 : 2 * a + 2, :])
            )
        for i in range(8):
            out[i][z] = wall(float(ALONG_X[0, i]) * along_z[0] + float(ALONG_X[1, i]) * along_z[1])
    return out


def coarse_stage(tree_ref, factor_ref, table_ref, coarse_ref, spare_ref):
    write(coarse_ref, coarse_field(tree_ref, factor_ref, table_ref))
    spare_ref[...] = jnp.zeros((8, 128), F32)


def last_sweep(
    applied_ref, across_ref, within_ref, rhs_ref, inverse_ref, smooth_ref, update_ref, rows_ref,
    coarse_ref, near_ref, table_ref,
    precond_ref, out_ref, send_ref,
):
    smooth, update = relax(
        2, 2, applied_ref, across_ref, within_ref, rhs_ref, inverse_ref, smooth_ref, update_ref
    )
    precond = each(lambda s, c: s + c, smooth, read(coarse_ref))
    write(precond_ref, precond)
    applied = element_apply(precond, 0, rows_ref, table_ref)
    write(out_ref, applied)
    first = jnp.zeros((8, 128), F32)
    second = jnp.zeros((8, 128), F32)
    for i in range(8):
        for z in range(2):
            first = first + near_rows(near_ref, i, z) * precond[i][z]
            second = second + applied[i][z] * precond[i][z]
    send_along_x(
        applied,
        jnp.sum(first, axis=1, keepdims=True),
        jnp.sum(second, axis=1, keepdims=True),
        send_ref,
    )


def middle(applied_ref, received_ref, summed_ref, send_ref):
    field = sum_x(read(applied_ref), *x_faces_received(received_ref))
    write(summed_ref, field)
    sums = received_ref[0, 0:8, :]
    for e in range(1, N_GX):
        sums = sums + received_ref[e, 0:8, :]
    send_along_z(field, sums, send_ref)


def finish(summed_ref, received_ref, precond_ref, rhs_ref, solution_ref, residual_ref):
    below, above = neighbours("gz", N_GZ, END_Z)
    field = sum_z(
        read(summed_ref),
        lambda i: received_ref[below, i : i + 1, :],
        lambda i: received_ref[above, i : i + 1, :],
    )
    image = each(wall, sum_y(field))
    sums = received_ref[0]
    for e in range(1, N_GZ):
        sums = sums + received_ref[e]
    sums = jnp.sum(sums, axis=0, keepdims=True)
    alpha = spread(sums[:, 0:1] / sums[:, 127:128])
    write(solution_ref, each(lambda p: alpha * p, read(precond_ref)))
    write(residual_ref, each(lambda r, a: r - alpha * a, read(rhs_ref, 2, 2), image))


def field_shape(count):
    return (8, count, 8, 128)


def run(kernel, shapes, *operands, first=False, last=False, after=None):
    spec = pl.BlockSpec(memory_space=pltpu.VMEM)
    outs = [
        jax.ShapeDtypeStruct(shape, F32) if last else pltpu.VMEM(shape, F32) for shape in shapes
    ]
    if not first:
        operands = [pltpu.with_memory_space_constraint(value, pltpu.VMEM) for value in operands]
    specs = [spec] * len(operands)
    if after is not None:
        operands, specs = [*operands, after], [*specs, pl.BlockSpec(memory_space=pl.ANY)]
    return pl.pallas_call(
        kernel, out_shape=outs, in_specs=specs, out_specs=[spec] * len(outs)
    )(*operands)


def swap_z(value, distance, first=0):
    count = lax.axis_size("gz")
    pairs = [(i, (((i - first) % count ^ distance) + first) % count) for i in range(count)]
    return lax.ppermute(value, "gz", pairs)


def swap_x(across, within):
    count = lax.axis_size("gx")
    over = [(i, (((i - 1) % count) ^ 1) + 1) for i in range(count)]
    over = [(i, target % count) for i, target in over]
    inside = [(i, i ^ 1) for i in range(count)]
    return lax.ppermute(across, "gx", over), lax.ppermute(within, "gx", inside)


def send_chunks(chunks, axis, head):
    count = lax.axis_size(axis)
    group = [(head + k) % count for k in range(count)]
    return lax.all_to_all(chunks, axis, 0, 0, tiled=True, axis_index_groups=[group])


def send_pairs(pairs, axis, head):
    return send_chunks(pairs.reshape(-1, 2, 128), axis, head).reshape(pairs.shape)


def per_device(element_rhs_load, metric, coarse_factor):
    constants = jnp.asarray(TABLE)
    factor = coarse_factor.reshape(10, 32, 16).transpose(1, 0, 2).reshape(32, 160)
    factor = jnp.pad(factor, ((0, 0), (0, 96)))
    near, inner, outer = run(
        pack, [(136, 128), (80, 128), (80, 128)], element_rhs_load, metric, first=True
    )
    near_even, near_odd = swap_z(near, 1), swap_z(near, 1, 1)
    far_inner, far_outer = swap_z(inner, 2), swap_z(outer, 2, 2)
    (send,) = run(coarse_start, [(2 * N_GZ, 128)], near, factor, constants)
    tree = send_pairs(send, "gz", TREE_Z)
    rows, low, high = run(
        gather, [(32, 128)] + [(FACE_ROWS, 128)] * 2,
        near, near_even, near_odd, far_inner, far_outer, after=send,
    )
    left, right = swap_x(low, high)
    rhs, inverse, smooth, wide, low, high = run(
        begin, [field_shape(6)] * 3 + [field_shape(8)] + [(64, 128)] * 2,
        near, near_even, near_odd, far_inner, far_outer, rows, left, right, constants,
    )
    left, right = swap_x(low, high)
    applied, _ = run(apply_wide, [field_shape(8), (8, 128)], wide, rows, constants)
    (send,) = run(lower_tree, [(2 * N_GX, 128)], tree)
    tree = send_pairs(send, "gx", TREE_X)
    update = smooth
    for step, count in ((0, 6), (1, 4)):

        def stage(*refs, step=step, count=count):
            sweep(*refs, step=step, count=count)

        smooth, update, applied, low, high = run(
            stage, [field_shape(count)] * 3 + [(8 * count, 128)] * 2,
            applied, left, right, rhs, inverse, smooth, update, rows, constants,
        )
        left, right = swap_x(low, high)
    coarse, _ = run(coarse_stage, [field_shape(2), (8, 128)], tree, factor, constants)
    precond, applied, send = run(
        last_sweep, [field_shape(2)] * 2 + [(N_GX, 16, 128)],
        applied, left, right, rhs, inverse, smooth, update, rows, coarse, near, constants,
    )
    received = send_chunks(send, "gx", END_X)
    summed, send = run(middle, [field_shape(2), (N_GZ, 8, 128)], applied, received)
    received = send_chunks(send, "gz", END_Z)
    solution_field, residual = run(
        finish, [field_shape(2)] * 2, summed, received, precond, rhs, last=True
    )
    shape = element_rhs_load.shape
    return solution_field.reshape(shape), residual.reshape(shape)


def solution(mesh):
    placed = (
        P("gx", None, "gz", None, None),
        P(None, "gx", "gz", None),
        P("gx", "gz", None, None, None),
    )
    return jax.shard_map(
        per_device,
        mesh=mesh,
        in_specs=placed,
        out_specs=(P("gx", None, "gz", None, None), P("gx", None, "gz", None, None)),
        check_vma=False,
    )
```
